32 devices in a mesh: seq: 4 (over y, x), batch: 8 (over z, core).
Axes of the slice: x: 2, y: 2, z: 4, core: 2. Of those that a mesh axis runs over, the one named last changes fastest.
Arguments:
- block_input: bfloat16 [8, 1024, 2048], P('batch', 'seq'), may hold values from -6 to 6
- lengths: int32 [8], P('batch'), may hold values from 769 to 1024, as said below
- ln1_gain: bfloat16 [2048], P(('seq', 'batch')), may hold values from 0.5 to 1.5
- ln1_bias: bfloat16 [2048], P(('seq', 'batch')), may hold values from -3 to 3
- w_qkv: bfloat16 [2048, 6144], P(('seq', 'batch')), may hold values from -0.125 to 0.125
- qv_bias: bfloat16 [4096], P(('seq', 'batch')), may hold values from -3 to 3
- w_out: bfloat16 [2048, 2048], P(('seq', 'batch')), may hold values from -1.5 to 1.5
- out_bias: bfloat16 [2048], P(('seq', 'batch')), may hold values from -3 to 3
- ln2_gain: bfloat16 [2048], P(('seq', 'batch')), may hold values from 0.5 to 1.5
- ln2_bias: bfloat16 [2048], P(('seq', 'batch')), may hold values from -3 to 3
- w_fc1: bfloat16 [2048, 8192], P(('seq', 'batch')), may hold values from -0.125 to 0.125
- fc1_bias: bfloat16 [8192], P(('seq', 'batch')), may hold values from -3 to 3
- w_fc2: bfloat16 [8192, 2048], P(('seq', 'batch')), may hold values from -0.0625 to 0.0625
- fc2_bias: bfloat16 [2048], P(('seq', 'batch')), may hold values from -3 to 3
- out_cotangent: bfloat16 [8, 1024, 2048], P('batch', 'seq'), may hold values from -6 to 6
Outputs:
- block_output: bfloat16 [8, 1024, 2048], P('batch', 'seq')
- grad_input: float32 [8, 1024, 2048], P('batch', 'seq')
- grad_ln1_gain: float32 [2048], P(('seq', 'batch'))
- grad_ln1_bias: float32 [2048], P(('seq', 'batch'))
- grad_w_qkv: float32 [2048, 6144], P(('seq', 'batch'))
- grad_qv_bias: float32 [4096], P(('seq', 'batch'))
- grad_w_out: float32 [2048, 2048], P(('seq', 'batch'))
- grad_out_bias: float32 [2048], P(('seq', 'batch'))
- grad_ln2_gain: float32 [2048], P(('seq', 'batch'))
- grad_ln2_bias: float32 [2048], P(('seq', 'batch'))
- grad_w_fc1: float32 [2048, 8192], P(('seq', 'batch'))
- grad_fc1_bias: float32 [8192], P(('seq', 'batch'))
- grad_w_fc2: float32 [8192, 2048], P(('seq', 'batch'))
- grad_fc2_bias: float32 [2048], P(('seq', 'batch'))
The draws below stay inside these ranges and needn't reach their ends.
Inputs may be any that keep to these rules, and one draw needn't show every extreme that they name: `lengths`: positions from a sequence's length on are padding; one sequence has length 1024.
All inputs are finite; a program needn't handle non-finite values.
Results may differ from the reference program's by a relative error of at most 0.011.
Values may be sent and summed in bfloat16 or wider, within the bound.
A program may use at most 384 MiB of HBM per device.

```python
import jax
import jax.numpy as jnp
from jax import lax

D = 2048
FF = 8192
HEADS = 16
HEAD_DIM = 128
WINDOW = 256
BLK = 256
LENGTH = 1024
SEQS = 8


def draw_lengths(key, part):
    key = jax.random.fold_in(key, 11)
    key_len, key_pick = jax.random.split(key)
    drawn = jax.random.randint(key_len, (SEQS,), LENGTH - BLK + 1, LENGTH + 1, dtype=jnp.int32)
    chosen = jax.random.randint(key_pick, (), 0, SEQS, dtype=jnp.int32)
    return jnp.where(jnp.arange(SEQS, dtype=jnp.int32) == chosen, LENGTH, drawn).astype(jnp.int32)


def levels(key, shape, pieces, smallest, high):
    loudness, own = 1.0, jax.random.fold_in(key, 6)
    for dim, parts in pieces:
        draws = jnp.exp(jax.random.uniform(jax.random.fold_in(own, dim), (parts,), jnp.float32, smallest / len(pieces), high / len(pieces)))
        loudness = loudness * jnp.repeat(draws, shape[dim] // parts).reshape([-1 if axis == dim else 1 for axis in range(len(shape))])
    return loudness


def scatter_about(stream_key, shape, width, reach, shards=(), kind=jnp.bfloat16):
    gain = levels(stream_key, shape, shards, -0.22, 0.18) if shards else 1.0
    values = jax.random.normal(stream_key, shape, jnp.float32) * width * gain
    return jnp.minimum(jnp.maximum(values, -reach), reach).astype(kind)


def setup_inputs(seed: int = 0) -> dict:
    splits = jax.random.split(jax.random.key(seed), 16)
    block_input = scatter_about(splits[0], (SEQS, LENGTH, D), 1.0, 6.0, ((0, 8), (1, 4)))
    lengths = draw_lengths(jax.random.fold_in(splits[15], 71), 0)
    ln1_gain = jnp.clip(1.0 + 0.1 * jax.random.normal(splits[2], (D,), jnp.float32), 0.5, 1.5).astype(jnp.bfloat16)
    ln1_bias = scatter_about(splits[3], (D,), 0.5, 3.0, ((0, 32),))
    w_qkv = scatter_about(splits[4], (D, 3 * D), D ** -0.5, 0.125, ((0, 32),))
    qv_bias = scatter_about(splits[5], (2 * D,), 0.5, 3.0, ((0, 32),))
    w_out = scatter_about(splits[6], (D, D), (D // 128) ** -0.5, 1.5, ((0, 32),))
    out_bias = scatter_about(splits[7], (D,), 0.5, 3.0, ((0, 32),))
    ln2_gain = jnp.clip(1.0 + 0.1 * jax.random.normal(splits[8], (D,), jnp.float32), 0.5, 1.5).astype(jnp.bfloat16)
    ln2_bias = scatter_about(splits[9], (D,), 0.5, 3.0, ((0, 32),))
    w_fc1 = scatter_about(splits[10], (D, FF), D ** -0.5, 0.125, ((0, 32),))
    fc1_bias = scatter_about(splits[11], (FF,), 0.5, 3.0, ((0, 32),))
    w_fc2 = scatter_about(splits[12], (FF, D), FF ** -0.5, 0.0625, ((0, 32),))
    fc2_bias = scatter_about(splits[13], (D,), 0.5, 3.0, ((0, 32),))
    out_cotangent = scatter_about(splits[14], (SEQS, LENGTH, D), 1.0, 6.0, ((0, 8), (1, 4)))
    return {"block_input": block_input, "lengths": lengths, "ln1_gain": ln1_gain, "ln1_bias": ln1_bias, "w_qkv": w_qkv, "qv_bias": qv_bias, "w_out": w_out, "out_bias": out_bias, "ln2_gain": ln2_gain, "ln2_bias": ln2_bias, "w_fc1": w_fc1, "fc1_bias": fc1_bias, "w_fc2": w_fc2, "fc2_bias": fc2_bias, "out_cotangent": out_cotangent}


EPS = 1e-05
HIGH = lax.Precision.HIGHEST

@jax.custom_vjp
def low(v):
    return lax.optimization_barrier(v.astype(jnp.bfloat16)).astype(jnp.float32)

@jax.custom_vjp
def low_back(v):
    return v

def low_keep(v):
    return (low(v), None)

def low_pass(kept, grad):
    return (grad,)

def back_keep(v):
    return (v, None)

def back_low(kept, grad):
    return (low(grad),)
low.defvjp(low_keep, low_pass)
low_back.defvjp(back_keep, back_low)

def layer_norm(values, gain_vec, shift_vec):
    row_mean = lax.optimization_barrier(jnp.mean(values, -1, keepdims=True))
    centred = values - row_mean
    row_var = lax.optimization_barrier(jnp.mean(centred * centred, -1, keepdims=True))
    return centred * lax.rsqrt(row_var + EPS) * gain_vec + shift_vec

def matmul(left, right):
    return jnp.dot(left, right, precision=HIGH, preferred_element_type=jnp.float32)

def block_mask(start, length):
    query_pos = start + lax.broadcasted_iota(jnp.int32, (BLK, BLK + WINDOW), 0)
    key_pos = start - WINDOW + lax.broadcasted_iota(jnp.int32, (BLK, BLK + WINDOW), 1)
    return (key_pos >= 0) & (key_pos <= query_pos) & (query_pos - key_pos < WINDOW) & ((key_pos < length) | (key_pos == query_pos))

def attend(queries, keys, values, length):
    padding = jnp.zeros((WINDOW, D), keys.dtype)
    key_pad = jnp.concatenate([padding, keys], 0)
    value_pad = jnp.concatenate([padding, values], 0)

    def one_block(index):
        start = (index * BLK).astype(jnp.int32)
        query_blk = lax.dynamic_slice_in_dim(queries, start, BLK, 0).reshape(BLK, HEADS, HEAD_DIM)
        key_blk = lax.dynamic_slice_in_dim(key_pad, start, BLK + WINDOW, 0).reshape(BLK + WINDOW, HEADS, HEAD_DIM)
        value_blk = lax.dynamic_slice_in_dim(value_pad, start, BLK + WINDOW, 0).reshape(BLK + WINDOW, HEADS, HEAD_DIM)
        scores = jnp.einsum('qhd,khd->hqk', query_blk, key_blk, precision=HIGH) * HEAD_DIM ** (-0.5)
        scores = low_back(scores)
        masked = jnp.where(block_mask(start, length)[None], scores, -1e+30)
        probs = low(jax.nn.softmax(masked, -1))
        return jnp.einsum('hqk,khd->qhd', probs, value_blk, precision=HIGH).reshape(BLK, D)
    blocks = lax.map(jax.checkpoint(one_block), jnp.arange(LENGTH // BLK, dtype=jnp.int32))
    return blocks.reshape(LENGTH, D)

def forward(seq_in, params, length):
    gain_one, shift_one, qkv_full, qv_full, out_full, obias_full, gain_two, shift_two, fc1_full, fc1_shift, fc2_full, fc2_shift = params
    hidden_one = low(layer_norm(seq_in, gain_one, shift_one))
    projected = matmul(hidden_one, qkv_full)
    queries = low(low_back(projected[:, :D] + qv_full[:D]))
    keys = low(low_back(projected[:, D:2 * D]))
    values = low(low_back(projected[:, 2 * D:] + qv_full[D:]))
    attended = low(low_back(attend(queries, keys, values, length)))
    attn_out = low_back(matmul(attended, out_full) + obias_full)
    middle = seq_in + attn_out
    hidden_two = low(layer_norm(middle, gain_two, shift_two))
    pre_act = low_back(matmul(hidden_two, fc1_full) + fc1_shift)
    act_low = low(jax.nn.gelu(pre_act, approximate=True))
    branch = low_back(matmul(act_low, fc2_full) + fc2_shift)
    return middle + branch

def reference(block_input, lengths, ln1_gain, ln1_bias, w_qkv, qv_bias, w_out, out_bias, ln2_gain, ln2_bias, w_fc1, fc1_bias, w_fc2, fc2_bias, out_cotangent):
    params = tuple((weight.astype(jnp.float32) for weight in (ln1_gain, ln1_bias, w_qkv, qv_bias, w_out, out_bias, ln2_gain, ln2_bias, w_fc1, fc1_bias, w_fc2, fc2_bias)))

    def one_sequence(running, inputs):
        seq_in, length, seq_grad = inputs
        outputs, pullback = jax.vjp(lambda acts, weights: forward(acts, weights, length), seq_in.astype(jnp.float32), params)
        grad_in, grad_params = pullback(seq_grad.astype(jnp.float32))
        running = tuple((before + addend for before, addend in zip(running, grad_params)))
        return (running, (outputs.astype(jnp.bfloat16), grad_in))
    zero_grads = tuple((jnp.zeros(weight.shape, jnp.float32) for weight in params))
    sums, (outputs, grad_in) = lax.scan(one_sequence, zero_grads, (block_input, lengths, out_cotangent))
    return (outputs, grad_in, sums[0], sums[1], sums[2], sums[3], sums[4], sums[5], sums[6], sums[7], sums[8], sums[9], sums[10], sums[11])
```

```python
import jax
import jax.numpy as jnp
from jax import lax
from jax.sharding import PartitionSpec as P

HEAD_DIM = 128
WINDOW = 256
EPS = 1e-05
BF = jnp.bfloat16
F32 = jnp.float32


def swap(value, bit):
    count = lax.axis_size("seq")
    return lax.ppermute(value, "seq", [(i, i ^ bit) for i in range(count)])


def gather_xor(value):
    half = value.shape[0] // 2
    by_x = swap(value, 1)
    by_y = swap(value, 2)
    far_top = swap(by_x[:half], 2)
    far_low = swap(by_y[half:], 1)
    return [value, by_x, by_y, jnp.concatenate([far_top, far_low], 0)]


def gather_seq(value):
    count = lax.axis_size("seq")
    if count != 4:
        return lax.all_gather(value, "seq", axis=0, tiled=False)
    me = lax.axis_index("seq")
    got = gather_xor(value)
    out = jnp.zeros((4,) + value.shape, value.dtype)
    for k in range(4):
        out = lax.dynamic_update_index_in_dim(out, got[k], me ^ k, 0)
    return out


def scatter_seq(parts):
    count = lax.axis_size("seq")
    if count != 4:
        return lax.psum_scatter(parts.astype(BF).astype(F32), "seq", scatter_dimension=0, tiled=False)
    me = lax.axis_index("seq")
    half = parts.shape[1] // 2
    own, to_x, to_y, far = (lax.dynamic_index_in_dim(parts, me ^ k, 0, keepdims=False) for k in range(4))
    far = far.astype(BF)
    via_y = swap(far[:half], 2)
    via_x = swap(far[half:], 1)
    x_low = swap(to_x[half:].astype(BF), 1)
    y_top = swap(to_y[:half].astype(BF), 2)
    x_top = swap((to_x[:half] + via_y.astype(F32)).astype(BF), 1)
    y_low = swap((to_y[half:] + via_x.astype(F32)).astype(BF), 2)
    top = own[:half] + x_top.astype(F32) + y_top.astype(F32)
    low = own[half:] + x_low.astype(F32) + y_low.astype(F32)
    return jnp.concatenate([top, low], 0)


def scatter_batch(parts):
    flat = parts.astype(BF).reshape(-1, parts.shape[-1])
    return lax.psum_scatter(flat, "batch", scatter_dimension=0, tiled=True).reshape(parts.shape[1:])


def norm_stats(values):
    mean = jnp.mean(values, -1, keepdims=True)
    centred = values - mean
    rstd = lax.rsqrt(jnp.mean(centred * centred, -1, keepdims=True) + EPS)
    return centred * rstd, rstd


def norm_back(grad, normed, rstd, gain):
    dn = grad * gain
    return rstd * (
        dn - jnp.mean(dn, -1, keepdims=True) - normed * jnp.mean(dn * normed, -1, keepdims=True)
    )


def block_masks(count, rows, length):
    shape = (count, rows, rows + WINDOW)
    start = lax.broadcasted_iota(jnp.int32, shape, 0) * rows
    query_pos = start + lax.broadcasted_iota(jnp.int32, shape, 1)
    key_pos = start - WINDOW + lax.broadcasted_iota(jnp.int32, shape, 2)
    return (
        (key_pos >= 0)
        & (key_pos <= query_pos)
        & (query_pos - key_pos < WINDOW)
        & ((key_pos < length) | (key_pos == query_pos))
    )


def windows(value):
    prior = jnp.concatenate([jnp.zeros_like(value[:1]), value[:-1]], 0)
    return jnp.concatenate([prior, value], 1)


def unwindow(grad):
    rows = grad.shape[1] // 2
    own, prior = grad[:, rows:], grad[:, :rows]
    return own + jnp.concatenate([prior[1:], jnp.zeros_like(prior[:1])], 0)


def body(
    block_input,
    lengths,
    ln1_gain,
    ln1_bias,
    w_qkv,
    qv_bias,
    w_out,
    out_bias,
    ln2_gain,
    ln2_bias,
    w_fc1,
    fc1_bias,
    w_fc2,
    fc2_bias,
    out_cotangent,
):
    ns, nb = lax.axis_size("seq"), lax.axis_size("batch")
    seq = lax.axis_index("seq")
    rows, width = block_input.shape[1:]
    share = width // ns
    heads = share // HEAD_DIM
    tokens = ns * rows
    hidden = w_fc1.shape[1] // ns
    depth = w_fc1.shape[0]
    scale = HEAD_DIM ** (-0.5)
    length = lengths[0]

    vectors = (ln1_gain, ln1_bias, qv_bias, out_bias, ln2_gain, ln2_bias, fc1_bias, fc2_bias)
    packed = lax.all_gather(jnp.concatenate(vectors), ("seq", "batch"), axis=0, tiled=False)
    full, at = [], 0
    for vec in vectors:
        full.append(packed[:, at : at + vec.shape[0]].reshape(-1).astype(F32))
        at += vec.shape[0]
    gain1, shift1, qv, obias, gain2, shift2, bias1, bias2 = full
    bias1 = lax.dynamic_slice_in_dim(bias1, seq * hidden, hidden)
    qbias = lax.dynamic_slice_in_dim(qv[:width], seq * share, share)
    vbias = lax.dynamic_slice_in_dim(qv[width:], seq * share, share)

    qkv_part = lax.all_to_all(w_qkv.reshape(depth, 3, ns, share), "seq", 2, 0)
    qkv_part = lax.all_gather(qkv_part.reshape(ns, depth, 3 * share), "batch", axis=0)
    wqkv = qkv_part.transpose(1, 0, 2, 3).reshape(width, 3 * share)
    wout = lax.all_gather(w_out, "batch", axis=0, tiled=True)
    fc1_part = lax.all_to_all(w_fc1.reshape(depth, ns, hidden), "seq", 1, 0)
    fc1_part = lax.all_gather(fc1_part, "batch", axis=0)
    w1 = fc1_part.transpose(1, 0, 2, 3).reshape(width, hidden)
    w2 = lax.all_gather(w_fc2, "batch", axis=0, tiled=True)

    mine = block_input[0]
    acts = gather_seq(mine).reshape(tokens, width).astype(F32)
    normed1, _ = norm_stats(acts)
    h1 = (normed1 * gain1 + shift1).astype(BF)
    proj = jnp.dot(h1, wqkv, preferred_element_type=F32)
    shape = (ns, rows, heads, HEAD_DIM)
    q = (proj[:, :share] + qbias).astype(BF).reshape(shape)
    k = windows(proj[:, share : 2 * share].astype(BF).reshape(shape))
    v = windows((proj[:, 2 * share :] + vbias).astype(BF).reshape(shape))
    mask = block_masks(ns, rows, length)[:, None]
    scores = jnp.einsum("nqhd,nkhd->nhqk", q, k, preferred_element_type=F32) * scale
    scores = jnp.where(mask, scores, -1e30)
    top = jnp.max(scores, -1, keepdims=True)
    expo = jnp.exp(scores - top)
    total = jnp.sum(expo, -1, keepdims=True)
    probs = expo / total
    probs_low = probs.astype(BF)
    o = jnp.einsum("nhqk,nkhd->nqhd", probs_low, v, preferred_element_type=F32)
    o = o.astype(BF).reshape(tokens, share)
    a = jnp.dot(o, wout, preferred_element_type=F32)
    a = scatter_seq(a.reshape(ns, rows, width))
    mine_f = mine.astype(F32)
    x1 = mine_f + (a + obias)
    normed2, rstd2 = norm_stats(x1)
    h2_mine = (normed2 * gain2 + shift2).astype(BF)

    cot_mine = out_cotangent[0]
    h2 = gather_seq(h2_mine).reshape(tokens, width)
    cot = gather_seq(cot_mine).reshape(tokens, width)
    u = jnp.dot(h2, w1, preferred_element_type=F32) + bias1
    g, pull = jax.vjp(lambda t: jax.nn.gelu(t, approximate=True), u)
    g = g.astype(BF)
    y = jnp.dot(g, w2, preferred_element_type=F32)
    dg = jnp.einsum("td,fd->tf", cot, w2, preferred_element_type=F32)
    du = pull(dg)[0].astype(BF)
    gw2 = jnp.einsum("tf,td->fd", g, cot, preferred_element_type=F32)
    gw1 = jnp.einsum("td,tf->df", h2, du, preferred_element_type=F32)
    gb1 = jnp.sum(du.astype(F32), 0)
    dh2 = jnp.einsum("tf,df->td", du, w1, preferred_element_type=F32)
    gw2 = scatter_batch(gw2.reshape(nb, -1, width))
    gw1 = scatter_batch(gw1.reshape(ns, nb, depth, hidden).transpose(1, 0, 2, 3))
    dh2 = scatter_seq(dh2.reshape(ns, rows, width))
    y = scatter_seq(y.reshape(ns, rows, width))
    out = (x1 + (y + bias2)).astype(BF)
    gb2 = jnp.sum(cot_mine.astype(F32), 0)
    cot_f = cot_mine.astype(F32)
    ggain2 = jnp.sum(dh2 * normed2, 0)
    gshift2 = jnp.sum(dh2, 0)
    dx1 = cot_f + norm_back(dh2, normed2, rstd2, gain2)
    da_mine = dx1.astype(BF)

    gob = jnp.sum(da_mine.astype(F32), 0)
    da = gather_seq(da_mine).reshape(tokens, width)
    gwo = jnp.einsum("td,te->de", o, da, preferred_element_type=F32)
    do = jnp.einsum("te,de->td", da, wout, preferred_element_type=F32).astype(BF).reshape(shape)
    dp = jnp.einsum("nqhd,nkhd->nhqk", do, v, preferred_element_type=F32)
    ds = (probs * (dp - jnp.sum(dp * probs, -1, keepdims=True))).astype(BF)
    dq = jnp.einsum("nhqk,nkhd->nqhd", ds, k, preferred_element_type=F32) * scale
    dk = unwindow(jnp.einsum("nhqk,nqhd->nkhd", ds, q, preferred_element_type=F32)) * scale
    dv = unwindow(jnp.einsum("nhqk,nqhd->nkhd", probs_low, do, preferred_element_type=F32))
    dproj = jnp.concatenate([t.astype(BF).reshape(tokens, share) for t in (dq, dk, dv)], 1)
    gwqkv = jnp.einsum("td,te->de", h1, dproj, preferred_element_type=F32)
    gqv = jnp.sum(dproj.astype(F32), 0)
    dh1 = jnp.einsum("te,de->td", dproj, wqkv, preferred_element_type=F32)
    gwo = scatter_batch(gwo.reshape(nb, depth, width))
    gwqkv = scatter_batch(gwqkv.reshape(ns, nb, depth, 3 * share).transpose(1, 0, 2, 3))
    dh1 = scatter_seq(dh1.reshape(ns, rows, width))
    nmine, rmine = norm_stats(mine_f)
    ggain1 = jnp.sum(dh1 * nmine, 0)
    gshift1 = jnp.sum(dh1, 0)
    gx = dx1 + norm_back(dh1, nmine, rmine, gain1)

    gw1 = lax.all_to_all(gw1.astype(BF), "seq", 0, 1).astype(F32).reshape(depth, ns * hidden)
    gwqkv = lax.all_to_all(gwqkv.astype(BF).reshape(ns, depth, 3, share), "seq", 0, 2)
    gwqkv = gwqkv.astype(F32).reshape(depth, 3 * width)

    def place(part, size):
        return lax.dynamic_update_slice_in_dim(jnp.zeros((size,), F32), part, seq * part.shape[0], 0)

    gqv = jnp.concatenate([place(gqv[:share], width), place(gqv[2 * share :], width)])
    sums = (ggain1, gshift1, gqv, gob, ggain2, gshift2, place(gb1, ns * hidden), gb2)
    sums = jnp.concatenate([t.reshape(ns * nb, -1) for t in sums], 1)
    sums = lax.psum_scatter(sums, ("seq", "batch"), scatter_dimension=0, tiled=True)[0]
    small, at = [], 0
    for vec in vectors:
        small.append(sums[at : at + vec.shape[0]])
        at += vec.shape[0]
    return (
        out[None],
        gx[None],
        small[0],
        small[1],
        gwqkv,
        small[2],
        gwo.astype(F32),
        small[3],
        small[4],
        small[5],
        gw1,
        small[6],
        gw2.astype(F32),
        small[7],
    )


def solution(mesh):
    shard = P(("seq", "batch"))
    shard2 = P(("seq", "batch"), None)
    acts = P("batch", "seq", None)
    return jax.shard_map(
        body,
        mesh=mesh,
        in_specs=(acts, P("batch"), shard, shard, shard2, shard, shard2, shard, shard, shard, shard2, shard, shard2, shard, acts),
        out_specs=(acts, acts, shard, shard, shard2, shard, shard2, shard, shard, shard, shard2, shard, shard2, shard),
        check_vma=False,
    )
```

```python
import functools
import math

import jax
import jax.numpy as jnp
from jax import lax
from jax.experimental import pallas as pl
from jax.experimental.pallas import tpu as pltpu
from jax.sharding import PartitionSpec as P

HEAD_DIM = 128
WINDOW = 256
EPS = 1e-05
BF = jnp.bfloat16
F32 = jnp.float32
ROOT = math.sqrt(2.0 / math.pi)


def norm_stats(values):
    mean = jnp.mean(values, -1, keepdims=True)
    centred = values - mean
    rstd = lax.rsqrt(jnp.mean(centred * centred, -1, keepdims=True) + EPS)
    return centred * rstd, rstd


def norm_back(grad, normed, rstd, gain):
    dn = grad * gain
    return rstd * (
        dn - jnp.mean(dn, -1, keepdims=True) - normed * jnp.mean(dn * normed, -1, keepdims=True)
    )


def dot_t(left, right):
    return lax.dot_general(left, right, (((1,), (1,)), ((), ())), preferred_element_type=F32)


def t_dot(left, right):
    return lax.dot_general(left, right, (((0,), (0,)), ((), ())), preferred_element_type=F32)


def load_rows(ns, nb, depth, src, dst, sem):
    def one(k, carry):
        s, b = k // nb, lax.rem(k, nb)
        pltpu.make_async_copy(
            src.at[b, pl.ds(s * depth, depth), :], dst.at[pl.ds(k * depth, depth), :], sem
        ).start()
        return carry

    lax.fori_loop(0, ns * nb, one, 0)


def soft_block(query, keys, block, first, length):
    rows, count = query.shape[0], keys.shape[0]
    scores = dot_t(query, keys) * HEAD_DIM ** (-0.5)
    query_pos = block * rows + lax.broadcasted_iota(jnp.int32, (rows, count), 0)
    key_pos = first + lax.broadcasted_iota(jnp.int32, (rows, count), 1)
    back = query_pos - key_pos
    valid = (back >= 0) & (back < WINDOW) & ((key_pos < length) | (back == 0))
    scores = jnp.where(valid, scores, -1e30)
    expo = jnp.exp(scores - jnp.max(scores, -1, keepdims=True))
    return expo / jnp.sum(expo, -1, keepdims=True)


def attend_kernel(ns, nb, length, h1, wq, bias, qkv, o, w, sem):
    tokens, width = h1.shape
    share = o.shape[1]
    rows = tokens // ns
    load_rows(ns, nb, width // (ns * nb), wq, w, sem)
    pltpu.make_async_copy(w, w, sem).wait()
    wide = min(512, 3 * share)

    def project(j, carry):
        cols = pl.ds(pl.multiple_of(j * wide, wide), wide)
        for r in range(0, tokens, 256):
            part = jnp.dot(h1[r : r + 256, :], w[:, cols], preferred_element_type=F32)
            qkv[r : r + 256, cols] = (part + bias[:, cols]).astype(BF)
        return carry

    lax.fori_loop(0, 3 * share // wide, project, 0)
    limit = length[0]

    def head(h, carry):
        at = h * HEAD_DIM
        col_q = pl.ds(pl.multiple_of(at, HEAD_DIM), HEAD_DIM)
        col_k = pl.ds(pl.multiple_of(share + at, HEAD_DIM), HEAD_DIM)
        col_v = pl.ds(pl.multiple_of(2 * share + at, HEAD_DIM), HEAD_DIM)
        for n in range(ns):
            first = max(n - 1, 0) * rows
            mine, seen = slice(n * rows, n * rows + rows), slice(first, first + 2 * rows)
            probs = soft_block(qkv[mine, col_q], qkv[seen, col_k], n, first, limit)
            part = jnp.dot(probs.astype(BF), qkv[seen, col_v], preferred_element_type=F32)
            o[mine, col_q] = part.astype(BF)
        return carry

    lax.fori_loop(0, share // HEAD_DIM, head, 0)


def attend(ns, nb, lengths, h1, wq, bias):
    tokens, width = h1.shape
    share = wq.shape[2] // 3
    vm = pl.BlockSpec(memory_space=pltpu.VMEM)
    return pl.pallas_call(
        functools.partial(attend_kernel, ns, nb),
        out_shape=(
            jax.ShapeDtypeStruct((tokens, 3 * share), BF),
            jax.ShapeDtypeStruct((tokens, share), BF),
        ),
        in_specs=[pl.BlockSpec(memory_space=pltpu.SMEM), vm, pl.BlockSpec(memory_space=pl.ANY), vm],
        out_specs=(vm, vm),
        scratch_shapes=[pltpu.VMEM((width, 3 * share), BF), pltpu.SemaphoreType.DMA],
        compiler_params=pltpu.CompilerParams(vmem_limit_bytes=56 * 2**20),
        cost_estimate=pl.CostEstimate(
            flops=6 * tokens * width * share, bytes_accessed=2 * wq.size, transcendentals=tokens * 512 * share // 128
        ),
        name="attend",
    )(lengths, h1, wq, bias)


def attend_back_kernel(ns, nb, length, h1, da, wout, o, qkv, packed, dproj, gqv, h1t, do, gw, gwo, acc_k, acc_v, sems):
    tokens, width = h1.shape
    share = o.shape[1]
    rows = tokens // ns
    depth = width // (ns * nb)
    scale = HEAD_DIM ** (-0.5)
    limit = length[0]
    for r in range(0, tokens, 256):
        h1t[:, r : r + 256] = h1[r : r + 256, :].T
        do[r : r + 256, :] = dot_t(da[r : r + 256, :], wout[...]).astype(BF)
    ot = o[...].T
    for c in range(0, width, 512):
        gwo[:, c : c + 512] = jnp.dot(ot, da[:, c : c + 512], preferred_element_type=F32).astype(BF)

    def store_out(b, carry):
        for p in range(ns):
            pltpu.make_async_copy(
                gwo.at[pl.ds(b * depth, depth), p * share : (p + 1) * share],
                packed.at[b, (3 * ns + p) * depth : (3 * ns + p + 1) * depth, :],
                sems.at[0],
            ).start()
        return carry

    lax.fori_loop(0, nb, store_out, 0)

    def head(h, carry):
        at = h * HEAD_DIM
        col_q = pl.ds(pl.multiple_of(at, HEAD_DIM), HEAD_DIM)
        col_k = pl.ds(pl.multiple_of(share + at, HEAD_DIM), HEAD_DIM)
        col_v = pl.ds(pl.multiple_of(2 * share + at, HEAD_DIM), HEAD_DIM)
        acc_k[...] = jnp.zeros_like(acc_k)
        acc_v[...] = jnp.zeros_like(acc_v)
        for n in range(ns):
            first = max(n - 1, 0) * rows
            mine, seen = slice(n * rows, n * rows + rows), slice(first, first + 2 * rows)
            query, keys, grad = qkv[mine, col_q], qkv[seen, col_k], do[mine, col_q]
            probs = soft_block(query, keys, n, first, limit)
            dp = dot_t(grad, qkv[seen, col_v])
            ds = (probs * (dp - jnp.sum(dp * probs, -1, keepdims=True))).astype(BF)
            dq = jnp.dot(ds, keys, preferred_element_type=F32) * scale
            dproj[mine, col_q] = dq.astype(BF)
            acc_k[seen, :] += t_dot(ds, query)
            acc_v[seen, :] += t_dot(probs.astype(BF), grad)
        dproj[:, col_k] = (acc_k[...] * scale).astype(BF)
        dproj[:, col_v] = acc_v[...].astype(BF)
        return carry

    lax.fori_loop(0, share // HEAD_DIM, head, 0)
    wide = min(512, 3 * share)

    def weights(j, carry):
        cols = pl.ds(pl.multiple_of(j * wide, wide), wide)
        gqv[:, cols] = jnp.sum(dproj[:, cols].astype(F32), 0, keepdims=True)
        for r in range(0, width, 512):
            gw[r : r + 512, cols] = jnp.dot(
                h1t[r : r + 512, :], dproj[:, cols], preferred_element_type=F32
            ).astype(BF)
        return carry

    lax.fori_loop(0, 3 * share // wide, weights, 0)

    def store(k, c):
        s, b = k // nb, lax.rem(k, nb)
        for t in range(3):
            pltpu.make_async_copy(
                gw.at[pl.ds(k * depth, depth), t * share : (t + 1) * share],
                packed.at[b, pl.ds((t * ns + s) * depth, depth), :],
                sems.at[1],
            ).start()
        return c

    lax.fori_loop(0, ns * nb, store, 0)
    pltpu.make_async_copy(gw, gw, sems.at[1]).wait()
    pltpu.make_async_copy(gwo, gwo, sems.at[0]).wait()


def attend_back(ns, nb, lengths, h1, da, wout, o, qkv):
    tokens, width = h1.shape
    share = o.shape[1]
    vm = pl.BlockSpec(memory_space=pltpu.VMEM)
    hbm = pl.BlockSpec(memory_space=pl.ANY)
    return pl.pallas_call(
        functools.partial(attend_back_kernel, ns, nb),
        out_shape=(
            jax.ShapeDtypeStruct((nb, 4 * width // nb, share), BF),
            jax.ShapeDtypeStruct((tokens, 3 * share), BF),
            jax.ShapeDtypeStruct((1, 3 * share), F32),
        ),
        in_specs=[pl.BlockSpec(memory_space=pltpu.SMEM), vm, vm, vm, vm, vm],
        out_specs=(hbm, vm, vm),
        scratch_shapes=[
            pltpu.VMEM((width, tokens), BF),
            pltpu.VMEM((tokens, share), BF),
            pltpu.VMEM((width, 3 * share), BF),
            pltpu.VMEM((share, width), BF),
            pltpu.VMEM((tokens, HEAD_DIM), F32),
            pltpu.VMEM((tokens, HEAD_DIM), F32),
            pltpu.SemaphoreType.DMA((2,)),
        ],
        compiler_params=pltpu.CompilerParams(vmem_limit_bytes=56 * 2**20),
        cost_estimate=pl.CostEstimate(
            flops=12 * tokens * width * share, bytes_accessed=12 * width * share, transcendentals=tokens * 512 * share // 128
        ),
        name="attend_back",
    )(lengths, h1, da, wout, o, qkv)


def ff_kernel(ns, nb, h2, cot, wg, bias, gwg, g_out, du_out, gb, w1, w2, h2t, gw1, gw2, sems):
    tokens, width = h2.shape
    chunk = g_out.shape[1]
    depth = width // (ns * nb)
    part = chunk // nb
    pieces = width // chunk
    half = ns * depth
    tile = min(512, chunk)
    tiles = chunk // tile
    step = min(256, tokens)

    def load1(k, carry):
        s, b = k // nb, lax.rem(k, nb)
        pltpu.make_async_copy(
            wg.at[b, pl.ds(s * depth, depth), :], w1.at[pl.ds(k * depth, depth), :], sems.at[0]
        ).start()
        return carry

    def load2(k, carry):
        for p in range(pieces):
            pltpu.make_async_copy(
                wg.at[k, pl.ds(half + p * part, part), :],
                w2.at[pl.ds(k * part, part), p * chunk : (p + 1) * chunk],
                sems.at[1],
            ).start()
        return carry

    lax.fori_loop(0, ns * nb, load1, 0)
    lax.fori_loop(0, nb, load2, 0)
    for r in range(0, tokens, step):
        h2t[:, r : r + step] = h2[r : r + step, :].T
    pltpu.make_async_copy(w1, w1, sems.at[0]).wait()
    pltpu.make_async_copy(w2, w2, sems.at[1]).wait()

    def one_tile(j, carry):
        at = pl.multiple_of(j * tile, tile)
        cols = pl.ds(at, tile)
        total = jnp.zeros((1, tile), F32)
        for r in range(0, tokens, step):
            rows = slice(r, r + step)
            u = jnp.dot(h2[rows, :], w1[:, cols], preferred_element_type=F32) + bias[:, cols]
            dg = lax.dot_general(
                cot[rows, :], w2[cols, :], (((1,), (1,)), ((), ())), preferred_element_type=F32
            )
            sq = u * u
            th = jnp.tanh(ROOT * u * (1.0 + 0.044715 * sq))
            cdf = 0.5 * (1.0 + th)
            g_out[rows, cols] = (u * cdf).astype(BF)
            slope = cdf + 0.5 * u * (1.0 - th * th) * (ROOT * (1.0 + 3.0 * 0.044715 * sq))
            du = (dg * slope).astype(BF)
            du_out[rows, cols] = du
            total += jnp.sum(du.astype(F32), 0, keepdims=True)
        gb[:, cols] = total
        for r in range(0, width, 512):
            gw1[j, r : r + 512, :] = jnp.dot(
                h2t[r : r + 512, :], du_out[:, cols], preferred_element_type=F32
            ).astype(BF)
        gt = g_out[:, cols].T
        for r in range(0, width, 512):
            gw2[j, :, r : r + 512] = jnp.dot(
                gt, cot[:, r : r + 512], preferred_element_type=F32
            ).astype(BF)

        def store1(k, c):
            s, b = k // nb, lax.rem(k, nb)
            pltpu.make_async_copy(
                gw1.at[j, pl.ds(k * depth, depth), :],
                gwg.at[b, pl.ds(s * depth, depth), cols],
                sems.at[2],
            ).start()
            return c

        lax.fori_loop(0, ns * nb, store1, 0)
        count = tile // part

        def store2(k, c):
            for p in range(pieces):
                pltpu.make_async_copy(
                    gw2.at[j, pl.ds(k * part, part), p * chunk : (p + 1) * chunk],
                    gwg.at[j * count + k, pl.ds(half + p * part, part), :],
                    sems.at[3],
                ).start()
            return c

        lax.fori_loop(0, count, store2, 0)
        return carry

    lax.fori_loop(0, tiles, one_tile, 0)
    pltpu.make_async_copy(gw1, gw1, sems.at[2]).wait()
    pltpu.make_async_copy(gw2, gw2, sems.at[3]).wait()


def ff_chunk(ns, nb, h2, cot, wg, bias):
    tokens, width = h2.shape
    chunk = wg.shape[2]
    tile = min(512, chunk)
    vm = pl.BlockSpec(memory_space=pltpu.VMEM)
    hbm = pl.BlockSpec(memory_space=pl.ANY)
    return pl.pallas_call(
        functools.partial(ff_kernel, ns, nb),
        out_shape=(
            jax.ShapeDtypeStruct(wg.shape, BF),
            jax.ShapeDtypeStruct((tokens, chunk), BF),
            jax.ShapeDtypeStruct((tokens, chunk), BF),
            jax.ShapeDtypeStruct((1, chunk), F32),
        ),
        in_specs=[vm, vm, hbm, vm],
        out_specs=(hbm, vm, vm, vm),
        scratch_shapes=[
            pltpu.VMEM((width, chunk), BF),
            pltpu.VMEM((chunk, width), BF),
            pltpu.VMEM((width, tokens), BF),
            pltpu.VMEM((chunk // tile, width, tile), BF),
            pltpu.VMEM((chunk // tile, tile, width), BF),
            pltpu.SemaphoreType.DMA((4,)),
        ],
        compiler_params=pltpu.CompilerParams(vmem_limit_bytes=56 * 2**20),
        cost_estimate=pl.CostEstimate(
            flops=8 * tokens * width * chunk, bytes_accessed=4 * wg.size, transcendentals=tokens * chunk
        ),
        name="ff_chunk",
    )(h2, cot, wg, bias)


MESH = pl.DeviceIdType.MESH


def greet():
    me, batch = lax.axis_index("seq"), lax.axis_index("batch")
    by_x = me + 1 - 2 * lax.rem(me, 2)
    by_y = lax.rem(me + 2, 4)
    barrier = pltpu.get_barrier_semaphore()
    for other in (by_x, by_y):
        pl.semaphore_signal(barrier, inc=1, device_id=(other, batch), device_id_type=MESH)
    pl.semaphore_wait(barrier, 2)
    return me, by_x, by_y, (by_x, batch), (by_y, batch)


def scatter_sum(partial, place, buffers, send, recv):
    me, by_x, by_y, to_x, to_y = place
    out, via, from_x, from_y = buffers
    half = via.shape[1]
    top, low = slice(0, half), slice(half, 2 * half)
    far = 3 - me

    def copy(k, src, dst, to):
        one = pltpu.make_async_remote_copy(
            src_ref=src, dst_ref=dst, send_sem=send.at[k], recv_sem=recv.at[k], device_id=to, device_id_type=MESH
        )
        one.start()
        return one

    out[0, top] = partial(far, 0).astype(BF)
    c0 = copy(0, out.at[0, top], via.at[0], to_y)
    out[0, low] = partial(far, 1).astype(BF)
    c1 = copy(1, out.at[0, low], via.at[1], to_x)
    out[1, low] = partial(by_x, 1).astype(BF)
    c2 = copy(2, out.at[1, low], from_x.at[low], to_x)
    out[2, top] = partial(by_y, 0).astype(BF)
    c3 = copy(3, out.at[2, top], from_y.at[top], to_y)
    x_top = partial(by_x, 0)
    c0.wait_recv()
    out[1, top] = (x_top + via[0].astype(F32)).astype(BF)
    c4 = copy(4, out.at[1, top], from_x.at[top], to_x)
    y_low = partial(by_y, 1)
    c1.wait_recv()
    out[2, low] = (y_low + via[1].astype(F32)).astype(BF)
    c5 = copy(5, out.at[2, low], from_y.at[low], to_y)
    mine_top, mine_low = partial(me, 0), partial(me, 1)
    c3.wait_recv()
    c4.wait_recv()
    mine_top = mine_top + from_x[top].astype(F32) + from_y[top].astype(F32)
    c2.wait_recv()
    c5.wait_recv()
    mine_low = mine_low + from_x[low].astype(F32) + from_y[low].astype(F32)
    for one in (c0, c1, c2, c3, c4, c5):
        one.wait_send()
    return mine_top, mine_low


def scatter_scratch(rows, width):
    return [
        pltpu.VMEM((3, rows, width), BF),
        pltpu.VMEM((2, rows // 2, width), BF),
        pltpu.VMEM((rows, width), BF),
        pltpu.VMEM((rows, width), BF),
        pltpu.SemaphoreType.DMA((6,)),
        pltpu.SemaphoreType.DMA((6,)),
    ]


def gather_blocks(full, rows, place, send, recv):
    me, by_x, by_y, to_x, to_y = place
    half = rows // 2

    def copy(k, block, part, to):
        at = full.at[pl.ds(pl.multiple_of(block * rows + part * half, half), half)]
        one = pltpu.make_async_remote_copy(
            src_ref=at, dst_ref=at, send_sem=send.at[k], recv_sem=recv.at[k], device_id=to, device_id_type=MESH
        )
        one.start()
        return one

    c0 = copy(0, me, 0, to_x)
    c3 = copy(3, me, 1, to_y)
    c2 = copy(2, me, 0, to_y)
    c1 = copy(1, me, 1, to_x)
    c0.wait_recv()
    c4 = copy(4, by_x, 0, to_y)
    c3.wait_recv()
    c5 = copy(5, by_y, 1, to_x)
    for one in (c1, c2, c4, c5):
        one.wait_recv()
    for one in (c0, c1, c2, c3, c4, c5):
        one.wait_send()


GATHER_SEMS = [pltpu.SemaphoreType.DMA((6,)), pltpu.SemaphoreType.DMA((6,))]


def middle_kernel(o, wout, mine, obias, gain, shift, x1, h2, out, via, from_x, from_y, s1, r1, s2, r2):
    rows, width = mine.shape
    half = rows // 2
    place = greet()

    def partial(block, part):
        at = pl.multiple_of(block * rows + part * half, half)
        return jnp.dot(o[pl.ds(at, half), :], wout[...], preferred_element_type=F32)

    sums = scatter_sum(partial, place, (out, via, from_x, from_y), s1, r1)
    for part, total in enumerate(sums):
        span = slice(part * half, part * half + half)
        res = mine[span, :].astype(F32) + (total + obias[...])
        x1[span, :] = res
        normed, _ = norm_stats(res)
        at = pl.multiple_of(place[0] * rows + part * half, half)
        h2[pl.ds(at, half), :] = (normed * gain[...] + shift[...]).astype(BF)
    gather_blocks(h2, rows, place, s2, r2)


def middle(o, wout, mine, obias, gain, shift):
    tokens, share = o.shape
    rows, width = mine.shape
    vm = pl.BlockSpec(memory_space=pltpu.VMEM)
    return pl.pallas_call(
        middle_kernel,
        out_shape=(jax.ShapeDtypeStruct((rows, width), F32), jax.ShapeDtypeStruct((tokens, width), BF)),
        in_specs=[vm] * 6,
        out_specs=(vm, vm),
        scratch_shapes=scatter_scratch(rows, width) + GATHER_SEMS,
        compiler_params=pltpu.CompilerParams(collective_id=1, has_side_effects=True, vmem_limit_bytes=56 * 2**20),
        cost_estimate=pl.CostEstimate(flops=40 * 10**9, bytes_accessed=12 * tokens * width, transcendentals=0),
        name="project_out",
    )(o, wout, mine, obias, gain, shift)


def ff_back_kernel(ns, nb, count, *refs):
    dus, wgs = refs[:count], refs[count : 2 * count]
    x1, cot, gain, dx1, da, ggain, gshift, gob = refs[2 * count : 2 * count + 8]
    ws = refs[2 * count + 8 : 3 * count + 8]
    load_sem, out, via, from_x, from_y, s1, r1, s2, r2 = refs[3 * count + 8 :]
    rows, width = x1.shape
    half = rows // 2
    for c in range(count):
        load_rows(ns, nb, width // (ns * nb), wgs[c], ws[c], load_sem.at[c])
    place = greet()
    for c in range(count):
        pltpu.make_async_copy(ws[c], ws[c], load_sem.at[c]).wait()

    def partial(block, part):
        at = pl.multiple_of(block * rows + part * half, half)
        total = dot_t(dus[0][pl.ds(at, half), :], ws[0][...])
        for c in range(1, count):
            total += dot_t(dus[c][pl.ds(at, half), :], ws[c][...])
        return total

    sums = scatter_sum(partial, place, (out, via, from_x, from_y), s1, r1)
    totals = [jnp.zeros((1, width), F32)] * 3
    for part, grad in enumerate(sums):
        span = slice(part * half, part * half + half)
        normed, rstd = norm_stats(x1[span, :])
        res = cot[span, :].astype(F32) + norm_back(grad, normed, rstd, gain[...])
        dx1[span, :] = res
        low = res.astype(BF)
        at = pl.multiple_of(place[0] * rows + part * half, half)
        da[pl.ds(at, half), :] = low
        for k, term in enumerate((grad * normed, grad, low.astype(F32))):
            totals[k] += jnp.sum(term, 0, keepdims=True)
    ggain[...], gshift[...], gob[...] = totals
    gather_blocks(da, rows, place, s2, r2)


def ff_back(ns, nb, dus, wgs, x1, cot, gain):
    rows, width = x1.shape
    tokens, chunk = dus[0].shape
    count = len(dus)
    vm = pl.BlockSpec(memory_space=pltpu.VMEM)
    hbm = pl.BlockSpec(memory_space=pl.ANY)
    row = jax.ShapeDtypeStruct((1, width), F32)
    return pl.pallas_call(
        functools.partial(ff_back_kernel, ns, nb, count),
        out_shape=(
            jax.ShapeDtypeStruct((rows, width), F32),
            jax.ShapeDtypeStruct((tokens, width), BF),
            row,
            row,
            row,
        ),
        in_specs=[vm] * count + [hbm] * count + [vm] * 3,
        out_specs=(vm,) * 5,
        scratch_shapes=[pltpu.VMEM((width, chunk), BF)] * count
        + [pltpu.SemaphoreType.DMA((count,))]
        + scatter_scratch(rows, width)
        + GATHER_SEMS,
        compiler_params=pltpu.CompilerParams(collective_id=2, has_side_effects=True, vmem_limit_bytes=56 * 2**20),
        cost_estimate=pl.CostEstimate(flops=40 * 10**9, bytes_accessed=12 * tokens * width, transcendentals=0),
        name="ff_back",
    )(*dus, *wgs, x1, cot, gain)


def finish_kernel(ns, nb, dproj, wq, mine, dx1, gain, gx, ggain, gshift, w, load_sem, out, via, from_x, from_y, s1, r1):
    rows, width = mine.shape
    half = rows // 2
    load_rows(ns, nb, width // (ns * nb), wq, w, load_sem)
    place = greet()
    pltpu.make_async_copy(w, w, load_sem).wait()

    def partial(block, part):
        at = pl.multiple_of(block * rows + part * half, half)
        return dot_t(dproj[pl.ds(at, half), :], w[...])

    sums = scatter_sum(partial, place, (out, via, from_x, from_y), s1, r1)
    totals = [jnp.zeros((1, width), F32)] * 2
    for part, grad in enumerate(sums):
        span = slice(part * half, part * half + half)
        normed, rstd = norm_stats(mine[span, :].astype(F32))
        gx[span, :] = dx1[span, :] + norm_back(grad, normed, rstd, gain[...])
        for k, term in enumerate((grad * normed, grad)):
            totals[k] += jnp.sum(term, 0, keepdims=True)
    ggain[...], gshift[...] = totals


def finish(ns, nb, dproj, wq, mine, dx1, gain):
    rows, width = mine.shape
    vm = pl.BlockSpec(memory_space=pltpu.VMEM)
    row = jax.ShapeDtypeStruct((1, width), F32)
    return pl.pallas_call(
        functools.partial(finish_kernel, ns, nb),
        out_shape=(jax.ShapeDtypeStruct((rows, width), F32), row, row),
        in_specs=[vm, pl.BlockSpec(memory_space=pl.ANY), vm, vm, vm],
        out_specs=(vm,) * 3,
        scratch_shapes=[pltpu.VMEM((width, wq.shape[2]), BF), pltpu.SemaphoreType.DMA] + scatter_scratch(rows, width),
        compiler_params=pltpu.CompilerParams(collective_id=3, has_side_effects=True, vmem_limit_bytes=56 * 2**20),
        cost_estimate=pl.CostEstimate(flops=20 * 10**9, bytes_accessed=12 * rows * width, transcendentals=0),
        name="attend_input",
    )(dproj, wq, mine, dx1, gain)


def ff_out_kernel(nb, count, *refs):
    gs, wgs = refs[:count], refs[count : 2 * count]
    x1, bias, result = refs[2 * count : 2 * count + 3]
    ws = refs[2 * count + 3 : 3 * count + 3]
    load_sem, out, via, from_x, from_y, s1, r1 = refs[3 * count + 3 :]
    rows, width = x1.shape
    half = rows // 2
    chunk = gs[0].shape[1]
    part_rows, pieces, base = chunk // nb, width // chunk, width // nb
    for c in range(count):

        def load(k, carry):
            for p in range(pieces):
                pltpu.make_async_copy(
                    wgs[c].at[k, pl.ds(base + p * part_rows, part_rows), :],
                    ws[c].at[pl.ds(k * part_rows, part_rows), p * chunk : (p + 1) * chunk],
                    load_sem.at[c],
                ).start()
            return carry

        lax.fori_loop(0, nb, load, 0)
    place = greet()
    for c in range(count):
        pltpu.make_async_copy(ws[c], ws[c], load_sem.at[c]).wait()

    def partial(block, part):
        at = pl.multiple_of(block * rows + part * half, half)
        total = jnp.dot(gs[0][pl.ds(at, half), :], ws[0][...], preferred_element_type=F32)
        for c in range(1, count):
            total += jnp.dot(gs[c][pl.ds(at, half), :], ws[c][...], preferred_element_type=F32)
        return total

    sums = scatter_sum(partial, place, (out, via, from_x, from_y), s1, r1)
    for part, total in enumerate(sums):
        span = slice(part * half, part * half + half)
        result[span, :] = (x1[span, :] + (total + bias[...])).astype(BF)


def ff_out(nb, gs, wgs, x1, bias):
    rows, width = x1.shape
    chunk = gs[0].shape[1]
    count = len(gs)
    vm = pl.BlockSpec(memory_space=pltpu.VMEM)
    hbm = pl.BlockSpec(memory_space=pl.ANY)
    return pl.pallas_call(
        functools.partial(ff_out_kernel, nb, count),
        out_shape=jax.ShapeDtypeStruct((rows, width), BF),
        in_specs=[vm] * count + [hbm] * count + [vm] * 2,
        out_specs=vm,
        scratch_shapes=[pltpu.VMEM((chunk, width), BF)] * count
        + [pltpu.SemaphoreType.DMA((count,))]
        + scatter_scratch(rows, width),
        compiler_params=pltpu.CompilerParams(collective_id=4, has_side_effects=True, vmem_limit_bytes=56 * 2**20),
        cost_estimate=pl.CostEstimate(flops=20 * 10**9, bytes_accessed=12 * rows * width, transcendentals=0),
        name="ff_out",
    )(*gs, *wgs, x1, bias)


def greet_all(ns, nb):
    me, batch = lax.axis_index("seq"), lax.axis_index("batch")
    along_seq = [(lax.rem(me + d, ns), batch) for d in range(1, ns)]
    along_batch = [(me, lax.rem(batch + d, nb)) for d in range(1, nb)]
    barrier = pltpu.get_barrier_semaphore()
    for other in along_seq + along_batch:
        pl.semaphore_signal(barrier, inc=1, device_id=other, device_id_type=MESH)
    pl.semaphore_wait(barrier, ns + nb - 2)
    return me, batch, along_seq, along_batch


def send(src, dst, sends, recvs, to):
    one = pltpu.make_async_remote_copy(
        src_ref=src, dst_ref=dst, send_sem=sends, recv_sem=recvs, device_id=to, device_id_type=MESH
    )
    one.start()
    return one


def spread_kernel(ns, nb, w_qkv, vec, packed, vecs, local, s0, r0, s1, r1, s2, r2):
    depth = w_qkv.shape[0]
    share = packed.shape[1] // 3
    width = ns * share
    me, batch, along_seq, along_batch = greet_all(ns, nb)
    own = pltpu.make_async_copy(vec, vecs.at[batch, me], local.at[3])
    own.start()
    small = [send(vec, vecs.at[batch, me], s1.at[d], r1.at[d], to) for d, to in enumerate(along_seq)]
    rows = pl.ds(pl.multiple_of(me * depth, depth), depth)
    copies = []
    for t in range(3):
        keep = pl.ds(pl.multiple_of(t * width + me * share, share), share)
        here = packed.at[rows, t * share : (t + 1) * share]
        one = pltpu.make_async_copy(w_qkv.at[:, keep], here, local.at[t])
        one.start()
        copies.append(one)
        for d, to in enumerate(along_seq):
            cols = pl.ds(pl.multiple_of(t * width + to[0] * share, share), share)
            copies.append(send(w_qkv.at[:, cols], here, s0.at[t, d], r0.at[t, d], to))
    for one in small:
        one.wait_recv()
    own.wait()
    far = [send(vecs.at[batch], vecs.at[batch], s2.at[d], r2.at[d], to) for d, to in enumerate(along_batch)]
    for one in small:
        one.wait_send()
    for one in copies + far:
        one.wait()


def spread(ns, nb, w_qkv, vec):
    depth, width = w_qkv.shape
    hbm = pl.BlockSpec(memory_space=pl.ANY)
    dma = pltpu.SemaphoreType.DMA
    return pl.pallas_call(
        functools.partial(spread_kernel, ns, nb),
        out_shape=(
            jax.ShapeDtypeStruct((ns * depth, width // ns), BF),
            jax.ShapeDtypeStruct((nb, ns) + vec.shape, F32),
        ),
        in_specs=[hbm, hbm],
        out_specs=(hbm, hbm),
        scratch_shapes=[
            dma((4,)),
            dma((3, ns - 1)),
            dma((3, ns - 1)),
            dma((ns - 1,)),
            dma((ns - 1,)),
            dma((nb - 1,)),
            dma((nb - 1,)),
        ],
        compiler_params=pltpu.CompilerParams(collective_id=5, has_side_effects=True),
        cost_estimate=pl.CostEstimate(flops=5 * 10**9, bytes_accessed=2 * w_qkv.size, transcendentals=0),
        name="spread_qkv",
    )(w_qkv, vec)


def collect_kernel(ns, nb, parts, w1, w2, mine, cot, gain, shift, *refs):
    packs = refs[:parts]
    h1, cots, acts, local, s0, r0, s1, r1, s2, r2 = refs[parts:]
    depth = w1.shape[0]
    rows, width = mine.shape
    half = rows // 2
    hidden = w1.shape[1] // ns
    part = hidden // (parts * nb)
    chunk = hidden // parts
    pieces = width // chunk
    me, batch = lax.axis_index("seq"), lax.axis_index("batch")
    by_x = me + 1 - 2 * lax.rem(me, 2)
    by_y = lax.rem(me + 2, 4)
    others = [(lax.rem(me + d, ns), batch) for d in range(1, ns)]
    barrier = pltpu.get_barrier_semaphore()
    for other in others:
        pl.semaphore_signal(barrier, inc=1, device_id=other, device_id_type=MESH)
    at_me = pl.ds(pl.multiple_of(me * rows, rows), rows)
    acts[at_me, :] = mine[...]
    own = pltpu.make_async_copy(cot, cots.at[at_me], local.at[parts])
    own.start()
    for c in range(parts):
        for p in range(pieces):
            pltpu.make_async_copy(
                w2.at[c * part : (c + 1) * part, p * chunk : (p + 1) * chunk],
                packs[c].at[ns * depth + p * part : ns * depth + (p + 1) * part, :],
                local.at[c],
            ).start()
    at = pl.ds(pl.multiple_of(me * depth, depth), depth)

    def keep(b, carry):
        for c in range(parts):
            cols = pl.ds(pl.multiple_of(me * hidden + (b * parts + c) * part, part), part)
            here = packs[c].at[at, pl.ds(pl.multiple_of(b * part, part), part)]
            pltpu.make_async_copy(w1.at[:, cols], here, local.at[c]).start()
        return carry

    lax.fori_loop(0, nb, keep, 0)
    pl.semaphore_wait(barrier, ns - 1)
    to_x, to_y = (by_x, batch), (by_y, batch)

    def ship(b, carry):
        for c in range(parts):
            here = packs[c].at[at, pl.ds(pl.multiple_of(b * part, part), part)]
            for d, to in enumerate(others):
                cols = pl.ds(pl.multiple_of(to[0] * hidden + (b * parts + c) * part, part), part)
                send(w1.at[:, cols], here, s0.at[c, d], r0.at[c, d], to)
        return carry

    lax.fori_loop(0, nb, ship, 0)

    def normalise(block):
        span = pl.ds(pl.multiple_of(block * rows, rows), rows)
        normed, _ = norm_stats(acts[span, :].astype(F32))
        h1[span, :] = (normed * gain[...] + shift[...]).astype(BF)

    def copy(k, full, block, side, to, sends, recvs):
        span = full.at[pl.ds(pl.multiple_of(block * rows + side * half, half), half)]
        return send(span, span, sends.at[k], recvs.at[k], to)

    c0 = copy(0, acts, me, 0, to_x, s1, r1)
    c3 = copy(3, acts, me, 1, to_y, s1, r1)
    c2 = copy(2, acts, me, 0, to_y, s1, r1)
    c1 = copy(1, acts, me, 1, to_x, s1, r1)
    normalise(me)
    c0.wait_recv()
    c4 = copy(4, acts, by_x, 0, to_y, s1, r1)
    c3.wait_recv()
    c5 = copy(5, acts, by_y, 1, to_x, s1, r1)
    own.wait()
    d0 = copy(0, cots, me, 0, to_x, s2, r2)
    d3 = copy(3, cots, me, 1, to_y, s2, r2)
    d2 = copy(2, cots, me, 0, to_y, s2, r2)
    d1 = copy(1, cots, me, 1, to_x, s2, r2)
    c1.wait_recv()
    normalise(by_x)
    c2.wait_recv()
    normalise(by_y)
    c4.wait_recv()
    c5.wait_recv()
    normalise(3 - me)
    d0.wait_recv()
    d4 = copy(4, cots, by_x, 0, to_y, s2, r2)
    d3.wait_recv()
    d5 = copy(5, cots, by_y, 1, to_x, s2, r2)
    for one in (d1, d2, d4, d5):
        one.wait_recv()
    for one in (c0, c1, c2, c3, c4, c5, d0, d1, d2, d3, d4, d5):
        one.wait_send()
    for c in range(parts):
        pack = packs[c].at[: depth]
        for d, to in enumerate(others):
            rest = pltpu.make_async_remote_copy(
                src_ref=pack, dst_ref=pack, send_sem=s0.at[c, d], recv_sem=r0.at[c, d], device_id=to, device_id_type=MESH
            )
            rest.wait()
        whole = packs[c].at[: depth + pieces * part]
        pltpu.make_async_copy(whole, whole, local.at[c]).wait()


def collect(ns, nb, parts, w1, w2, mine, cot, gain, shift):
    depth = w1.shape[0]
    rows, width = mine.shape
    chunk = w1.shape[1] // (ns * parts)
    vm = pl.BlockSpec(memory_space=pltpu.VMEM)
    hbm = pl.BlockSpec(memory_space=pl.ANY)
    dma = pltpu.SemaphoreType.DMA
    pack = jax.ShapeDtypeStruct((2 * ns * depth, chunk), BF)
    full = jax.ShapeDtypeStruct((ns * rows, width), BF)
    return pl.pallas_call(
        functools.partial(collect_kernel, ns, nb, parts),
        out_shape=(pack,) * parts + (full, full),
        in_specs=[hbm, hbm, vm, hbm, vm, vm],
        out_specs=(hbm,) * parts + (vm, hbm),
        scratch_shapes=[
            pltpu.VMEM((ns * rows, width), BF),
            dma((parts + 1,)),
            dma((parts, ns - 1)),
            dma((parts, ns - 1)),
            dma((6,)),
            dma((6,)),
            dma((6,)),
            dma((6,)),
        ],
        compiler_params=pltpu.CompilerParams(collective_id=6, has_side_effects=True, vmem_limit_bytes=40 * 2**20),
        cost_estimate=pl.CostEstimate(flops=40 * 10**9, bytes_accessed=12 * rows * width, transcendentals=0),
        name="collect",
    )(w1, w2, mine, cot, gain, shift)


def small_kernel(ns, nb, sums, result, near, mid, far, s1, r1, s2, r2):
    me, batch, along_seq, along_batch = greet_all(ns, nb)
    copies = [send(sums.at[to[1]], near.at[d], s1.at[d], r1.at[d], to) for d, to in enumerate(along_batch)]
    total = sums[batch]
    for d, one in enumerate(copies):
        one.wait_recv()
        total += near[d]
    mid[...] = total
    more = [send(mid.at[to[0]], far.at[d], s2.at[d], r2.at[d], to) for d, to in enumerate(along_seq)]
    total = mid[me]
    for d, one in enumerate(more):
        one.wait_recv()
        total += far[d]
    result[...] = total
    for one in copies + more:
        one.wait_send()


def small_sums(ns, nb, sums):
    tail = sums.shape[2:]
    vm = pl.BlockSpec(memory_space=pltpu.VMEM)
    dma = pltpu.SemaphoreType.DMA
    return pl.pallas_call(
        functools.partial(small_kernel, ns, nb),
        out_shape=jax.ShapeDtypeStruct(tail, F32),
        in_specs=[vm],
        out_specs=vm,
        scratch_shapes=[
            pltpu.VMEM((nb - 1, ns) + tail, F32),
            pltpu.VMEM((ns,) + tail, F32),
            pltpu.VMEM((ns - 1,) + tail, F32),
            dma((nb - 1,)),
            dma((nb - 1,)),
            dma((ns - 1,)),
            dma((ns - 1,)),
        ],
        compiler_params=pltpu.CompilerParams(collective_id=7, has_side_effects=True),
        cost_estimate=pl.CostEstimate(flops=5 * 10**9, bytes_accessed=4 * sums.size, transcendentals=0),
        name="small_sums",
    )(sums)


def home_kernel(ns, summed, gqkv, gout, stage, local, s0, r0):
    depth, width = gout.shape
    share = width // ns
    me, batch = lax.axis_index("seq"), lax.axis_index("batch")
    others = [(lax.rem(me + d, ns), batch) for d in range(1, ns)]
    barrier = pltpu.get_barrier_semaphore()
    for other in others:
        pl.semaphore_signal(barrier, inc=1, device_id=other, device_id_type=MESH)
    pl.semaphore_wait(barrier, ns - 1)
    copies = []
    for t in range(3):
        cols = pl.ds(pl.multiple_of(t * width + me * share, share), share)
        for d, to in enumerate(others):
            rows = pl.ds(pl.multiple_of((t * ns + to[0]) * depth, depth), depth)
            copies.append(send(summed.at[rows], stage.at[:, cols], s0.at[t, d], r0.at[t, d], to))
        rows = pl.ds(pl.multiple_of((t * ns + me) * depth, depth), depth)
        own = pltpu.make_async_copy(summed.at[rows], stage.at[:, cols], local.at[t])
        own.start()
        copies.append(own)
    for p in range(ns):
        rows = slice((3 * ns + p) * depth, (3 * ns + p + 1) * depth)
        gout[:, p * share : (p + 1) * share] = summed[rows, :].astype(F32)
    for one in copies:
        one.wait()
    gqkv[...] = stage[...].astype(F32)


def home(ns, summed):
    rows, share = summed.shape
    depth, width = rows // (4 * ns), ns * share
    vm = pl.BlockSpec(memory_space=pltpu.VMEM)
    dma = pltpu.SemaphoreType.DMA
    return pl.pallas_call(
        functools.partial(home_kernel, ns),
        out_shape=(jax.ShapeDtypeStruct((depth, 3 * width), F32), jax.ShapeDtypeStruct((depth, width), F32)),
        in_specs=[vm],
        out_specs=(vm, vm),
        scratch_shapes=[pltpu.VMEM((depth, 3 * width), BF), dma((3,)), dma((3, ns - 1)), dma((3, ns - 1))],
        compiler_params=pltpu.CompilerParams(collective_id=8, has_side_effects=True),
        cost_estimate=pl.CostEstimate(flops=5 * 10**9, bytes_accessed=4 * summed.size, transcendentals=0),
        name="home",
    )(summed)


PARTS = 2


def gather_seq(value):
    return lax.all_gather(value, "seq", axis=0, tiled=True)


def scatter_seq(partial):
    return lax.psum_scatter(partial, "seq", scatter_dimension=0, tiled=True)


def scatter_batch(parts):
    flat = parts.reshape(-1, parts.shape[-1])
    return lax.psum_scatter(flat, "batch", scatter_dimension=0, tiled=True)


def unpermute(ns, nb, gathered):
    depth = gathered.shape[1] // ns
    return gathered.reshape(nb, ns, depth, -1).transpose(1, 0, 2, 3).reshape(ns * nb * depth, -1)


def body(
    block_input,
    lengths,
    ln1_gain,
    ln1_bias,
    w_qkv,
    qv_bias,
    w_out,
    out_bias,
    ln2_gain,
    ln2_bias,
    w_fc1,
    fc1_bias,
    w_fc2,
    fc2_bias,
    out_cotangent,
):
    ns, nb = lax.axis_size("seq"), lax.axis_size("batch")
    seq = lax.axis_index("seq")
    rows, width = block_input.shape[1:]
    share = width // ns
    depth = width // (ns * nb)
    hidden = w_fc1.shape[1] // ns
    chunk = hidden // PARTS
    part = chunk // nb
    pieces = width // chunk
    planar = ns == 4 and part % 128 == 0
    mine, cot_mine = block_input[0], out_cotangent[0]

    vectors = (ln1_gain, ln1_bias, qv_bias, out_bias, ln2_gain, ln2_bias, fc1_bias, fc2_bias)
    vector = jnp.concatenate(vectors).astype(F32)
    wout = lax.all_gather(w_out, "batch", axis=0, tiled=True)
    if planar:
        padded = jnp.pad(vector, (0, 1024 - vector.shape[0])).reshape(8, 128)
        qkv_part, packed = spread(ns, nb, w_qkv, padded)
        packed = packed.transpose(1, 0, 2, 3).reshape(ns * nb, 1024)
    else:
        qkv_part = lax.all_to_all(w_qkv.reshape(depth, 3, ns, share), "seq", 2, 0).reshape(ns * depth, 3 * share)
        packed = lax.all_gather(vector, ("seq", "batch"), axis=0, tiled=False)
    wq = lax.all_gather(qkv_part, "batch", axis=0, tiled=True).reshape(nb, ns * depth, 3 * share)
    full, at = [], 0
    for vec in vectors:
        full.append(packed[:, at : at + vec.shape[0]].reshape(1, -1))
        at += vec.shape[0]
    gain1, shift1, qv, obias, gain2, shift2, bias1, bias2 = full
    bias1 = lax.dynamic_slice_in_dim(bias1, seq * hidden, hidden, 1).reshape(nb, PARTS, part)
    qbias = lax.dynamic_slice_in_dim(qv, seq * share, share, 1)
    vbias = lax.dynamic_slice_in_dim(qv, width + seq * share, share, 1)
    bias3 = jnp.concatenate([qbias, jnp.zeros_like(qbias), vbias], 1)

    if planar:
        *packs, h1, cot = collect(ns, nb, PARTS, w_fc1, w_fc2, mine, cot_mine, gain1, shift1)
    else:
        fc1_part = lax.all_to_all(w_fc1.reshape(depth, ns, hidden), "seq", 1, 0)
        fc1_part = fc1_part.reshape(ns * depth, nb, PARTS, part)
        fc2_part = w_fc2.reshape(PARTS, part, pieces, chunk)
        packs = []
        for c in range(PARTS):
            first = fc1_part[:, :, c].reshape(ns * depth, chunk)
            second = fc2_part[c].transpose(1, 0, 2).reshape(pieces * part, chunk)
            packs.append(jnp.concatenate([first, second], 0))
        h1 = (norm_stats(gather_seq(mine).astype(F32))[0] * gain1 + shift1).astype(BF)
        cot = gather_seq(cot_mine)
    wgs = [lax.all_gather(pack, "batch", axis=0, tiled=True).reshape(nb, -1, chunk) for pack in packs]

    qkv, o = attend(ns, nb, lengths, h1, wq, bias3)
    if planar:
        x1, h2 = middle(o, wout, mine, obias, gain2, shift2)
    else:
        a = scatter_seq(jnp.dot(o, wout, preferred_element_type=F32))
        x1 = mine.astype(F32) + (a + obias)
        h2 = gather_seq((norm_stats(x1)[0] * gain2 + shift2).astype(BF))

    gws, gs, dus, gb1 = [], [], [], []
    for c in range(PARTS):
        gw, g, du, gb = ff_chunk(ns, nb, h2, cot, wgs[c], bias1[:, c].reshape(1, chunk))
        gws.append(scatter_batch(gw))
        gs.append(g)
        dus.append(du)
        gb1.append(gb.reshape(nb, 1, part))
    cot_f = cot_mine.astype(F32)
    if planar:
        dx1, da, ggain2, gshift2, gob = ff_back(ns, nb, dus, wgs, x1, cot_mine, gain2)
    else:
        dh2 = sum(dot_t(du, unpermute(ns, nb, wg[:, : ns * depth])) for du, wg in zip(dus, wgs))
        dh2 = scatter_seq(dh2)
        normed2, rstd2 = norm_stats(x1)
        ggain2 = jnp.sum(dh2 * normed2, 0)
        gshift2 = jnp.sum(dh2, 0)
        dx1 = cot_f + norm_back(dh2, normed2, rstd2, gain2)
        da_mine = dx1.astype(BF)
        gob = jnp.sum(da_mine.astype(F32), 0)
        da = gather_seq(da_mine)

    if planar:
        da, gws[0] = lax.optimization_barrier((da, gws[0]))
    gattn, dproj, gqv = attend_back(ns, nb, lengths, h1, da, wout, o, qkv)
    gattn = scatter_batch(gattn)
    if planar:
        gx, ggain1, gshift1 = finish(ns, nb, dproj, wq, mine, dx1, gain1)
        x1, gws[1] = lax.optimization_barrier((x1, gws[1]))
        out = ff_out(nb, gs, wgs, x1, bias2)
    else:
        dh1 = scatter_seq(dot_t(dproj, unpermute(ns, nb, wq)))
        normed1, rstd1 = norm_stats(mine.astype(F32))
        ggain1 = jnp.sum(dh1 * normed1, 0)
        gshift1 = jnp.sum(dh1, 0)
        gx = dx1 + norm_back(dh1, normed1, rstd1, gain1)
        y = 0.0
        for g, wg in zip(gs, wgs):
            w2 = wg[:, ns * depth :].reshape(nb, pieces, part, chunk).transpose(0, 2, 1, 3).reshape(chunk, width)
            y += jnp.dot(g, w2, preferred_element_type=F32)
        out = (x1 + (scatter_seq(y) + bias2)).astype(BF)

    gw1 = jnp.stack([gw[: ns * depth].reshape(ns, depth, nb, part) for gw in gws], 3)
    gw1 = lax.all_to_all(gw1, "seq", 0, 1).astype(F32).reshape(depth, ns * hidden)
    gw2 = jnp.stack([gw[ns * depth :].reshape(pieces, part, chunk) for gw in gws], 0)
    gw2 = gw2.astype(F32).transpose(0, 2, 1, 3).reshape(PARTS * part, width)
    if planar:
        gwqkv, gwo = home(ns, gattn)
    else:
        gwqkv = gattn[: 3 * ns * depth].reshape(3, ns, depth, share)
        gwqkv = lax.all_to_all(gwqkv, "seq", 1, 2).astype(F32).transpose(1, 0, 2, 3).reshape(depth, 3 * width)
        gwo = gattn[3 * ns * depth :].reshape(ns, depth, share).astype(F32).transpose(1, 0, 2).reshape(depth, width)

    def place(part, size):
        return lax.dynamic_update_slice_in_dim(jnp.zeros((size,), F32), part, seq * part.shape[0], 0)

    gqv = gqv[0]
    gqv = jnp.concatenate([place(gqv[:share], width), place(gqv[2 * share :], width)])
    gb1 = place(jnp.stack(gb1, 1).reshape(-1), ns * hidden)
    gb2 = jnp.sum(cot_f, 0)
    sums = (ggain1, gshift1, gqv, gob, ggain2, gshift2, gb1, gb2)
    sums = jnp.concatenate([t.reshape(ns * nb, -1) for t in sums], 1)
    if planar:
        sums = jnp.pad(sums, ((0, 0), (0, 1024 - sums.shape[1]))).reshape(ns, nb, 8, 128)
        sums = small_sums(ns, nb, sums.transpose(1, 0, 2, 3)).reshape(-1)
    else:
        sums = lax.psum_scatter(sums, ("seq", "batch"), scatter_dimension=0, tiled=True)[0]
    small, at = [], 0
    for vec in vectors:
        small.append(sums[at : at + vec.shape[0]])
        at += vec.shape[0]
    return (
        out[None],
        gx[None],
        small[0],
        small[1],
        gwqkv,
        small[2],
        gwo,
        small[3],
        small[4],
        small[5],
        gw1,
        small[6],
        gw2,
        small[7],
    )


def solution(mesh):
    shard = P(("seq", "batch"))
    shard2 = P(("seq", "batch"), None)
    acts = P("batch", "seq", None)
    return jax.shard_map(
        body,
        mesh=mesh,
        in_specs=(acts, P("batch"), shard, shard, shard2, shard, shard2, shard, shard, shard, shard2, shard, shard2, shard, acts),
        out_specs=(acts, acts, shard, shard, shard2, shard, shard2, shard, shard, shard, shard2, shard, shard2, shard),
        check_vma=False,
    )
```

```python
import functools
import math

import jax
import jax.numpy as jnp
from jax import lax
from jax.experimental import pallas as pl
from jax.experimental.pallas import tpu as pltpu
from jax.sharding import PartitionSpec as P

HEAD_DIM = 128
WINDOW = 256
EPS = 1e-05
BF = jnp.bfloat16
F32 = jnp.float32
ROOT = math.sqrt(2.0 / math.pi)


def norm_stats(values):
    mean = jnp.mean(values, -1, keepdims=True)
    centred = values - mean
    rstd = lax.rsqrt(jnp.mean(centred * centred, -1, keepdims=True) + EPS)
    return centred * rstd, rstd


def norm_back(grad, normed, rstd, gain):
    dn = grad * gain
    return rstd * (
        dn - jnp.mean(dn, -1, keepdims=True) - normed * jnp.mean(dn * normed, -1, keepdims=True)
    )


def dot_t(left, right):
    return lax.dot_general(left, right, (((1,), (1,)), ((), ())), preferred_element_type=F32)


def t_dot(left, right):
    return lax.dot_general(left, right, (((0,), (0,)), ((), ())), preferred_element_type=F32)


def load_rows(ns, nb, depth, src, dst, sem):
    def one(k, carry):
        s, b = k // nb, lax.rem(k, nb)
        pltpu.make_async_copy(
            src.at[b, pl.ds(s * depth, depth), :], dst.at[pl.ds(k * depth, depth), :], sem
        ).start()
        return carry

    lax.fori_loop(0, ns * nb, one, 0)


def load_attention(ns, nb, packed, w, sem):
    share = packed.shape[2]
    depth = packed.shape[1] // (4 * ns)

    def one(k, carry):
        s, b = k // nb, lax.rem(k, nb)
        for t in range(3):
            pltpu.make_async_copy(
                packed.at[b, pl.ds((t * ns + s) * depth, depth), :],
                w.at[pl.ds(k * depth, depth), t * share : (t + 1) * share],
                sem,
            ).start()
        return carry

    lax.fori_loop(0, ns * nb, one, 0)


def load_out(ns, nb, packed, wout, sem):
    share = packed.shape[2]
    depth = packed.shape[1] // (4 * ns)

    def one(b, carry):
        for p in range(ns):
            pltpu.make_async_copy(
                packed.at[b, (3 * ns + p) * depth : (3 * ns + p + 1) * depth, :],
                wout.at[pl.ds(b * depth, depth), p * share : (p + 1) * share],
                sem,
            ).start()
        return carry

    lax.fori_loop(0, nb, one, 0)


def soft_block(query, keys, block, first, length):
    rows, count = query.shape[0], keys.shape[0]
    scores = dot_t(query, keys) * HEAD_DIM ** (-0.5)
    query_pos = block * rows + lax.broadcasted_iota(jnp.int32, (rows, count), 0)
    key_pos = first + lax.broadcasted_iota(jnp.int32, (rows, count), 1)
    back = query_pos - key_pos
    valid = (back >= 0) & (back < WINDOW) & ((key_pos < length) | (back == 0))
    scores = jnp.where(valid, scores, -1e30)
    expo = jnp.exp(scores - jnp.max(scores, -1, keepdims=True))
    return expo / jnp.sum(expo, -1, keepdims=True)


def attend_kernel(ns, nb, length, h1, wq, bias, qkv, o, h1t, w, sem):
    tokens, width = h1.shape
    share = o.shape[1]
    rows = tokens // ns
    load_attention(ns, nb, wq, w, sem)
    for r in range(0, tokens, 256):
        h1t[:, r : r + 256] = h1[r : r + 256, :].T
    pltpu.make_async_copy(w, w, sem).wait()
    wide = min(512, 3 * share)

    def project(j, carry):
        cols = pl.ds(pl.multiple_of(j * wide, wide), wide)
        for r in range(0, tokens, 256):
            part = jnp.dot(h1[r : r + 256, :], w[:, cols], preferred_element_type=F32)
            qkv[r : r + 256, cols] = (part + bias[:, cols]).astype(BF)
        return carry

    lax.fori_loop(0, 3 * share // wide, project, 0)
    limit = length[0]

    def head(h, carry):
        at = h * HEAD_DIM
        col_q = pl.ds(pl.multiple_of(at, HEAD_DIM), HEAD_DIM)
        col_k = pl.ds(pl.multiple_of(share + at, HEAD_DIM), HEAD_DIM)
        col_v = pl.ds(pl.multiple_of(2 * share + at, HEAD_DIM), HEAD_DIM)
        for n in range(ns):
            first = max(n - 1, 0) * rows
            mine, seen = slice(n * rows, n * rows + rows), slice(first, first + 2 * rows)
            probs = soft_block(qkv[mine, col_q], qkv[seen, col_k], n, first, limit)
            part = jnp.dot(probs.astype(BF), qkv[seen, col_v], preferred_element_type=F32)
            o[mine, col_q] = part.astype(BF)
        return carry

    lax.fori_loop(0, share // HEAD_DIM, head, 0)


def attend(ns, nb, lengths, h1, wq, bias):
    tokens, width = h1.shape
    share = wq.shape[2]
    vm = pl.BlockSpec(memory_space=pltpu.VMEM)
    return pl.pallas_call(
        functools.partial(attend_kernel, ns, nb),
        out_shape=(
            jax.ShapeDtypeStruct((tokens, 3 * share), BF),
            jax.ShapeDtypeStruct((tokens, share), BF),
            jax.ShapeDtypeStruct((width, tokens), BF),
        ),
        in_specs=[pl.BlockSpec(memory_space=pltpu.SMEM), vm, pl.BlockSpec(memory_space=pl.ANY), vm],
        out_specs=(vm, vm, vm),
        scratch_shapes=[pltpu.VMEM((width, 3 * share), BF), pltpu.SemaphoreType.DMA],
        compiler_params=pltpu.CompilerParams(vmem_limit_bytes=56 * 2**20),
        cost_estimate=pl.CostEstimate(
            flops=6 * tokens * width * share, bytes_accessed=2 * wq.size, transcendentals=tokens * 512 * share // 128
        ),
        name="attend",
    )(lengths, h1, wq, bias)


def attend_back_kernel(ns, nb, length, h1t, da, wq, o, qkv, packed, dproj, gqv, do, gw, gwo, wout, acc_k, acc_v, sems):
    width, tokens = h1t.shape
    share = o.shape[1]
    rows = tokens // ns
    depth = width // (ns * nb)
    scale = HEAD_DIM ** (-0.5)
    limit = length[0]
    load_out(ns, nb, wq, wout, sems.at[2])
    pltpu.make_async_copy(wout, wout, sems.at[2]).wait()
    for r in range(0, tokens, 256):
        do[r : r + 256, :] = dot_t(da[r : r + 256, :], wout[...]).astype(BF)
    ot = o[...].T
    for c in range(0, width, 512):
        gwo[:, c : c + 512] = jnp.dot(ot, da[:, c : c + 512], preferred_element_type=F32).astype(BF)

    def store_out(b, carry):
        for p in range(ns):
            pltpu.make_async_copy(
                gwo.at[pl.ds(b * depth, depth), p * share : (p + 1) * share],
                packed.at[b, (3 * ns + p) * depth : (3 * ns + p + 1) * depth, :],
                sems.at[0],
            ).start()
        return carry

    lax.fori_loop(0, nb, store_out, 0)

    def head(h, carry):
        at = h * HEAD_DIM
        col_q = pl.ds(pl.multiple_of(at, HEAD_DIM), HEAD_DIM)
        col_k = pl.ds(pl.multiple_of(share + at, HEAD_DIM), HEAD_DIM)
        col_v = pl.ds(pl.multiple_of(2 * share + at, HEAD_DIM), HEAD_DIM)
        acc_k[...] = jnp.zeros_like(acc_k)
        acc_v[...] = jnp.zeros_like(acc_v)
        for n in range(ns):
            first = max(n - 1, 0) * rows
            mine, seen = slice(n * rows, n * rows + rows), slice(first, first + 2 * rows)
            query, keys, grad = qkv[mine, col_q], qkv[seen, col_k], do[mine, col_q]
            probs = soft_block(query, keys, n, first, limit)
            dp = dot_t(grad, qkv[seen, col_v])
            ds = (probs * (dp - jnp.sum(dp * probs, -1, keepdims=True))).astype(BF)
            dq = jnp.dot(ds, keys, preferred_element_type=F32) * scale
            dproj[mine, col_q] = dq.astype(BF)
            acc_k[seen, :] += t_dot(ds, query)
            acc_v[seen, :] += t_dot(probs.astype(BF), grad)
        dproj[:, col_k] = (acc_k[...] * scale).astype(BF)
        dproj[:, col_v] = acc_v[...].astype(BF)
        return carry

    lax.fori_loop(0, share // HEAD_DIM, head, 0)
    wide = min(512, 3 * share)

    def weights(j, carry):
        cols = pl.ds(pl.multiple_of(j * wide, wide), wide)
        gqv[:, cols] = jnp.sum(dproj[:, cols].astype(F32), 0, keepdims=True)
        for r in range(0, width, 512):
            gw[r : r + 512, cols] = jnp.dot(
                h1t[r : r + 512, :], dproj[:, cols], preferred_element_type=F32
            ).astype(BF)
        return carry

    lax.fori_loop(0, 3 * share // wide, weights, 0)

    def store(k, c):
        s, b = k // nb, lax.rem(k, nb)
        for t in range(3):
            pltpu.make_async_copy(
                gw.at[pl.ds(k * depth, depth), t * share : (t + 1) * share],
                packed.at[b, pl.ds((t * ns + s) * depth, depth), :],
                sems.at[1],
            ).start()
        return c

    lax.fori_loop(0, ns * nb, store, 0)
    pltpu.make_async_copy(gw, gw, sems.at[1]).wait()
    pltpu.make_async_copy(gwo, gwo, sems.at[0]).wait()


def attend_back(ns, nb, lengths, h1t, da, wq, o, qkv):
    width, tokens = h1t.shape
    share = o.shape[1]
    vm = pl.BlockSpec(memory_space=pltpu.VMEM)
    hbm = pl.BlockSpec(memory_space=pl.ANY)
    return pl.pallas_call(
        functools.partial(attend_back_kernel, ns, nb),
        out_shape=(
            jax.ShapeDtypeStruct((nb, 4 * width // nb, share), BF),
            jax.ShapeDtypeStruct((tokens, 3 * share), BF),
            jax.ShapeDtypeStruct((1, 3 * share), F32),
        ),
        in_specs=[pl.BlockSpec(memory_space=pltpu.SMEM), vm, vm, hbm, vm, vm],
        out_specs=(hbm, vm, vm),
        scratch_shapes=[
            pltpu.VMEM((tokens, share), BF),
            pltpu.VMEM((width, 3 * share), BF),
            pltpu.VMEM((share, width), BF),
            pltpu.VMEM((share, width), BF),
            pltpu.VMEM((tokens, HEAD_DIM), F32),
            pltpu.VMEM((tokens, HEAD_DIM), F32),
            pltpu.SemaphoreType.DMA((3,)),
        ],
        compiler_params=pltpu.CompilerParams(vmem_limit_bytes=56 * 2**20),
        cost_estimate=pl.CostEstimate(
            flops=40 * 10**9, bytes_accessed=12 * width * share, transcendentals=tokens * 512 * share // 128
        ),
        name="attend_back",
    )(lengths, h1t, da, wq, o, qkv)


MESH = pl.DeviceIdType.MESH


def send(src, dst, sends, recvs, to):
    one = pltpu.make_async_remote_copy(
        src_ref=src, dst_ref=dst, send_sem=sends, recv_sem=recvs, device_id=to, device_id_type=MESH
    )
    one.start()
    return one


class Line:
    def __init__(self, step, own, prior, got, held, load, sends, recvs):
        self.step, self.own, self.prior, self.got, self.held = step, own, prior, got, held
        self.load, self.sends, self.recvs = load, sends, recvs
        self.last = own.shape[0] - 1
        self.seq, batch = lax.axis_index("seq"), lax.axis_index("batch")
        self.chip, self.core = batch // 2, lax.rem(batch, 2)

    def ready(self):
        self.got[...] = jnp.zeros_like(self.got)
        ahead = self.last - self.step
        wanted = jnp.minimum(self.chip + ahead, self.last), jnp.maximum(self.chip - ahead, 0)
        for way, chunk in enumerate(wanted):
            pltpu.make_async_copy(self.own.at[chunk], self.held.at[way], self.load.at[way]).start()

    def neighbours(self):
        count = self.last + 1
        return [(self.seq, 2 * lax.rem(self.chip + d, count) + self.core) for d in (1, count - 1)]

    def copy(self, way):
        to = jnp.minimum(self.chip + 1, self.last) if way == 0 else jnp.maximum(self.chip - 1, 0)
        return pltpu.make_async_remote_copy(
            src_ref=self.held.at[way],
            dst_ref=self.got.at[way],
            send_sem=self.sends.at[way],
            recv_sem=self.recvs.at[way],
            device_id=(self.seq, 2 * to + self.core),
            device_id_type=MESH,
        )

    def roles(self):
        chip, last, step = self.chip, self.last, self.step
        gives = chip <= step, chip >= last - step
        takes = (chip >= 1) & (chip <= step + 1), (chip <= last - 1) & (chip >= last - 1 - step)
        return gives, takes

    def go(self):
        for way in range(2):
            here = self.held.at[way]
            pltpu.make_async_copy(here, here, self.load.at[way]).wait()
            if self.prior is not None:
                total = self.held[way].astype(F32) + self.prior[way].astype(F32)
                self.held[way] = total.astype(BF)

            @pl.when(self.roles()[0][way])
            def _():
                self.copy(way).start()

    def stop(self):
        gives, takes = self.roles()
        for way in range(2):

            @pl.when(takes[way])
            def _():
                self.copy(way).wait_recv()

            @pl.when(gives[way])
            def _():
                self.copy(way).wait_send()


def line_scratch(rows, width):
    dma = pltpu.SemaphoreType.DMA
    return [pltpu.VMEM((2, rows, width), BF), dma((2,)), dma((2,)), dma((2,))]


def ff_kernel(ns, nb, first, moving, *refs):
    line = None
    if first:
        h2, cot, wg, bias, *gwg, g_out, du_out, gb, h2t, dh2, w1, w2, gw1, gw2, sems = refs
    elif moving:
        h2, h2t, cot, wg, bias, own, *gwg, g_out, du_out, gb, got, w1, w2, gw1, gw2, sems, held, s0, s1, s2 = refs
        line = Line(0, own, None, got, held, s0, s1, s2)
    else:
        h2, h2t, cot, wg, bias, *gwg, g_out, du_out, gb, w1, w2, gw1, gw2, sems = refs
    core = lax.rem(lax.axis_index("batch"), 2)

    def store(src, b, rows, cols, sem):
        if len(gwg) == 1:
            pltpu.make_async_copy(src, gwg[0].at[b, rows, cols], sem).start()
        else:

            @pl.when(lax.rem(b, 2) == core)
            def _():
                pltpu.make_async_copy(src, gwg[0].at[b // 2, rows, cols], sem).start()

            @pl.when(lax.rem(b, 2) != core)
            def _():
                pltpu.make_async_copy(src, gwg[1].at[b // 2, rows, cols], sem).start()

    tokens, width = h2.shape
    chunk = g_out.shape[1]
    depth = width // (ns * nb)
    part = chunk // nb
    pieces = width // chunk
    half = ns * depth
    tile = min(512, chunk)
    tiles = chunk // tile
    step = min(256, tokens)

    def load1(k, carry):
        s, b = k // nb, lax.rem(k, nb)
        pltpu.make_async_copy(
            wg.at[b, pl.ds(s * depth, depth), :], w1.at[pl.ds(k * depth, depth), :], sems.at[0]
        ).start()
        return carry

    def load2(k, carry):
        for p in range(pieces):
            pltpu.make_async_copy(
                wg.at[k, pl.ds(half + p * part, part), :],
                w2.at[pl.ds(k * part, part), p * chunk : (p + 1) * chunk],
                sems.at[1],
            ).start()
        return carry

    lax.fori_loop(0, ns * nb, load1, 0)
    lax.fori_loop(0, nb, load2, 0)
    if moving:
        line.ready()
        barrier = pltpu.get_barrier_semaphore()
        for other in line.neighbours():
            pl.semaphore_signal(barrier, inc=1, device_id=other, device_id_type=MESH)
        pl.semaphore_wait(barrier, 2)
        line.go()
    if first:
        for r in range(0, tokens, step):
            h2t[:, r : r + step] = h2[r : r + step, :].T
    pltpu.make_async_copy(w1, w1, sems.at[0]).wait()
    pltpu.make_async_copy(w2, w2, sems.at[1]).wait()

    def one_tile(j, carry):
        at = pl.multiple_of(j * tile, tile)
        cols = pl.ds(at, tile)
        total = jnp.zeros((1, tile), F32)
        for r in range(0, tokens, step):
            rows = slice(r, r + step)
            u = jnp.dot(h2[rows, :], w1[:, cols], preferred_element_type=F32) + bias[:, cols]
            dg = lax.dot_general(
                cot[rows, :], w2[cols, :], (((1,), (1,)), ((), ())), preferred_element_type=F32
            )
            sq = u * u
            th = jnp.tanh(ROOT * u * (1.0 + 0.044715 * sq))
            cdf = 0.5 * (1.0 + th)
            g_out[rows, cols] = (u * cdf).astype(BF)
            slope = cdf + 0.5 * u * (1.0 - th * th) * (ROOT * (1.0 + 3.0 * 0.044715 * sq))
            du = (dg * slope).astype(BF)
            du_out[rows, cols] = du
            total += jnp.sum(du.astype(F32), 0, keepdims=True)
        gb[:, cols] = total
        for r in range(0, width, 512):
            gw1[j, r : r + 512, :] = jnp.dot(
                h2t[r : r + 512, :], du_out[:, cols], preferred_element_type=F32
            ).astype(BF)
        gt = g_out[:, cols].T
        for r in range(0, width, 512):
            gw2[j, :, r : r + 512] = jnp.dot(
                gt, cot[:, r : r + 512], preferred_element_type=F32
            ).astype(BF)

        def store1(k, c):
            s, b = k // nb, lax.rem(k, nb)
            store(gw1.at[j, pl.ds(k * depth, depth), :], b, pl.ds(s * depth, depth), cols, sems.at[2])
            return c

        lax.fori_loop(0, ns * nb, store1, 0)
        count = tile // part

        def store2(k, c):
            for p in range(pieces):
                src = gw2.at[j, pl.ds(k * part, part), p * chunk : (p + 1) * chunk]
                store(src, j * count + k, pl.ds(half + p * part, part), slice(None), sems.at[3])
            return c

        lax.fori_loop(0, count, store2, 0)
        return carry

    lax.fori_loop(0, tiles, one_tile, 0)
    if first:
        for r in range(0, tokens, step):
            for c in range(0, width, 512):
                part_sum = dot_t(du_out[r : r + step, :], w1[c : c + 512, :])
                dh2[r : r + step, c : c + 512] = part_sum.astype(BF)
    pltpu.make_async_copy(gw1, gw1, sems.at[2]).wait()
    pltpu.make_async_copy(gw2, gw2, sems.at[3]).wait()
    if moving:
        line.stop()


def ff_chunk(ns, nb, h2, h2t, cot, wg, bias, split, own=None):
    tokens, width = h2.shape
    chunk = wg.shape[2]
    tile = min(512, chunk)
    first = h2t is None
    vm = pl.BlockSpec(memory_space=pltpu.VMEM)
    hbm = pl.BlockSpec(memory_space=pl.ANY)
    grads = (jax.ShapeDtypeStruct((nb // 2,) + wg.shape[1:], BF),) * 2 if split else (jax.ShapeDtypeStruct(wg.shape, BF),)
    inner = jax.ShapeDtypeStruct((tokens, chunk), BF)
    extra = (jax.ShapeDtypeStruct((width, tokens), BF), jax.ShapeDtypeStruct((tokens, width), BF)) if first else ()
    given = (h2, cot, wg, bias) if first else (h2, h2t, cot, wg, bias)
    moving = own is not None
    more = []
    if moving:
        given += (own,)
        extra = (jax.ShapeDtypeStruct((2,) + own.shape[1:], BF),)
        more = line_scratch(*own.shape[1:])
    return pl.pallas_call(
        functools.partial(ff_kernel, ns, nb, first, moving),
        out_shape=grads + (inner, inner, jax.ShapeDtypeStruct((1, chunk), F32)) + extra,
        in_specs=[hbm if one is wg or one is own else vm for one in given],
        out_specs=(hbm,) * len(grads) + (vm,) * (3 + len(extra)),
        scratch_shapes=[
            pltpu.VMEM((width, chunk), BF),
            pltpu.VMEM((chunk, width), BF),
            pltpu.VMEM((chunk // tile, width, tile), BF),
            pltpu.VMEM((chunk // tile, tile, width), BF),
            pltpu.SemaphoreType.DMA((4,)),
        ]
        + more,
        compiler_params=pltpu.CompilerParams(
            collective_id=4 if moving else None, has_side_effects=moving, vmem_limit_bytes=60 * 2**20
        ),
        cost_estimate=pl.CostEstimate(
            flops=40 * 10**9,
            bytes_accessed=4 * wg.size,
            transcendentals=tokens * chunk,
        ),
        name="ff_first" if first else "ff_chunk",
    )(*given)


def greet(more=()):
    me, batch = lax.axis_index("seq"), lax.axis_index("batch")
    by_x = me + 1 - 2 * lax.rem(me, 2)
    by_y = lax.rem(me + 2, 4)
    barrier = pltpu.get_barrier_semaphore()
    for other in [(by_x, batch), (by_y, batch), *more]:
        pl.semaphore_signal(barrier, inc=1, device_id=other, device_id_type=MESH)
    pl.semaphore_wait(barrier, 2 + len(more))
    return me, by_x, by_y, (by_x, batch), (by_y, batch)


def scatter_steps(partial, place, buffers, send, recv):
    me, by_x, by_y, to_x, to_y = place
    out, via, from_x, from_y = buffers
    half = via.shape[1]
    top, low = slice(0, half), slice(half, 2 * half)
    far = 3 - me

    def copy(k, src, dst, to):
        one = pltpu.make_async_remote_copy(
            src_ref=src, dst_ref=dst, send_sem=send.at[k], recv_sem=recv.at[k], device_id=to, device_id_type=MESH
        )
        one.start()
        return one

    out[0] = partial(far).astype(BF)
    c0 = copy(0, out.at[0, top], via.at[0], to_y)
    c1 = copy(1, out.at[0, low], via.at[1], to_x)
    yield
    block = partial(by_x)
    out[1, low] = block[low].astype(BF)
    c2 = copy(2, out.at[1, low], from_x.at[low], to_x)
    x_top = block[top]
    yield
    block = partial(by_y)
    out[2, top] = block[top].astype(BF)
    c3 = copy(3, out.at[2, top], from_y.at[top], to_y)
    y_low = block[low]
    yield
    c0.wait_recv()
    out[1, top] = (x_top + via[0].astype(F32)).astype(BF)
    c4 = copy(4, out.at[1, top], from_x.at[top], to_x)
    c1.wait_recv()
    out[2, low] = (y_low + via[1].astype(F32)).astype(BF)
    c5 = copy(5, out.at[2, low], from_y.at[low], to_y)
    yield
    mine = partial(me)
    yield
    c3.wait_recv()
    c4.wait_recv()
    mine_top = mine[top] + from_x[top].astype(F32) + from_y[top].astype(F32)
    c2.wait_recv()
    c5.wait_recv()
    mine_low = mine[low] + from_x[low].astype(F32) + from_y[low].astype(F32)
    for one in (c0, c1, c2, c3, c4, c5):
        one.wait_send()
    yield mine_top, mine_low


def scatter_sum(partial, place, buffers, send, recv):
    return list(scatter_steps(partial, place, buffers, send, recv))[-1]


def scatter_scratch(rows, width):
    return [
        pltpu.VMEM((3, rows, width), BF),
        pltpu.VMEM((2, rows // 2, width), BF),
        pltpu.VMEM((rows, width), BF),
        pltpu.VMEM((rows, width), BF),
        pltpu.SemaphoreType.DMA((6,)),
        pltpu.SemaphoreType.DMA((6,)),
    ]


def gather_blocks(full, rows, place, send, recv):
    me, by_x, by_y, to_x, to_y = place
    half = rows // 2

    def copy(k, block, part, to):
        at = full.at[pl.ds(pl.multiple_of(block * rows + part * half, half), half)]
        one = pltpu.make_async_remote_copy(
            src_ref=at, dst_ref=at, send_sem=send.at[k], recv_sem=recv.at[k], device_id=to, device_id_type=MESH
        )
        one.start()
        return one

    c0 = copy(0, me, 0, to_x)
    c3 = copy(3, me, 1, to_y)
    c2 = copy(2, me, 0, to_y)
    c1 = copy(1, me, 1, to_x)
    c0.wait_recv()
    c4 = copy(4, by_x, 0, to_y)
    c3.wait_recv()
    c5 = copy(5, by_y, 1, to_x)
    for one in (c1, c2, c4, c5):
        one.wait_recv()
    for one in (c0, c1, c2, c3, c4, c5):
        one.wait_send()


GATHER_SEMS = [pltpu.SemaphoreType.DMA((6,)), pltpu.SemaphoreType.DMA((6,))]


def middle_kernel(ns, nb, o, wq, mine, obias, gain, shift, x1, h2, wout, load_sem, out, via, from_x, from_y, s1, r1, s2, r2):
    rows, width = mine.shape
    half = rows // 2
    load_out(ns, nb, wq, wout, load_sem)
    place = greet()
    pltpu.make_async_copy(wout, wout, load_sem).wait()

    def partial(block):
        at = pl.multiple_of(block * rows, rows)
        return jnp.dot(o[pl.ds(at, rows), :], wout[...], preferred_element_type=F32)

    sums = scatter_sum(partial, place, (out, via, from_x, from_y), s1, r1)
    for part, total in enumerate(sums):
        span = slice(part * half, part * half + half)
        res = mine[span, :].astype(F32) + (total + obias[...])
        x1[span, :] = res
        normed, _ = norm_stats(res)
        at = pl.multiple_of(place[0] * rows + part * half, half)
        h2[pl.ds(at, half), :] = (normed * gain[...] + shift[...]).astype(BF)
    gather_blocks(h2, rows, place, s2, r2)


def middle(ns, nb, o, wq, mine, obias, gain, shift):
    tokens, share = o.shape
    rows, width = mine.shape
    vm = pl.BlockSpec(memory_space=pltpu.VMEM)
    return pl.pallas_call(
        functools.partial(middle_kernel, ns, nb),
        out_shape=(jax.ShapeDtypeStruct((rows, width), F32), jax.ShapeDtypeStruct((tokens, width), BF)),
        in_specs=[vm, pl.BlockSpec(memory_space=pl.ANY)] + [vm] * 4,
        out_specs=(vm, vm),
        scratch_shapes=[pltpu.VMEM((share, width), BF), pltpu.SemaphoreType.DMA] + scatter_scratch(rows, width) + GATHER_SEMS,
        compiler_params=pltpu.CompilerParams(collective_id=1, has_side_effects=True, vmem_limit_bytes=56 * 2**20),
        cost_estimate=pl.CostEstimate(flops=40 * 10**9, bytes_accessed=12 * tokens * width, transcendentals=0),
        name="project_out",
    )(o, wq, mine, obias, gain, shift)


def ff_back_kernel(ns, nb, du, wg, before, x1, cot, gain, own, prior, *refs):
    dx1, da, ggain, gshift, gob, got, w, load_sem, out, via, from_x, from_y, s1, r1, s2, r2, *moving = refs
    line = Line(1, own, prior, got, *moving)
    rows, width = x1.shape
    half = rows // 2
    load_rows(ns, nb, width // (ns * nb), wg, w, load_sem)
    line.ready()
    place = greet(line.neighbours())
    pltpu.make_async_copy(w, w, load_sem).wait()

    def partial(block):
        at = pl.multiple_of(block * rows, rows)
        return before[pl.ds(at, rows), :].astype(F32) + dot_t(du[pl.ds(at, rows), :], w[...])

    steps = scatter_steps(partial, place, (out, via, from_x, from_y), s1, r1)
    next(steps)
    line.go()
    *_, sums = steps
    totals = [jnp.zeros((1, width), F32)] * 3
    for part, grad in enumerate(sums):
        span = slice(part * half, part * half + half)
        normed, rstd = norm_stats(x1[span, :])
        res = cot[span, :].astype(F32) + norm_back(grad, normed, rstd, gain[...])
        dx1[span, :] = res
        low = res.astype(BF)
        at = pl.multiple_of(place[0] * rows + part * half, half)
        da[pl.ds(at, half), :] = low
        for k, term in enumerate((grad * normed, grad, low.astype(F32))):
            totals[k] += jnp.sum(term, 0, keepdims=True)
    ggain[...], gshift[...], gob[...] = totals
    gather_blocks(da, rows, place, s2, r2)
    line.stop()


def ff_back(ns, nb, du, wg, before, x1, cot, gain, own, prior):
    rows, width = x1.shape
    tokens, chunk = du.shape
    vm = pl.BlockSpec(memory_space=pltpu.VMEM)
    hbm = pl.BlockSpec(memory_space=pl.ANY)
    row = jax.ShapeDtypeStruct((1, width), F32)
    return pl.pallas_call(
        functools.partial(ff_back_kernel, ns, nb),
        out_shape=(
            jax.ShapeDtypeStruct((rows, width), F32),
            jax.ShapeDtypeStruct((tokens, width), BF),
            row,
            row,
            row,
            jax.ShapeDtypeStruct(prior.shape, BF),
        ),
        in_specs=[vm, hbm] + [vm] * 4 + [hbm, vm],
        out_specs=(vm,) * 6,
        scratch_shapes=[pltpu.VMEM((width, chunk), BF), pltpu.SemaphoreType.DMA]
        + scatter_scratch(rows, width)
        + GATHER_SEMS
        + line_scratch(*prior.shape[1:]),
        compiler_params=pltpu.CompilerParams(collective_id=2, has_side_effects=True, vmem_limit_bytes=56 * 2**20),
        cost_estimate=pl.CostEstimate(flops=40 * 10**9, bytes_accessed=12 * tokens * width, transcendentals=0),
        name="ff_back",
    )(du, wg, before, x1, cot, gain, own, prior)


def finish_kernel(ns, nb, count, *refs):
    dproj, wq = refs[:2]
    gs, wgs = refs[2 : 2 + count], refs[2 + count : 2 + 2 * count]
    own_sum, prior, *later = refs[2 + 2 * count : 3 + 3 * count]
    refs = refs[3 + 3 * count :]
    mine, dx1, gain, x1, bias, gx, ggain, gshift, result, gw1, gw2, w = refs[:12]
    ws, stage = refs[12 : 12 + count], refs[12 + count]
    gw2_low, load_sem, s0, r0, got, *rest = refs[13 + count :]
    first, second, moving = rest[:6], rest[6:12], rest[12:]
    line = Line(2, own_sum, prior, got, *moving)
    total = moving[0].at[0]
    summed = [total, *later]
    rows, width = mine.shape
    half = rows // 2
    chunk = gs[0].shape[1]
    part_rows, pieces, base = chunk // nb, width // chunk, width // nb
    load_attention(ns, nb, wq, w, load_sem.at[count])
    for c in range(count):

        def load(k, carry):
            for p in range(pieces):
                pltpu.make_async_copy(
                    wgs[c].at[k, pl.ds(base + p * part_rows, part_rows), :],
                    ws[c].at[pl.ds(k * part_rows, part_rows), p * chunk : (p + 1) * chunk],
                    load_sem.at[c],
                ).start()
            return carry

        lax.fori_loop(0, nb, load, 0)
    line.ready()
    me, others, met = greet_seq(ns, line.neighbours())
    by_x, by_y, batch = me + 1 - 2 * lax.rem(me, 2), lax.rem(me + 2, 4), lax.axis_index("batch")
    place = me, by_x, by_y, (by_x, batch), (by_y, batch)
    depth, hidden = gw1.shape[0], gw1.shape[1] // ns

    def ship(chunks, b, carry):
        for c in chunks:
            cols = pl.ds(pl.multiple_of(me * hidden + (b * count + c) * part_rows, part_rows), part_rows)
            from_cols = pl.ds(pl.multiple_of(b * part_rows, part_rows), part_rows)
            own = pl.ds(pl.multiple_of(me * depth, depth), depth)
            pltpu.make_async_copy(summed[c].at[own, from_cols], stage.at[:, cols], load_sem.at[count + 1]).start()
            for d, to in enumerate(others):
                theirs = pl.ds(pl.multiple_of(to[0] * depth, depth), depth)
                send(summed[c].at[theirs, from_cols], stage.at[:, cols], s0.at[d], r0.at[d], to)
        return carry

    def bring(chunks):
        lax.fori_loop(0, nb, functools.partial(ship, chunks), 0)
        for c in chunks:
            for p in range(pieces):
                here = pltpu.make_async_copy(
                    summed[c].at[ns * depth + p * part_rows : ns * depth + (p + 1) * part_rows],
                    gw2_low.at[c * part_rows : (c + 1) * part_rows, p * chunk : (p + 1) * chunk],
                    load_sem.at[count + 2],
                )
                here.start()

    met()
    line.go()
    bring(range(1, count))

    def input_grad(block):
        at = pl.multiple_of(block * rows, rows)
        return dot_t(dproj[pl.ds(at, rows), :], w[...])

    def branch(block):
        at = pl.multiple_of(block * rows, rows)
        total = jnp.dot(gs[0][pl.ds(at, rows), :], ws[0][...], preferred_element_type=F32)
        for c in range(1, count):
            total += jnp.dot(gs[c][pl.ds(at, rows), :], ws[c][...], preferred_element_type=F32)
        return total

    pltpu.make_async_copy(w, w, load_sem.at[count]).wait()
    one = scatter_steps(input_grad, place, first[:4], *first[4:])
    two = scatter_steps(branch, place, second[:4], *second[4:])
    for _ in range(3):
        next(one)
    for c in range(count):
        pltpu.make_async_copy(ws[c], ws[c], load_sem.at[c]).wait()
    next(two)
    next(one)
    next(two)
    next(two)
    next(one)
    sums = next(one)
    next(two)
    line.stop()
    own_part = pltpu.make_async_copy(own_sum.at[line.chip], total, load_sem.at[count + 3])
    own_part.start()
    own_part.wait()
    total[...] = (total[...].astype(F32) + got[0].astype(F32) + got[1].astype(F32)).astype(BF)
    bring([0])
    totals = [jnp.zeros((1, width), F32)] * 2
    for part, grad in enumerate(sums):
        span = slice(part * half, part * half + half)
        normed, rstd = norm_stats(mine[span, :].astype(F32))
        gx[span, :] = dx1[span, :] + norm_back(grad, normed, rstd, gain[...])
        for k, term in enumerate((grad * normed, grad)):
            totals[k] += jnp.sum(term, 0, keepdims=True)
    ggain[...], gshift[...] = totals
    pltpu.make_async_copy(gw2_low, gw2_low, load_sem.at[count + 2]).wait()
    gw2[...] = gw2_low[...].astype(F32)
    next(two)
    strip = stage.at[:, :hidden]
    pltpu.make_async_copy(strip, strip, load_sem.at[count + 1]).wait()
    for d, to in enumerate(others):
        pltpu.make_async_remote_copy(
            src_ref=strip, dst_ref=strip, send_sem=s0.at[d], recv_sem=r0.at[d], device_id=to, device_id_type=MESH
        ).wait()
    gw1[...] = stage[...].astype(F32)
    for part, branch_sum in enumerate(next(two)):
        span = slice(part * half, part * half + half)
        result[span, :] = (x1[span, :] + (branch_sum + bias[...])).astype(BF)


def finish(ns, nb, dproj, wq, gs, wgs, own, prior, summed, mine, dx1, gain, x1, bias):
    rows, width = mine.shape
    count, chunk = len(gs), gs[0].shape[1]
    depth, hidden = width // (ns * nb), count * chunk
    vm = pl.BlockSpec(memory_space=pltpu.VMEM)
    hbm = pl.BlockSpec(memory_space=pl.ANY)
    row = jax.ShapeDtypeStruct((1, width), F32)
    return pl.pallas_call(
        functools.partial(finish_kernel, ns, nb, count),
        out_shape=(
            jax.ShapeDtypeStruct((rows, width), F32),
            row,
            row,
            jax.ShapeDtypeStruct((rows, width), BF),
            jax.ShapeDtypeStruct((depth, hidden * ns), F32),
            jax.ShapeDtypeStruct((hidden // nb, width), F32),
        ),
        in_specs=[vm, hbm] + [vm] * count + [hbm] * (count + 1) + [vm] + [hbm] * (count - 1) + [vm] * 5,
        out_specs=(vm,) * 6,
        scratch_shapes=[pltpu.VMEM((width, dproj.shape[1]), BF)]
        + [pltpu.VMEM((chunk, width), BF)] * count
        + [pltpu.VMEM((depth, hidden * ns), BF), pltpu.VMEM((hidden // nb, width), BF)]
        + [pltpu.SemaphoreType.DMA((count + 4,)), pltpu.SemaphoreType.DMA((ns - 1,)), pltpu.SemaphoreType.DMA((ns - 1,))]
        + [pltpu.VMEM(prior.shape, BF)]
        + scatter_scratch(rows, width) * 2
        + line_scratch(*prior.shape[1:]),
        compiler_params=pltpu.CompilerParams(collective_id=3, has_side_effects=True, vmem_limit_bytes=60 * 2**20),
        cost_estimate=pl.CostEstimate(flops=40 * 10**9, bytes_accessed=24 * rows * width, transcendentals=0),
        name="finish",
    )(dproj, wq, *gs, *wgs, own, prior, *summed, mine, dx1, gain, x1, bias)


def greet_all(ns, nb):
    me, batch = lax.axis_index("seq"), lax.axis_index("batch")
    along_seq = [(lax.rem(me + d, ns), batch) for d in range(1, ns)]
    along_batch = [(me, lax.rem(batch + d, nb)) for d in range(1, nb)]
    barrier = pltpu.get_barrier_semaphore()
    for other in along_seq + along_batch:
        pl.semaphore_signal(barrier, inc=1, device_id=other, device_id_type=MESH)
    pl.semaphore_wait(barrier, ns + nb - 2)
    return me, batch, along_seq, along_batch


def greet_seq(ns, more=()):
    me, batch = lax.axis_index("seq"), lax.axis_index("batch")
    others = [(lax.rem(me + d, ns), batch) for d in range(1, ns)]
    barrier = pltpu.get_barrier_semaphore()
    for other in [*others, *more]:
        pl.semaphore_signal(barrier, inc=1, device_id=other, device_id_type=MESH)
    return me, others, lambda: pl.semaphore_wait(barrier, ns - 1 + len(more))


def spread_kernel(ns, w_qkv, w_out, packed, local, s0, r0):
    depth, width = w_out.shape
    share = packed.shape[1]
    me, others, met = greet_seq(ns)
    copies = []
    for p in range(ns):
        rows = slice((3 * ns + p) * depth, (3 * ns + p + 1) * depth)
        copies.append(pltpu.make_async_copy(w_out.at[:, p * share : (p + 1) * share], packed.at[rows], local.at[3 + p]))
    for t in range(3):
        cols = pl.ds(pl.multiple_of(t * width + me * share, share), share)
        rows = pl.ds(pl.multiple_of((t * ns + me) * depth, depth), depth)
        copies.append(pltpu.make_async_copy(w_qkv.at[:, cols], packed.at[rows], local.at[t]))
    for one in copies:
        one.start()
    met()
    for t in range(3):
        rows = pl.ds(pl.multiple_of((t * ns + me) * depth, depth), depth)
        for d, to in enumerate(others):
            cols = pl.ds(pl.multiple_of(t * width + to[0] * share, share), share)
            copies.append(send(w_qkv.at[:, cols], packed.at[rows], s0.at[t, d], r0.at[t, d], to))
    for one in copies:
        one.wait()


def spread(ns, w_qkv, w_out):
    depth, width = w_out.shape
    hbm = pl.BlockSpec(memory_space=pl.ANY)
    dma = pltpu.SemaphoreType.DMA
    return pl.pallas_call(
        functools.partial(spread_kernel, ns),
        out_shape=jax.ShapeDtypeStruct((4 * ns * depth, width // ns), BF),
        in_specs=[hbm, hbm],
        out_specs=hbm,
        scratch_shapes=[dma((3 + ns,)), dma((3, ns - 1)), dma((3, ns - 1))],
        compiler_params=pltpu.CompilerParams(collective_id=5, has_side_effects=True),
        cost_estimate=pl.CostEstimate(flops=5 * 10**9, bytes_accessed=2 * w_qkv.size, transcendentals=0),
        name="spread_qkv",
    )(w_qkv, w_out)


def whole_row(ns, nb, vecs, row, width):
    pieces = jnp.concatenate([vecs[b, s, row : row + 1, :] for b in range(nb) for s in range(ns)], 0)
    lanes = jnp.concatenate([pieces] * (width // pieces.shape[1]), 1)
    owner = lax.broadcasted_iota(jnp.int32, lanes.shape, 0)
    owner = lax.rem(owner, ns) * nb + owner // ns
    place = lax.broadcasted_iota(jnp.int32, lanes.shape, 1) // (width // (ns * nb))
    return jnp.sum(jnp.where(owner == place, lanes, 0.0), 0, keepdims=True)


def collect_kernel(ns, nb, parts, w1, w2, mine, cot, vec, *refs):
    packs = refs[:parts]
    h1, cots, vecs, acts, local, s0, r0, s1, r1, s2, r2, s3, r3, s4, r4 = refs[parts:]
    depth = w1.shape[0]
    rows, width = mine.shape
    half = rows // 2
    hidden = w1.shape[1] // ns
    part = hidden // (parts * nb)
    chunk = hidden // parts
    pieces = width // chunk
    me, batch = lax.axis_index("seq"), lax.axis_index("batch")
    by_x = me + 1 - 2 * lax.rem(me, 2)
    by_y = lax.rem(me + 2, 4)
    others = [(lax.rem(me + d, ns), batch) for d in range(1, ns)]
    column = [(me, lax.rem(batch + d, nb)) for d in range(1, nb)]
    barrier = pltpu.get_barrier_semaphore()
    for other in others + column:
        pl.semaphore_signal(barrier, inc=1, device_id=other, device_id_type=MESH)
    vecs[batch, me] = vec[...]
    at_me = pl.ds(pl.multiple_of(me * rows, rows), rows)
    acts[at_me, :] = mine[...]
    own = pltpu.make_async_copy(cot, cots.at[at_me], local.at[parts])
    own.start()
    for c in range(parts):
        for p in range(pieces):
            pltpu.make_async_copy(
                w2.at[c * part : (c + 1) * part, p * chunk : (p + 1) * chunk],
                packs[c].at[ns * depth + p * part : ns * depth + (p + 1) * part, :],
                local.at[c],
            ).start()
    at = pl.ds(pl.multiple_of(me * depth, depth), depth)

    def keep(b, carry):
        for c in range(parts):
            cols = pl.ds(pl.multiple_of(me * hidden + (b * parts + c) * part, part), part)
            here = packs[c].at[at, pl.ds(pl.multiple_of(b * part, part), part)]
            pltpu.make_async_copy(w1.at[:, cols], here, local.at[c]).start()
        return carry

    lax.fori_loop(0, nb, keep, 0)
    pl.semaphore_wait(barrier, ns + nb - 2)
    to_x, to_y = (by_x, batch), (by_y, batch)
    small = vecs.at[batch, me]
    near = [send(small, small, s3.at[d], r3.at[d], to) for d, to in enumerate(others)]

    def ship(b, carry):
        for c in range(parts):
            here = packs[c].at[at, pl.ds(pl.multiple_of(b * part, part), part)]
            for d, to in enumerate(others):
                cols = pl.ds(pl.multiple_of(to[0] * hidden + (b * parts + c) * part, part), part)
                send(w1.at[:, cols], here, s0.at[c, d], r0.at[c, d], to)
        return carry

    def normalise(block):
        span = pl.ds(pl.multiple_of(block * rows, rows), rows)
        normed, _ = norm_stats(acts[span, :].astype(F32))
        h1[span, :] = (normed * gain + shift).astype(BF)

    def copy(k, full, block, side, to, sends, recvs):
        span = full.at[pl.ds(pl.multiple_of(block * rows + side * half, half), half)]
        return send(span, span, sends.at[k], recvs.at[k], to)

    c0 = copy(0, acts, me, 0, to_x, s1, r1)
    c3 = copy(3, acts, me, 1, to_y, s1, r1)
    c2 = copy(2, acts, me, 0, to_y, s1, r1)
    c1 = copy(1, acts, me, 1, to_x, s1, r1)
    for one in near:
        one.wait_recv()
    row = vecs.at[batch]
    wide = [send(row, row, s4.at[d], r4.at[d], to) for d, to in enumerate(column)]
    lax.fori_loop(0, nb, ship, 0)
    for one in wide:
        one.wait_recv()
    gain, shift = whole_row(ns, nb, vecs, 0, width), whole_row(ns, nb, vecs, 1, width)
    normalise(me)
    c0.wait_recv()
    c4 = copy(4, acts, by_x, 0, to_y, s1, r1)
    c3.wait_recv()
    c5 = copy(5, acts, by_y, 1, to_x, s1, r1)
    own.wait()
    d0 = copy(0, cots, me, 0, to_x, s2, r2)
    d3 = copy(3, cots, me, 1, to_y, s2, r2)
    d2 = copy(2, cots, me, 0, to_y, s2, r2)
    d1 = copy(1, cots, me, 1, to_x, s2, r2)
    c1.wait_recv()
    normalise(by_x)
    c2.wait_recv()
    normalise(by_y)
    c4.wait_recv()
    c5.wait_recv()
    normalise(3 - me)
    d0.wait_recv()
    d4 = copy(4, cots, by_x, 0, to_y, s2, r2)
    d3.wait_recv()
    d5 = copy(5, cots, by_y, 1, to_x, s2, r2)
    for one in (d1, d2, d4, d5):
        one.wait_recv()
    for one in (c0, c1, c2, c3, c4, c5, d0, d1, d2, d3, d4, d5, *near, *wide):
        one.wait_send()
    for c in range(parts):
        pack = packs[c].at[: depth]
        for d, to in enumerate(others):
            rest = pltpu.make_async_remote_copy(
                src_ref=pack, dst_ref=pack, send_sem=s0.at[c, d], recv_sem=r0.at[c, d], device_id=to, device_id_type=MESH
            )
            rest.wait()
        whole = packs[c].at[: depth + pieces * part]
        pltpu.make_async_copy(whole, whole, local.at[c]).wait()


def collect(ns, nb, parts, w1, w2, mine, cot, vec):
    depth = w1.shape[0]
    rows, width = mine.shape
    chunk = w1.shape[1] // (ns * parts)
    vm = pl.BlockSpec(memory_space=pltpu.VMEM)
    hbm = pl.BlockSpec(memory_space=pl.ANY)
    dma = pltpu.SemaphoreType.DMA
    pack = jax.ShapeDtypeStruct((2 * ns * depth, chunk), BF)
    full = jax.ShapeDtypeStruct((ns * rows, width), BF)
    return pl.pallas_call(
        functools.partial(collect_kernel, ns, nb, parts),
        out_shape=(pack,) * parts + (full, full, jax.ShapeDtypeStruct((nb, ns) + vec.shape, F32)),
        in_specs=[hbm, hbm, vm, hbm, vm],
        out_specs=(hbm,) * parts + (vm, hbm, vm),
        scratch_shapes=[
            pltpu.VMEM((ns * rows, width), BF),
            dma((parts + 1,)),
            dma((parts, ns - 1)),
            dma((parts, ns - 1)),
            dma((6,)),
            dma((6,)),
            dma((6,)),
            dma((6,)),
            dma((ns - 1,)),
            dma((ns - 1,)),
            dma((nb - 1,)),
            dma((nb - 1,)),
        ],
        compiler_params=pltpu.CompilerParams(collective_id=6, has_side_effects=True, vmem_limit_bytes=40 * 2**20),
        cost_estimate=pl.CostEstimate(flops=40 * 10**9, bytes_accessed=12 * rows * width, transcendentals=0),
        name="collect",
    )(w1, w2, mine, cot, vec)


def home_kernel(ns, nb, summed, sums, gqkv, gout, small, stage, near, mid, far, local, s0, r0, s1, r1, s2, r2):
    depth, width = gout.shape
    share = width // ns
    me, batch, others, column = greet_all(ns, nb)
    first = [send(sums.at[to[1]], near.at[d], s1.at[d], r1.at[d], to) for d, to in enumerate(column)]
    copies = []
    for t in range(3):
        cols = pl.ds(pl.multiple_of(t * width + me * share, share), share)
        for d, to in enumerate(others):
            rows = pl.ds(pl.multiple_of((t * ns + to[0]) * depth, depth), depth)
            copies.append(send(summed.at[rows], stage.at[:, cols], s0.at[t, d], r0.at[t, d], to))
        rows = pl.ds(pl.multiple_of((t * ns + me) * depth, depth), depth)
        own = pltpu.make_async_copy(summed.at[rows], stage.at[:, cols], local.at[t])
        own.start()
        copies.append(own)
    for p in range(ns):
        rows = slice((3 * ns + p) * depth, (3 * ns + p + 1) * depth)
        gout[:, p * share : (p + 1) * share] = summed[rows, :].astype(F32)
    total = sums[batch]
    for d, one in enumerate(first):
        one.wait_recv()
        total += near[d]
    mid[...] = total
    second = [send(mid.at[to[0]], far.at[d], s2.at[d], r2.at[d], to) for d, to in enumerate(others)]
    for one in copies:
        one.wait()
    gqkv[...] = stage[...].astype(F32)
    total = mid[me]
    for d, one in enumerate(second):
        one.wait_recv()
        total += far[d]
    small[...] = total
    for one in first + second:
        one.wait_send()


def home(ns, nb, summed, sums):
    rows, share = summed.shape
    depth, width = rows // (4 * ns), ns * share
    tail = sums.shape[2:]
    vm = pl.BlockSpec(memory_space=pltpu.VMEM)
    dma = pltpu.SemaphoreType.DMA
    return pl.pallas_call(
        functools.partial(home_kernel, ns, nb),
        out_shape=(
            jax.ShapeDtypeStruct((depth, 3 * width), F32),
            jax.ShapeDtypeStruct((depth, width), F32),
            jax.ShapeDtypeStruct(tail, F32),
        ),
        in_specs=[vm, vm],
        out_specs=(vm, vm, vm),
        scratch_shapes=[
            pltpu.VMEM((depth, 3 * width), BF),
            pltpu.VMEM((nb - 1, ns) + tail, F32),
            pltpu.VMEM((ns,) + tail, F32),
            pltpu.VMEM((ns - 1,) + tail, F32),
            dma((3,)),
            dma((3, ns - 1)),
            dma((3, ns - 1)),
            dma((nb - 1,)),
            dma((nb - 1,)),
            dma((ns - 1,)),
            dma((ns - 1,)),
        ],
        compiler_params=pltpu.CompilerParams(collective_id=8, has_side_effects=True),
        cost_estimate=pl.CostEstimate(flops=5 * 10**9, bytes_accessed=4 * summed.size, transcendentals=0),
        name="home",
    )(summed, sums)


PARTS = 2


def gather_seq(value):
    return lax.all_gather(value, "seq", axis=0, tiled=True)


def scatter_seq(partial):
    return lax.psum_scatter(partial, "seq", scatter_dimension=0, tiled=True)


def scatter_batch(parts):
    flat = parts.reshape(-1, parts.shape[-1])
    return lax.psum_scatter(flat, "batch", scatter_dimension=0, tiled=True)


def own_sums(keep, give):
    count = lax.axis_size("batch")
    got = lax.ppermute(give, "batch", [(i, i ^ 1) for i in range(count)])
    return (keep.astype(F32) + got.astype(F32)).astype(BF)


def unpermute(ns, nb, gathered):
    depth = gathered.shape[1] // ns
    return gathered.reshape(nb, ns, depth, -1).transpose(1, 0, 2, 3).reshape(ns * nb * depth, -1)


def unpack_attention(ns, nb, packed):
    share = packed.shape[2]
    parts = packed.reshape(nb, 4, ns, -1, share)
    qkv = parts[:, :3].transpose(2, 0, 3, 1, 4).reshape(ns * share, 3 * share)
    return qkv, parts[:, 3].transpose(0, 2, 1, 3).reshape(share, ns * share)


def body(
    block_input,
    lengths,
    ln1_gain,
    ln1_bias,
    w_qkv,
    qv_bias,
    w_out,
    out_bias,
    ln2_gain,
    ln2_bias,
    w_fc1,
    fc1_bias,
    w_fc2,
    fc2_bias,
    out_cotangent,
):
    ns, nb = lax.axis_size("seq"), lax.axis_size("batch")
    seq = lax.axis_index("seq")
    rows, width = block_input.shape[1:]
    share = width // ns
    depth = width // (ns * nb)
    hidden = w_fc1.shape[1] // ns
    chunk = hidden // PARTS
    part = chunk // nb
    pieces = width // chunk
    planar = ns == 4 and nb == 8
    mine, cot_mine = block_input[0], out_cotangent[0]

    vectors = (ln1_gain, ln1_bias, qv_bias, out_bias, ln2_gain, ln2_bias, fc1_bias, fc2_bias)
    if planar:
        attn = spread(ns, w_qkv, w_out)
        attn, vectors = lax.optimization_barrier((attn, vectors))
        spare = jnp.zeros((1024 - 2 * depth - sum(vec.shape[0] for vec in vectors),), BF)
        block = jnp.concatenate([vectors[0], vectors[0], vectors[1], vectors[1], *vectors[2:], spare])
        block = block.astype(F32).reshape(8, 128)
        *packs, h1, cot, packed = collect(ns, nb, PARTS, w_fc1, w_fc2, mine, cot_mine, block)
        packed = packed.transpose(1, 0, 2, 3).reshape(ns * nb, 1024)
        packed = jnp.concatenate([packed[:, :depth], packed[:, 2 * depth : 3 * depth], packed[:, 4 * depth :]], 1)
    else:
        attn = lax.all_to_all(w_qkv.reshape(depth, 3, ns, share), "seq", 2, 0).transpose(2, 0, 1, 3)
        attn = jnp.concatenate([attn, w_out.reshape(depth, ns, share).transpose(1, 0, 2)[None]], 0)
        attn = attn.reshape(4 * ns * depth, share)
        vector = jnp.concatenate(vectors).astype(F32)
        packed = lax.all_gather(vector, ("seq", "batch"), axis=0, tiled=False)
    attn = lax.all_gather(attn, "batch", axis=0, tiled=True).reshape(nb, 4 * ns * depth, share)
    full, at = [], 0
    for vec in vectors:
        full.append(packed[:, at : at + vec.shape[0]].reshape(1, -1))
        at += vec.shape[0]
    gain1, shift1, qv, obias, gain2, shift2, bias1, bias2 = full
    bias1 = lax.dynamic_slice_in_dim(bias1, seq * hidden, hidden, 1).reshape(nb, PARTS, part)
    qbias = lax.dynamic_slice_in_dim(qv, seq * share, share, 1)
    vbias = lax.dynamic_slice_in_dim(qv, width + seq * share, share, 1)
    bias3 = jnp.concatenate([qbias, jnp.zeros_like(qbias), vbias], 1)

    if not planar:
        fc1_part = lax.all_to_all(w_fc1.reshape(depth, ns, hidden), "seq", 1, 0)
        fc1_part = fc1_part.reshape(ns * depth, nb, PARTS, part)
        fc2_part = w_fc2.reshape(PARTS, part, pieces, chunk)
        packs = []
        for c in range(PARTS):
            first = fc1_part[:, :, c].reshape(ns * depth, chunk)
            second = fc2_part[c].transpose(1, 0, 2).reshape(pieces * part, chunk)
            packs.append(jnp.concatenate([first, second], 0))
        h1 = (norm_stats(gather_seq(mine).astype(F32))[0] * gain1 + shift1).astype(BF)
        cot = gather_seq(cot_mine)
    wgs = [lax.all_gather(pack, "batch", axis=0, tiled=True).reshape(nb, -1, chunk) for pack in packs]

    qkv, o, h1t = attend(ns, nb, lengths, h1, attn, bias3)
    if planar:
        x1, h2 = middle(ns, nb, o, attn, mine, obias, gain2, shift2)
    else:
        wq, wout = unpack_attention(ns, nb, attn)
        a = scatter_seq(jnp.dot(o, wout, preferred_element_type=F32))
        x1 = mine.astype(F32) + (a + obias)
        h2 = gather_seq((norm_stats(x1)[0] * gain2 + shift2).astype(BF))

    *gw, g, du, gb, h2t, before = ff_chunk(ns, nb, h2, None, cot, wgs[0], bias1[:, 0].reshape(1, chunk), planar)
    gws, gs, dus, gb1 = [gw], [g], [du], [gb.reshape(nb, 1, part)]
    if planar:
        own = own_sums(*gw)
    else:
        gws = [scatter_batch(gw[0])]
    for c in range(1, PARTS):
        gw, g, du, gb, *got = ff_chunk(
            ns, nb, h2, h2t, cot, wgs[c], bias1[:, c].reshape(1, chunk), False, own if planar else None
        )
        gws.append(scatter_batch(gw))
        gs.append(g)
        dus.append(du)
        gb1.append(gb.reshape(nb, 1, part))
    cot_f = cot_mine.astype(F32)
    if planar:
        dx1, da, ggain2, gshift2, gob, got = ff_back(
            ns, nb, dus[1], wgs[1], before, x1, cot_mine, gain2, own, got[0]
        )
    else:
        dh2 = before.astype(F32) + dot_t(dus[1], unpermute(ns, nb, wgs[1][:, : ns * depth]))
        dh2 = scatter_seq(dh2)
        normed2, rstd2 = norm_stats(x1)
        ggain2 = jnp.sum(dh2 * normed2, 0)
        gshift2 = jnp.sum(dh2, 0)
        dx1 = cot_f + norm_back(dh2, normed2, rstd2, gain2)
        da_mine = dx1.astype(BF)
        gob = jnp.sum(da_mine.astype(F32), 0)
        da = gather_seq(da_mine)

    gattn, dproj, gqv = attend_back(ns, nb, lengths, h1t, da, attn, o, qkv)
    gattn = scatter_batch(gattn)
    if planar:
        gx, ggain1, gshift1, out, gw1, gw2 = finish(
            ns, nb, dproj, attn, gs, wgs, own, got, gws[1:], mine, dx1, gain1, x1, bias2
        )
    else:
        dh1 = scatter_seq(dot_t(dproj, wq))
        normed1, rstd1 = norm_stats(mine.astype(F32))
        ggain1 = jnp.sum(dh1 * normed1, 0)
        gshift1 = jnp.sum(dh1, 0)
        gx = dx1 + norm_back(dh1, normed1, rstd1, gain1)
        y = 0.0
        for g, wg in zip(gs, wgs):
            w2 = wg[:, ns * depth :].reshape(nb, pieces, part, chunk).transpose(0, 2, 1, 3).reshape(chunk, width)
            y += jnp.dot(g, w2, preferred_element_type=F32)
        out = (x1 + (scatter_seq(y) + bias2)).astype(BF)

    if not planar:
        gw1 = jnp.stack([gw[: ns * depth].reshape(ns, depth, nb, part) for gw in gws], 3)
        gw1 = lax.all_to_all(gw1, "seq", 0, 1).astype(F32).reshape(depth, ns * hidden)
        gw2 = jnp.stack([gw[ns * depth :].reshape(pieces, part, chunk) for gw in gws], 0)
        gw2 = gw2.astype(F32).transpose(0, 2, 1, 3).reshape(PARTS * part, width)
        gwqkv = gattn[: 3 * ns * depth].reshape(3, ns, depth, share)
        gwqkv = lax.all_to_all(gwqkv, "seq", 1, 2).astype(F32).transpose(1, 0, 2, 3).reshape(depth, 3 * width)
        gwo = gattn[3 * ns * depth :].reshape(ns, depth, share).astype(F32).transpose(1, 0, 2).reshape(depth, width)

    def place(part, size):
        return lax.dynamic_update_slice_in_dim(jnp.zeros((size,), F32), part, seq * part.shape[0], 0)

    gqv = gqv[0]
    gqv = jnp.concatenate([place(gqv[:share], width), place(gqv[2 * share :], width)])
    gb1 = place(jnp.stack(gb1, 1).reshape(-1), ns * hidden)
    gb2 = jnp.sum(cot_f, 0)
    sums = (ggain1, gshift1, gqv, gob, ggain2, gshift2, gb1, gb2)
    sums = jnp.concatenate([t.reshape(ns * nb, -1) for t in sums], 1)
    if planar:
        sums = jnp.pad(sums, ((0, 0), (0, 1024 - sums.shape[1]))).reshape(ns, nb, 8, 128)
        gwqkv, gwo, sums = home(ns, nb, gattn, sums.transpose(1, 0, 2, 3))
        sums = sums.reshape(-1)
    else:
        sums = lax.psum_scatter(sums, ("seq", "batch"), scatter_dimension=0, tiled=True)[0]
    small, at = [], 0
    for vec in vectors:
        small.append(sums[at : at + vec.shape[0]])
        at += vec.shape[0]
    return (
        out[None],
        gx[None],
        small[0],
        small[1],
        gwqkv,
        small[2],
        gwo,
        small[3],
        small[4],
        small[5],
        gw1,
        small[6],
        gw2,
        small[7],
    )


def solution(mesh):
    shard = P(("seq", "batch"))
    shard2 = P(("seq", "batch"), None)
    acts = P("batch", "seq", None)
    return jax.shard_map(
        body,
        mesh=mesh,
        in_specs=(acts, P("batch"), shard, shard, shard2, shard, shard2, shard, shard, shard, shard2, shard, shard2, shard, acts),
        out_specs=(acts, acts, shard, shard, shard2, shard, shard2, shard, shard, shard, shard2, shard, shard2, shard),
        check_vma=False,
    )
```

```python
import functools
import math

import jax
import jax.numpy as jnp
from jax import lax
from jax.experimental import pallas as pl
from jax.experimental.pallas import tpu as pltpu
from jax.sharding import PartitionSpec as P

HEAD_DIM = 128
WINDOW = 256
EPS = 1e-05
BF = jnp.bfloat16
F32 = jnp.float32
ROOT = math.sqrt(2.0 / math.pi)


def norm_stats(values):
    mean = jnp.mean(values, -1, keepdims=True)
    centred = values - mean
    rstd = lax.rsqrt(jnp.mean(centred * centred, -1, keepdims=True) + EPS)
    return centred * rstd, rstd


def norm_back(grad, normed, rstd, gain):
    dn = grad * gain
    return rstd * (
        dn - jnp.mean(dn, -1, keepdims=True) - normed * jnp.mean(dn * normed, -1, keepdims=True)
    )


MESH = pl.DeviceIdType.MESH


def send(src, dst, sends, recvs, to):
    one = pltpu.make_async_remote_copy(
        src_ref=src, dst_ref=dst, send_sem=sends, recv_sem=recvs, device_id=to, device_id_type=MESH
    )
    one.start()
    return one


class Line:
    def __init__(self, step, own, prior, got, held, load, sends, recvs):
        self.step, self.own, self.prior, self.got, self.held = step, own, prior, got, held
        self.load, self.sends, self.recvs = load, sends, recvs
        self.last = own.shape[0] - 1
        self.seq, batch = lax.axis_index("seq"), lax.axis_index("batch")
        self.chip, self.core = batch // 2, lax.rem(batch, 2)

    def ready(self):
        self.got[...] = jnp.zeros_like(self.got)
        ahead = self.last - self.step
        wanted = jnp.minimum(self.chip + ahead, self.last), jnp.maximum(self.chip - ahead, 0)
        for way, chunk in enumerate(wanted):
            pltpu.make_async_copy(self.own.at[chunk], self.held.at[way], self.load.at[way]).start()

    def neighbours(self):
        count = self.last + 1
        return [(self.seq, 2 * lax.rem(self.chip + d, count) + self.core) for d in (1, count - 1)]

    def copy(self, way):
        to = jnp.minimum(self.chip + 1, self.last) if way == 0 else jnp.maximum(self.chip - 1, 0)
        return pltpu.make_async_remote_copy(
            src_ref=self.held.at[way],
            dst_ref=self.got.at[way],
            send_sem=self.sends.at[way],
            recv_sem=self.recvs.at[way],
            device_id=(self.seq, 2 * to + self.core),
            device_id_type=MESH,
        )

    def roles(self):
        chip, last, step = self.chip, self.last, self.step
        gives = chip <= step, chip >= last - step
        takes = (chip >= 1) & (chip <= step + 1), (chip <= last - 1) & (chip >= last - 1 - step)
        return gives, takes

    def go(self):
        for way in range(2):
            here = self.held.at[way]
            pltpu.make_async_copy(here, here, self.load.at[way]).wait()
            if self.prior is not None:
                total = self.held[way].astype(F32) + self.prior[way].astype(F32)
                self.held[way] = total.astype(BF)

            @pl.when(self.roles()[0][way])
            def _():
                self.copy(way).start()

    def stop(self):
        gives, takes = self.roles()
        for way in range(2):

            @pl.when(takes[way])
            def _():
                self.copy(way).wait_recv()

            @pl.when(gives[way])
            def _():
                self.copy(way).wait_send()


def line_scratch(rows, width):
    dma = pltpu.SemaphoreType.DMA
    return [pltpu.VMEM((2, rows, width), BF), dma((2,)), dma((2,)), dma((2,))]


def dot_t(left, right):
    return lax.dot_general(left, right, (((1,), (1,)), ((), ())), preferred_element_type=F32)


def t_dot(left, right):
    return lax.dot_general(left, right, (((0,), (0,)), ((), ())), preferred_element_type=F32)


def load_rows(ns, nb, depth, src, dst, sem):
    def one(k, carry):
        s, b = k // nb, lax.rem(k, nb)
        pltpu.make_async_copy(
            src.at[b, pl.ds(s * depth, depth), :], dst.at[pl.ds(k * depth, depth), :], sem
        ).start()
        return carry

    lax.fori_loop(0, ns * nb, one, 0)


def load_attention(ns, nb, packed, w, sem):
    share = packed.shape[2]
    depth = packed.shape[1] // (3 * ns)

    def one(k, carry):
        s, b = k // nb, lax.rem(k, nb)
        for t in range(3):
            pltpu.make_async_copy(
                packed.at[b, pl.ds((t * ns + s) * depth, depth), :],
                w.at[pl.ds(k * depth, depth), t * share : (t + 1) * share],
                sem,
            ).start()
        return carry

    lax.fori_loop(0, ns * nb, one, 0)


def load_second(nb, packed, w, sem):
    chunk, width = w.shape
    part, pieces, base = chunk // nb, width // chunk, width // nb

    def one(k, carry):
        for p in range(pieces):
            pltpu.make_async_copy(
                packed.at[k, pl.ds(base + p * part, part), :],
                w.at[pl.ds(k * part, part), p * chunk : (p + 1) * chunk],
                sem,
            ).start()
        return carry

    lax.fori_loop(0, nb, one, 0)


def soft_block(query, keys, block, first, length):
    rows, count = query.shape[0], keys.shape[0]
    scores = dot_t(query, keys) * HEAD_DIM ** (-0.5)
    query_pos = block * rows + lax.broadcasted_iota(jnp.int32, (rows, count), 0)
    key_pos = first + lax.broadcasted_iota(jnp.int32, (rows, count), 1)
    back = query_pos - key_pos
    valid = (back >= 0) & (back < WINDOW) & ((key_pos < length) | (back == 0))
    scores = jnp.where(valid, scores, -1e30)
    expo = jnp.exp(scores - jnp.max(scores, -1, keepdims=True))
    return expo / jnp.sum(expo, -1, keepdims=True)


def attend_kernel(ns, nb, length, h1, wq, bias, qkv, o, h1t, w, sem):
    tokens, width = h1.shape
    share = o.shape[1]
    rows = tokens // ns
    load_attention(ns, nb, wq, w, sem)
    for r in range(0, tokens, 256):
        h1t[:, r : r + 256] = h1[r : r + 256, :].T
    pltpu.make_async_copy(w, w, sem).wait()
    wide = min(512, 3 * share)

    def project(j, carry):
        cols = pl.ds(pl.multiple_of(j * wide, wide), wide)
        for r in range(0, tokens, 256):
            part = jnp.dot(h1[r : r + 256, :], w[:, cols], preferred_element_type=F32)
            qkv[r : r + 256, cols] = (part + bias[:, cols]).astype(BF)
        return carry

    lax.fori_loop(0, 3 * share // wide, project, 0)
    limit = length[0]

    def head(h, carry):
        at = h * HEAD_DIM
        col_q = pl.ds(pl.multiple_of(at, HEAD_DIM), HEAD_DIM)
        col_k = pl.ds(pl.multiple_of(share + at, HEAD_DIM), HEAD_DIM)
        col_v = pl.ds(pl.multiple_of(2 * share + at, HEAD_DIM), HEAD_DIM)
        for n in range(ns):
            first = max(n - 1, 0) * rows
            mine, seen = slice(n * rows, n * rows + rows), slice(first, first + 2 * rows)
            probs = soft_block(qkv[mine, col_q], qkv[seen, col_k], n, first, limit)
            part = jnp.dot(probs.astype(BF), qkv[seen, col_v], preferred_element_type=F32)
            o[mine, col_q] = part.astype(BF)
        return carry

    lax.fori_loop(0, share // HEAD_DIM, head, 0)


def attend(ns, nb, lengths, h1, wq, bias):
    tokens, width = h1.shape
    share = wq.shape[2]
    vm = pl.BlockSpec(memory_space=pltpu.VMEM)
    return pl.pallas_call(
        functools.partial(attend_kernel, ns, nb),
        out_shape=(
            jax.ShapeDtypeStruct((tokens, 3 * share), BF),
            jax.ShapeDtypeStruct((tokens, share), BF),
            jax.ShapeDtypeStruct((width, tokens), BF),
        ),
        in_specs=[pl.BlockSpec(memory_space=pltpu.SMEM), vm, pl.BlockSpec(memory_space=pl.ANY), vm],
        out_specs=(vm, vm, vm),
        scratch_shapes=[pltpu.VMEM((width, 3 * share), BF), pltpu.SemaphoreType.DMA],
        compiler_params=pltpu.CompilerParams(vmem_limit_bytes=56 * 2**20),
        cost_estimate=pl.CostEstimate(flops=10**6, bytes_accessed=10**4, transcendentals=0),
        name="attend",
    )(lengths, h1, wq, bias)


def attend_back_kernel(ns, nb, moving, length, h1t, da, wout, o, qkv, *refs):
    line = None
    if moving:
        own, prior, g0, g1, wg0, wg1, packed, dproj, gqv, sums, branch_sum, do, gw, gwo, acc_k, acc_v, sems, *rest = refs
        out, via, from_x, from_y, s1, r1, got, *rest = rest
        line = Line(2, own, prior, got, *rest)
    else:
        packed, dproj, gqv, do, gw, gwo, acc_k, acc_v, sems = refs
    width, tokens = h1t.shape
    share = o.shape[1]
    rows = tokens // ns
    depth = width // (ns * nb)
    scale = HEAD_DIM ** (-0.5)
    limit = length[0]
    steps = None
    if moving:
        chunk = g0.shape[1]
        halves = gw.at[:chunk], gw.at[chunk:]
        for k, wg in enumerate((wg0, wg1)):
            load_second(nb, wg, halves[k], sems.at[2 + k])
        line.ready()
        place = greet(line.neighbours())
        line.go()

        def branch(block):
            at = pl.ds(pl.multiple_of(block * rows, rows), rows // 2)
            total = jnp.dot(g0[at, :], halves[0][...], preferred_element_type=F32)
            return total + jnp.dot(g1[at, :], halves[1][...], preferred_element_type=F32)

        for k in range(2):
            pltpu.make_async_copy(halves[k], halves[k], sems.at[2 + k]).wait()
        steps = scatter_steps(branch, place, (out, via, from_x, from_y), s1, r1)
        for _ in range(3):
            next(steps)
    for r in range(0, tokens, 256):
        do[r : r + 256, :] = dot_t(da[r : r + 256, :], wout[...]).astype(BF)
    ot = o[...].T
    for c in range(0, width, 512):
        gwo[:, c : c + 512] = jnp.dot(ot, da[:, c : c + 512], preferred_element_type=F32).astype(BF)

    def store_out(b, carry):
        for p in range(ns):
            pltpu.make_async_copy(
                gwo.at[pl.ds(b * depth, depth), p * share : (p + 1) * share],
                packed.at[b, (3 * ns + p) * depth : (3 * ns + p + 1) * depth, :],
                sems.at[0],
            ).start()
        return carry

    lax.fori_loop(0, nb, store_out, 0)
    if moving:
        next(steps)

    def head(h, carry):
        at = h * HEAD_DIM
        col_q = pl.ds(pl.multiple_of(at, HEAD_DIM), HEAD_DIM)
        col_k = pl.ds(pl.multiple_of(share + at, HEAD_DIM), HEAD_DIM)
        col_v = pl.ds(pl.multiple_of(2 * share + at, HEAD_DIM), HEAD_DIM)
        acc_k[...] = jnp.zeros_like(acc_k)
        acc_v[...] = jnp.zeros_like(acc_v)
        for n in range(ns):
            first = max(n - 1, 0) * rows
            mine, seen = slice(n * rows, n * rows + rows), slice(first, first + 2 * rows)
            query, keys, grad = qkv[mine, col_q], qkv[seen, col_k], do[mine, col_q]
            probs = soft_block(query, keys, n, first, limit)
            dp = dot_t(grad, qkv[seen, col_v])
            ds = (probs * (dp - jnp.sum(dp * probs, -1, keepdims=True))).astype(BF)
            dq = jnp.dot(ds, keys, preferred_element_type=F32) * scale
            dproj[mine, col_q] = dq.astype(BF)
            acc_k[seen, :] += t_dot(ds, query)
            acc_v[seen, :] += t_dot(probs.astype(BF), grad)
        dproj[:, col_k] = (acc_k[...] * scale).astype(BF)
        dproj[:, col_v] = acc_v[...].astype(BF)
        return carry

    lax.fori_loop(0, share // HEAD_DIM, head, 0)
    if moving:
        next(steps)
        fourth = rows // 4
        for part, total in enumerate(next(steps)):
            branch_sum[part * fourth : (part + 1) * fourth, :] = total
    wide = min(512, 3 * share)

    def weights(j, carry):
        cols = pl.ds(pl.multiple_of(j * wide, wide), wide)
        gqv[:, cols] = jnp.sum(dproj[:, cols].astype(F32), 0, keepdims=True)
        for r in range(0, width, 512):
            gw[r : r + 512, cols] = jnp.dot(
                h1t[r : r + 512, :], dproj[:, cols], preferred_element_type=F32
            ).astype(BF)
        return carry

    lax.fori_loop(0, 3 * share // wide, weights, 0)

    def store(k, c):
        s, b = k // nb, lax.rem(k, nb)
        for t in range(3):
            pltpu.make_async_copy(
                gw.at[pl.ds(k * depth, depth), t * share : (t + 1) * share],
                packed.at[b, pl.ds((t * ns + s) * depth, depth), :],
                sems.at[1],
            ).start()
        return c

    lax.fori_loop(0, ns * nb, store, 0)
    if moving:
        line.stop()
        mine = pltpu.make_async_copy(own.at[line.chip], line.held.at[0], sems.at[2])
        mine.start()
        mine.wait()
        sums[...] = (line.held[0].astype(F32) + got[0].astype(F32) + got[1].astype(F32)).astype(BF)
    stored = gw.at[:, : 3 * share]
    pltpu.make_async_copy(stored, stored, sems.at[1]).wait()
    pltpu.make_async_copy(gwo, gwo, sems.at[0]).wait()


def attend_back(ns, nb, lengths, h1t, da, wout, o, qkv, *more):
    width, tokens = h1t.shape
    share = o.shape[1]
    rows = tokens // ns
    vm = pl.BlockSpec(memory_space=pltpu.VMEM)
    hbm = pl.BlockSpec(memory_space=pl.ANY)
    moving = len(more) > 0
    extra, scratch = (), []
    if moving:
        prior = more[1]
        extra = jax.ShapeDtypeStruct(prior.shape[1:], BF), jax.ShapeDtypeStruct((rows // 2, width), F32)
        scratch = scatter_scratch(rows // 2, width) + [pltpu.VMEM(prior.shape, BF)] + line_scratch(*prior.shape[1:])
    return pl.pallas_call(
        functools.partial(attend_back_kernel, ns, nb, moving),
        out_shape=(
            jax.ShapeDtypeStruct((nb, 4 * width // nb, share), BF),
            jax.ShapeDtypeStruct((tokens, 3 * share), BF),
            jax.ShapeDtypeStruct((1, 3 * share), F32),
        )
        + extra,
        in_specs=[pl.BlockSpec(memory_space=pltpu.SMEM), vm, vm, vm, vm, vm] + [hbm, vm, vm, vm, hbm, hbm][: len(more)],
        out_specs=(hbm, vm, vm) + (vm,) * len(extra),
        scratch_shapes=[
            pltpu.VMEM((tokens, share), BF),
            pltpu.VMEM((width, width if moving else 3 * share), BF),
            pltpu.VMEM((share, width), BF),
            pltpu.VMEM((tokens, HEAD_DIM), F32),
            pltpu.VMEM((tokens, HEAD_DIM), F32),
            pltpu.SemaphoreType.DMA((4,)),
        ]
        + scratch,
        compiler_params=pltpu.CompilerParams(
            collective_id=9 if moving else None, has_side_effects=moving, vmem_limit_bytes=60 * 2**20
        ),
        cost_estimate=pl.CostEstimate(
            flops=40 * 10**9, bytes_accessed=12 * width * share, transcendentals=tokens * 512 * share // 128
        ),
        name="attend_back",
    )(lengths, h1t, da, wout, o, qkv, *more)


def slopes(u, dg):
    sq = u * u
    th = jnp.tanh(ROOT * u * (1.0 + 0.044715 * sq))
    cdf = 0.5 * (1.0 + th)
    slope = cdf + 0.5 * u * (1.0 - th * th) * (ROOT * (1.0 + 3.0 * 0.044715 * sq))
    return (u * cdf).astype(BF), (dg * slope).astype(BF)


def ff_first_kernel(ns, nb, h2, cot, wg, bias, own, g_out, du_out, gb, h2t, dh2, w1, w2, gw1, gw2, near2, near1, *sems):
    load, to2, from2, to1, from1 = sems
    tokens, width = h2.shape
    chunk = g_out.shape[1]
    depth = width // (ns * nb)
    part = chunk // nb
    pieces = width // chunk
    half = ns * depth
    chips = nb // 2
    tile = min(512, chunk)
    step = min(256, tokens)
    seq, batch = lax.axis_index("seq"), lax.axis_index("batch")
    chip, core = batch // 2, lax.rem(batch, 2)
    twin = (seq, 2 * chip + 1 - core)
    load_rows(ns, nb, depth, wg, w1, load.at[0])

    def load2(k, carry):
        for p in range(pieces):
            pltpu.make_async_copy(
                wg.at[k, pl.ds(half + p * part, part), :],
                w2.at[pl.ds(k * part, part), p * chunk : (p + 1) * chunk],
                load.at[1],
            ).start()
        return carry

    lax.fori_loop(0, nb, load2, 0)
    barrier = pltpu.get_barrier_semaphore()
    pl.semaphore_signal(barrier, inc=1, device_id=twin, device_id_type=MESH)
    for r in range(0, tokens, step):
        h2t[:, r : r + step] = h2[r : r + step, :].T
    pltpu.make_async_copy(w1, w1, load.at[0]).wait()
    pltpu.make_async_copy(w2, w2, load.at[1]).wait()

    def one_tile(j, carry):
        cols = pl.ds(pl.multiple_of(j * tile, tile), tile)
        total = jnp.zeros((1, tile), F32)
        for r in range(0, tokens, step):
            rows = slice(r, r + step)
            u = jnp.dot(h2[rows, :], w1[:, cols], preferred_element_type=F32) + bias[:, cols]
            g, du = slopes(u, dot_t(cot[rows, :], w2[cols, :]))
            g_out[rows, cols] = g
            du_out[rows, cols] = du
            total += jnp.sum(du.astype(F32), 0, keepdims=True)
        gb[:, cols] = total
        return carry

    lax.fori_loop(0, chunk // tile, one_tile, 0)

    def second(j, carry):
        cols = pl.ds(pl.multiple_of(j * tile, tile), tile)
        gt = g_out[:, cols].T
        for r in range(0, width, 512):
            gw2[cols, r : r + 512] = jnp.dot(gt, cot[:, r : r + 512], preferred_element_type=F32).astype(BF)
        return carry

    lax.fori_loop(0, chunk // tile, second, 0)
    pl.semaphore_wait(barrier, 1)

    def rows2(c, kept):
        return pl.ds(pl.multiple_of((2 * c + (core if kept else 1 - core)) * part, part), part)

    def rows1(c, s, kept):
        return pl.ds(pl.multiple_of((s * nb + 2 * c + (core if kept else 1 - core)) * depth, depth), depth)

    for c in range(chips):
        for p in range(pieces):
            span = slice(p * part, (p + 1) * part)
            send(gw2.at[rows2(c, False), p * chunk : (p + 1) * chunk], near2.at[c, span], to2, from2, twin)

    def first(j, carry):
        cols = pl.ds(pl.multiple_of(j * tile, tile), tile)
        for r in range(0, width, 512):
            gw1[r : r + 512, cols] = jnp.dot(
                h2t[r : r + 512, :], du_out[:, cols], preferred_element_type=F32
            ).astype(BF)
        return carry

    lax.fori_loop(0, chunk // tile, first, 0)
    for c in range(chips):
        for s in range(ns):
            send(gw1.at[rows1(c, s, False)], near1.at[c, s * depth : (s + 1) * depth], to1, from1, twin)

    def whole(near, send_sem, recv_sem):
        return pltpu.make_async_remote_copy(
            src_ref=near, dst_ref=near, send_sem=send_sem, recv_sem=recv_sem, device_id=twin, device_id_type=MESH
        )

    def back(k, carry):
        rows = pl.ds(pl.multiple_of(k * step, step), step)
        for c in range(0, width, 512):
            dh2[rows, c : c + 512] = dot_t(du_out[rows, :], w1[c : c + 512, :]).astype(BF)
        return carry

    lax.fori_loop(0, tokens // step, back, 0)
    whole(near2, to2, from2).wait_recv()
    for c in range(chips):
        for p in range(pieces):
            mine = gw2[rows2(c, True), p * chunk : (p + 1) * chunk]
            total = mine.astype(F32) + near2[c, p * part : (p + 1) * part].astype(F32)
            own[c, half + p * part : half + (p + 1) * part] = total.astype(BF)
    whole(near1, to1, from1).wait_recv()
    for c in range(chips):
        for s in range(ns):
            total = gw1[rows1(c, s, True), :].astype(F32) + near1[c, s * depth : (s + 1) * depth].astype(F32)
            own[c, s * depth : (s + 1) * depth] = total.astype(BF)
    whole(near2, to2, from2).wait_send()
    whole(near1, to1, from1).wait_send()


def ff_first(ns, nb, h2, cot, wg, bias):
    tokens, width = h2.shape
    chunk = wg.shape[2]
    half = width // nb
    vm = pl.BlockSpec(memory_space=pltpu.VMEM)
    dma = pltpu.SemaphoreType.DMA
    inner = jax.ShapeDtypeStruct((tokens, chunk), BF)
    near = pltpu.VMEM((nb // 2, half, chunk), BF)
    return pl.pallas_call(
        functools.partial(ff_first_kernel, ns, nb),
        out_shape=(
            jax.ShapeDtypeStruct((nb // 2, 2 * half, chunk), BF),
            inner,
            inner,
            jax.ShapeDtypeStruct((1, chunk), F32),
            jax.ShapeDtypeStruct((width, tokens), BF),
            jax.ShapeDtypeStruct((tokens, width), BF),
        ),
        in_specs=[vm, vm, pl.BlockSpec(memory_space=pl.ANY), vm],
        out_specs=(vm,) * 6,
        scratch_shapes=[
            pltpu.VMEM((width, chunk), BF),
            pltpu.VMEM((chunk, width), BF),
            pltpu.VMEM((width, chunk), BF),
            pltpu.VMEM((chunk, width), BF),
            near,
            near,
            dma((2,)),
            dma,
            dma,
            dma,
            dma,
        ],
        compiler_params=pltpu.CompilerParams(collective_id=7, has_side_effects=True, vmem_limit_bytes=60 * 2**20),
        cost_estimate=pl.CostEstimate(flops=40 * 10**9, bytes_accessed=8 * wg.size, transcendentals=tokens * chunk),
        name="ff_first",
    )(h2, cot, wg, bias)


def ff_kernel(ns, nb, first, moving, *refs):
    line = None
    if first:
        h2, cot, wg, bias, gwg, g_out, du_out, gb, h2t, dh2, w1, w2, gw1, gw2, sems = refs
    elif moving:
        h2, h2t, cot, wg, bias, own, gwg, g_out, du_out, gb, got, w1, w2, gw1, gw2, sems, held, s0, s1, s2 = refs
        line = Line(0, own, None, got, held, s0, s1, s2)
    else:
        h2, h2t, cot, wg, bias, gwg, g_out, du_out, gb, w1, w2, gw1, gw2, sems = refs
    tokens, width = h2.shape
    chunk = g_out.shape[1]
    depth = width // (ns * nb)
    part = chunk // nb
    pieces = width // chunk
    half = ns * depth
    tile = min(512, chunk)
    tiles = chunk // tile
    step = min(256, tokens)

    def load1(k, carry):
        s, b = k // nb, lax.rem(k, nb)
        pltpu.make_async_copy(
            wg.at[b, pl.ds(s * depth, depth), :], w1.at[pl.ds(k * depth, depth), :], sems.at[0]
        ).start()
        return carry

    def load2(k, carry):
        for p in range(pieces):
            pltpu.make_async_copy(
                wg.at[k, pl.ds(half + p * part, part), :],
                w2.at[pl.ds(k * part, part), p * chunk : (p + 1) * chunk],
                sems.at[1],
            ).start()
        return carry

    lax.fori_loop(0, ns * nb, load1, 0)
    lax.fori_loop(0, nb, load2, 0)
    if moving:
        line.ready()
        barrier = pltpu.get_barrier_semaphore()
        for other in line.neighbours():
            pl.semaphore_signal(barrier, inc=1, device_id=other, device_id_type=MESH)
        pl.semaphore_wait(barrier, 2)
        line.go()
    if first:
        for r in range(0, tokens, step):
            h2t[:, r : r + step] = h2[r : r + step, :].T
    pltpu.make_async_copy(w1, w1, sems.at[0]).wait()
    pltpu.make_async_copy(w2, w2, sems.at[1]).wait()

    def one_tile(j, carry):
        at = pl.multiple_of(j * tile, tile)
        cols = pl.ds(at, tile)
        total = jnp.zeros((1, tile), F32)
        for r in range(0, tokens, step):
            rows = slice(r, r + step)
            u = jnp.dot(h2[rows, :], w1[:, cols], preferred_element_type=F32) + bias[:, cols]
            dg = lax.dot_general(
                cot[rows, :], w2[cols, :], (((1,), (1,)), ((), ())), preferred_element_type=F32
            )
            g, du = slopes(u, dg)
            g_out[rows, cols] = g
            du_out[rows, cols] = du
            total += jnp.sum(du.astype(F32), 0, keepdims=True)
        gb[:, cols] = total
        for r in range(0, width, 512):
            gw1[j, r : r + 512, :] = jnp.dot(
                h2t[r : r + 512, :], du_out[:, cols], preferred_element_type=F32
            ).astype(BF)
        gt = g_out[:, cols].T
        for r in range(0, width, 512):
            gw2[j, :, r : r + 512] = jnp.dot(
                gt, cot[:, r : r + 512], preferred_element_type=F32
            ).astype(BF)

        def store1(k, c):
            s, b = k // nb, lax.rem(k, nb)
            pltpu.make_async_copy(
                gw1.at[j, pl.ds(k * depth, depth), :],
                gwg.at[b, pl.ds(s * depth, depth), cols],
                sems.at[2],
            ).start()
            return c

        lax.fori_loop(0, ns * nb, store1, 0)
        count = tile // part

        def store2(k, c):
            for p in range(pieces):
                pltpu.make_async_copy(
                    gw2.at[j, pl.ds(k * part, part), p * chunk : (p + 1) * chunk],
                    gwg.at[j * count + k, pl.ds(half + p * part, part), :],
                    sems.at[3],
                ).start()
            return c

        lax.fori_loop(0, count, store2, 0)
        return carry

    lax.fori_loop(0, tiles, one_tile, 0)
    if first:
        for r in range(0, tokens, step):
            for c in range(0, width, 512):
                part_sum = dot_t(du_out[r : r + step, :], w1[c : c + 512, :])
                dh2[r : r + step, c : c + 512] = part_sum.astype(BF)
    pltpu.make_async_copy(gw1, gw1, sems.at[2]).wait()
    pltpu.make_async_copy(gw2, gw2, sems.at[3]).wait()
    if moving:
        line.stop()


def ff_chunk(ns, nb, h2, h2t, cot, wg, bias, own=None):
    tokens, width = h2.shape
    chunk = wg.shape[2]
    tile = min(512, chunk)
    first = h2t is None
    vm = pl.BlockSpec(memory_space=pltpu.VMEM)
    hbm = pl.BlockSpec(memory_space=pl.ANY)
    inner = jax.ShapeDtypeStruct((tokens, chunk), BF)
    extra = (jax.ShapeDtypeStruct((width, tokens), BF), jax.ShapeDtypeStruct((tokens, width), BF)) if first else ()
    given = (h2, cot, wg, bias) if first else (h2, h2t, cot, wg, bias)
    moving = own is not None
    more = []
    if moving:
        given += (own,)
        extra = (jax.ShapeDtypeStruct((2,) + own.shape[1:], BF),)
        more = line_scratch(*own.shape[1:])
    return pl.pallas_call(
        functools.partial(ff_kernel, ns, nb, first, moving),
        out_shape=(jax.ShapeDtypeStruct(wg.shape, BF), inner, inner, jax.ShapeDtypeStruct((1, chunk), F32)) + extra,
        in_specs=[hbm if one is wg or one is own else vm for one in given],
        out_specs=(hbm,) + (vm,) * (3 + len(extra)),
        scratch_shapes=[
            pltpu.VMEM((width, chunk), BF),
            pltpu.VMEM((chunk, width), BF),
            pltpu.VMEM((chunk // tile, width, tile), BF),
            pltpu.VMEM((chunk // tile, tile, width), BF),
            pltpu.SemaphoreType.DMA((4,)),
        ]
        + more,
        compiler_params=pltpu.CompilerParams(
            collective_id=4 if moving else None, has_side_effects=moving, vmem_limit_bytes=60 * 2**20
        ),
        cost_estimate=pl.CostEstimate(
            flops=40 * 10**9,
            bytes_accessed=4 * wg.size,
            transcendentals=tokens * chunk,
        ),
        name="ff_chunk",
    )(*given)


def greet(more=()):
    me, batch = lax.axis_index("seq"), lax.axis_index("batch")
    by_x = me + 1 - 2 * lax.rem(me, 2)
    by_y = lax.rem(me + 2, 4)
    barrier = pltpu.get_barrier_semaphore()
    for other in [(by_x, batch), (by_y, batch), *more]:
        pl.semaphore_signal(barrier, inc=1, device_id=other, device_id_type=MESH)
    pl.semaphore_wait(barrier, 2 + len(more))
    return me, by_x, by_y, (by_x, batch), (by_y, batch)


def scatter_steps(partial, place, buffers, send, recv):
    me, by_x, by_y, to_x, to_y = place
    out, via, from_x, from_y = buffers
    half = via.shape[1]
    top, low = slice(0, half), slice(half, 2 * half)
    far = 3 - me

    def copy(k, src, dst, to):
        one = pltpu.make_async_remote_copy(
            src_ref=src, dst_ref=dst, send_sem=send.at[k], recv_sem=recv.at[k], device_id=to, device_id_type=MESH
        )
        one.start()
        return one

    out[0] = partial(far).astype(BF)
    c0 = copy(0, out.at[0, top], via.at[0], to_y)
    c1 = copy(1, out.at[0, low], via.at[1], to_x)
    yield
    block = partial(by_x)
    out[1, low] = block[low].astype(BF)
    c2 = copy(2, out.at[1, low], from_x.at[low], to_x)
    x_top = block[top]
    yield
    block = partial(by_y)
    out[2, top] = block[top].astype(BF)
    c3 = copy(3, out.at[2, top], from_y.at[top], to_y)
    y_low = block[low]
    yield
    c0.wait_recv()
    out[1, top] = (x_top + via[0].astype(F32)).astype(BF)
    c4 = copy(4, out.at[1, top], from_x.at[top], to_x)
    c1.wait_recv()
    out[2, low] = (y_low + via[1].astype(F32)).astype(BF)
    c5 = copy(5, out.at[2, low], from_y.at[low], to_y)
    yield
    mine = partial(me)
    yield
    c3.wait_recv()
    c4.wait_recv()
    mine_top = mine[top] + from_x[top].astype(F32) + from_y[top].astype(F32)
    c2.wait_recv()
    c5.wait_recv()
    mine_low = mine[low] + from_x[low].astype(F32) + from_y[low].astype(F32)
    for one in (c0, c1, c2, c3, c4, c5):
        one.wait_send()
    yield mine_top, mine_low


def scatter_sum(partial, place, buffers, send, recv):
    return list(scatter_steps(partial, place, buffers, send, recv))[-1]


def scatter_scratch(rows, width):
    return [
        pltpu.VMEM((3, rows, width), BF),
        pltpu.VMEM((2, rows // 2, width), BF),
        pltpu.VMEM((rows, width), BF),
        pltpu.VMEM((rows, width), BF),
        pltpu.SemaphoreType.DMA((6,)),
        pltpu.SemaphoreType.DMA((6,)),
    ]


def gather_steps(full, rows, place, send_sems, recv_sems):
    me, by_x, by_y, to_x, to_y = place
    half = rows // 2

    def copy(k, block, part, to):
        at = full.at[pl.ds(pl.multiple_of(block * rows + part * half, half), half)]
        return send(at, at, send_sems.at[k], recv_sems.at[k], to)

    c0 = copy(0, me, 0, to_x)
    c3 = copy(3, me, 1, to_y)
    c2 = copy(2, me, 0, to_y)
    c1 = copy(1, me, 1, to_x)
    yield
    c0.wait_recv()
    c4 = copy(4, by_x, 0, to_y)
    c3.wait_recv()
    c5 = copy(5, by_y, 1, to_x)
    yield
    for one in (c1, c2, c4, c5):
        one.wait_recv()
    for one in (c0, c1, c2, c3, c4, c5):
        one.wait_send()


def gather_blocks(full, rows, place, send_sems, recv_sems):
    for _ in gather_steps(full, rows, place, send_sems, recv_sems):
        pass


GATHER_SEMS = [pltpu.SemaphoreType.DMA((6,)), pltpu.SemaphoreType.DMA((6,))]


def middle_kernel(o, wout, mine, obias, gain, shift, x1, h2, out, via, from_x, from_y, s1, r1, s2, r2):
    rows, width = mine.shape
    half = rows // 2
    place = greet()

    def partial(block):
        at = pl.multiple_of(block * rows, rows)
        return jnp.dot(o[pl.ds(at, rows), :], wout[...], preferred_element_type=F32)

    sums = scatter_sum(partial, place, (out, via, from_x, from_y), s1, r1)
    for part, total in enumerate(sums):
        span = slice(part * half, part * half + half)
        res = mine[span, :].astype(F32) + (total + obias[...])
        x1[span, :] = res
        normed, _ = norm_stats(res)
        at = pl.multiple_of(place[0] * rows + part * half, half)
        h2[pl.ds(at, half), :] = (normed * gain[...] + shift[...]).astype(BF)
    gather_blocks(h2, rows, place, s2, r2)


def middle(o, wout, mine, obias, gain, shift):
    tokens = o.shape[0]
    rows, width = mine.shape
    vm = pl.BlockSpec(memory_space=pltpu.VMEM)
    return pl.pallas_call(
        middle_kernel,
        out_shape=(jax.ShapeDtypeStruct((rows, width), F32), jax.ShapeDtypeStruct((tokens, width), BF)),
        in_specs=[vm] * 6,
        out_specs=(vm, vm),
        scratch_shapes=scatter_scratch(rows, width) + GATHER_SEMS,
        compiler_params=pltpu.CompilerParams(collective_id=1, has_side_effects=True, vmem_limit_bytes=56 * 2**20),
        cost_estimate=pl.CostEstimate(flops=40 * 10**9, bytes_accessed=12 * tokens * width, transcendentals=0),
        name="project_out",
    )(o, wout, mine, obias, gain, shift)


def ff_back_kernel(ns, nb, du, wg, before, x1, cot, gain, own, prior, *refs):
    dx1, da, sums, got, w, load_sem, out, via, from_x, from_y, s1, r1, s2, r2, *moving = refs
    line = Line(1, own, prior, got, *moving)
    rows, width = x1.shape
    half = rows // 2
    load_rows(ns, nb, width // (ns * nb), wg, w, load_sem)
    line.ready()
    place = greet(line.neighbours())
    pltpu.make_async_copy(w, w, load_sem).wait()

    def partial(block):
        at = pl.multiple_of(block * rows, rows)
        return before[pl.ds(at, rows), :].astype(F32) + dot_t(du[pl.ds(at, rows), :], w[...])

    steps = scatter_steps(partial, place, (out, via, from_x, from_y), s1, r1)
    next(steps)
    line.go()
    *_, halves = steps
    totals = [jnp.zeros((1, width), F32)] * 3
    for part, grad in enumerate(halves):
        span = slice(part * half, part * half + half)
        normed, rstd = norm_stats(x1[span, :])
        res = cot[span, :].astype(F32) + norm_back(grad, normed, rstd, gain[...])
        dx1[span, :] = res
        low = res.astype(BF)
        at = pl.multiple_of(place[0] * rows + part * half, half)
        da[pl.ds(at, half), :] = low
        for k, term in enumerate((low.astype(F32), grad * normed, grad)):
            totals[k] += jnp.sum(term, 0, keepdims=True)
    gather = gather_steps(da, rows, place, s2, r2)
    next(gather)
    for k in range(3):
        sums[k : k + 1, :] = totals[k]
    for _ in gather:
        pass
    line.stop()


def ff_back(ns, nb, du, wg, before, x1, cot, gain, own, prior):
    rows, width = x1.shape
    tokens, chunk = du.shape
    vm = pl.BlockSpec(memory_space=pltpu.VMEM)
    hbm = pl.BlockSpec(memory_space=pl.ANY)
    return pl.pallas_call(
        functools.partial(ff_back_kernel, ns, nb),
        out_shape=(
            jax.ShapeDtypeStruct((rows, width), F32),
            jax.ShapeDtypeStruct((tokens, width), BF),
            jax.ShapeDtypeStruct((3, width), F32),
            jax.ShapeDtypeStruct(prior.shape, BF),
        ),
        in_specs=[vm, hbm] + [vm] * 4 + [hbm, vm],
        out_specs=(vm,) * 4,
        scratch_shapes=[pltpu.VMEM((width, chunk), BF), pltpu.SemaphoreType.DMA]
        + scatter_scratch(rows, width)
        + GATHER_SEMS
        + line_scratch(*prior.shape[1:]),
        compiler_params=pltpu.CompilerParams(collective_id=2, has_side_effects=True, vmem_limit_bytes=56 * 2**20),
        cost_estimate=pl.CostEstimate(flops=40 * 10**9, bytes_accessed=12 * tokens * width, transcendentals=0),
        name="ff_back",
    )(du, wg, before, x1, cot, gain, own, prior)


def finish_kernel(ns, nb, count, dproj, wq, *refs):
    summed, gs, wgs = refs[:count], refs[count : 2 * count], refs[2 * count : 3 * count]
    mine, gain, part_grad, gains, stage, gw2, low_sum, w = refs[3 * count : 3 * count + 8]
    ws = refs[3 * count + 8 : 4 * count + 8]
    load, s0, r0, *buffers = refs[4 * count + 8 :]
    buffers, more = buffers[:6], buffers[6:]
    rows, width = mine.shape
    half = rows // 2
    chunk = summed[0].shape[1]
    part_rows, pieces = chunk // nb, width // chunk
    load_attention(ns, nb, wq, w, load.at[0])
    for c in range(count):
        load_second(nb, wgs[c], ws[c], load.at[3 + c])
    me, others, met = greet_seq(ns)
    by_x, by_y, batch = me + 1 - 2 * lax.rem(me, 2), lax.rem(me + 2, 4), lax.axis_index("batch")
    place = me, by_x, by_y, (by_x, batch), (by_y, batch)
    depth, hidden = stage.shape[0], stage.shape[1] // ns

    def ship(b, carry):
        for c in range(count):
            cols = pl.ds(pl.multiple_of(me * hidden + (b * count + c) * part_rows, part_rows), part_rows)
            from_cols = pl.ds(pl.multiple_of(b * part_rows, part_rows), part_rows)
            own = pl.ds(pl.multiple_of(me * depth, depth), depth)
            pltpu.make_async_copy(summed[c].at[own, from_cols], stage.at[:, cols], load.at[1]).start()
            for d, to in enumerate(others):
                theirs = pl.ds(pl.multiple_of(to[0] * depth, depth), depth)
                send(summed[c].at[theirs, from_cols], stage.at[:, cols], s0.at[d], r0.at[d], to)
        return carry

    for c in range(count):
        for p in range(pieces):
            pltpu.make_async_copy(
                summed[c].at[ns * depth + p * part_rows : ns * depth + (p + 1) * part_rows],
                gw2.at[c * part_rows : (c + 1) * part_rows, p * chunk : (p + 1) * chunk],
                load.at[2],
            ).start()

    def input_grad(block):
        at = pl.multiple_of(block * rows, rows)
        return dot_t(dproj[pl.ds(at, rows), :], w[...])

    def branch(block):
        at = pl.ds(pl.multiple_of(block * rows + half, half), half)
        total = jnp.dot(gs[0][at, :], ws[0][...], preferred_element_type=F32)
        for c in range(1, count):
            total += jnp.dot(gs[c][at, :], ws[c][...], preferred_element_type=F32)
        return total

    met()
    pltpu.make_async_copy(w, w, load.at[0]).wait()
    steps = scatter_steps(input_grad, place, buffers[:4], *buffers[4:])
    for _ in range(3):
        next(steps)
    for c in range(count):
        pltpu.make_async_copy(ws[c], ws[c], load.at[3 + c]).wait()
    others_steps = scatter_steps(branch, place, more[:4], *more[4:])
    next(others_steps)
    next(steps)
    next(others_steps)
    next(others_steps)
    lax.fori_loop(0, nb, ship, 0)
    *_, sums = steps
    totals = [jnp.zeros((1, width), F32)] * 2
    for part, grad in enumerate(sums):
        span = slice(part * half, part * half + half)
        normed, rstd = norm_stats(mine[span, :].astype(F32))
        part_grad[span, :] = norm_back(grad, normed, rstd, gain[...])
        for k, term in enumerate((grad * normed, grad)):
            totals[k] += jnp.sum(term, 0, keepdims=True)
    for k in range(2):
        gains[k : k + 1, :] = totals[k]
    *_, lows = others_steps
    for part, total in enumerate(lows):
        low_sum[part * half // 2 : (part + 1) * half // 2, :] = total
    pltpu.make_async_copy(gw2, gw2, load.at[2]).wait()
    strip = stage.at[:, :hidden]
    pltpu.make_async_copy(strip, strip, load.at[1]).wait()
    for d, to in enumerate(others):
        pltpu.make_async_remote_copy(
            src_ref=strip, dst_ref=strip, send_sem=s0.at[d], recv_sem=r0.at[d], device_id=to, device_id_type=MESH
        ).wait()


def finish(ns, nb, dproj, wq, summed, gs, wgs, mine, gain):
    rows, width = mine.shape
    count, chunk = len(summed), summed[0].shape[1]
    depth, hidden = width // (ns * nb), count * chunk
    vm = pl.BlockSpec(memory_space=pltpu.VMEM)
    hbm = pl.BlockSpec(memory_space=pl.ANY)
    dma = pltpu.SemaphoreType.DMA
    return pl.pallas_call(
        functools.partial(finish_kernel, ns, nb, count),
        out_shape=(
            jax.ShapeDtypeStruct((rows, width), F32),
            jax.ShapeDtypeStruct((2, width), F32),
            jax.ShapeDtypeStruct((depth, hidden * ns), BF),
            jax.ShapeDtypeStruct((hidden // nb, width), BF),
            jax.ShapeDtypeStruct((rows // 2, width), F32),
        ),
        in_specs=[vm, hbm] + [hbm] * count + [vm] * count + [hbm] * count + [vm] * 2,
        out_specs=(vm,) * 5,
        scratch_shapes=[pltpu.VMEM((width, dproj.shape[1]), BF)]
        + [pltpu.VMEM((chunk, width), BF)] * count
        + [dma((3 + count,)), dma((ns - 1,)), dma((ns - 1,))]
        + scatter_scratch(rows, width)
        + scatter_scratch(rows // 2, width),
        compiler_params=pltpu.CompilerParams(collective_id=3, has_side_effects=True, vmem_limit_bytes=56 * 2**20),
        cost_estimate=pl.CostEstimate(flops=40 * 10**9, bytes_accessed=24 * rows * width, transcendentals=0),
        name="finish",
    )(dproj, wq, *summed, *gs, *wgs, mine, gain)


def greet_all(ns, nb):
    me, batch = lax.axis_index("seq"), lax.axis_index("batch")
    along_seq = [(lax.rem(me + d, ns), batch) for d in range(1, ns)]
    along_batch = [(me, lax.rem(batch + d, nb)) for d in range(1, nb)]
    barrier = pltpu.get_barrier_semaphore()
    for other in along_seq + along_batch:
        pl.semaphore_signal(barrier, inc=1, device_id=other, device_id_type=MESH)
    pl.semaphore_wait(barrier, ns + nb - 2)
    return me, batch, along_seq, along_batch


def greet_seq(ns, more=()):
    me, batch = lax.axis_index("seq"), lax.axis_index("batch")
    others = [(lax.rem(me + d, ns), batch) for d in range(1, ns)]
    barrier = pltpu.get_barrier_semaphore()
    for other in [*others, *more]:
        pl.semaphore_signal(barrier, inc=1, device_id=other, device_id_type=MESH)
    return me, others, lambda: pl.semaphore_wait(barrier, ns - 1 + len(more))


def spread_kernel(ns, w_qkv, qkv, local, s0, r0):
    depth = w_qkv.shape[0]
    share = qkv.shape[1]
    width = ns * share
    me, others, met = greet_seq(ns)
    copies = []
    for t in range(3):
        cols = pl.ds(pl.multiple_of(t * width + me * share, share), share)
        rows = pl.ds(pl.multiple_of((t * ns + me) * depth, depth), depth)
        one = pltpu.make_async_copy(w_qkv.at[:, cols], qkv.at[rows], local.at[t])
        one.start()
        copies.append(one)
    met()
    for t in range(3):
        rows = pl.ds(pl.multiple_of((t * ns + me) * depth, depth), depth)
        for d, to in enumerate(others):
            cols = pl.ds(pl.multiple_of(t * width + to[0] * share, share), share)
            copies.append(send(w_qkv.at[:, cols], qkv.at[rows], s0.at[t, d], r0.at[t, d], to))
    for one in copies:
        one.wait()


def spread(ns, w_qkv):
    depth, width = w_qkv.shape[0], w_qkv.shape[1] // 3
    hbm = pl.BlockSpec(memory_space=pl.ANY)
    dma = pltpu.SemaphoreType.DMA
    return pl.pallas_call(
        functools.partial(spread_kernel, ns),
        out_shape=jax.ShapeDtypeStruct((3 * ns * depth, width // ns), BF),
        in_specs=[hbm],
        out_specs=hbm,
        scratch_shapes=[dma((3,)), dma((3, ns - 1)), dma((3, ns - 1))],
        compiler_params=pltpu.CompilerParams(collective_id=5, has_side_effects=True),
        cost_estimate=pl.CostEstimate(flops=10**6, bytes_accessed=10**4, transcendentals=0),
        name="spread",
    )(w_qkv)


def spread_ff_kernel(ns, nb, parts, w1, w2, *refs):
    packs, (stage, local, s1, r1) = refs[:parts], refs[parts:]
    depth, rows2, width = w1.shape[0], w2.shape[0], w2.shape[1]
    hidden = w1.shape[1] // ns
    part, chunk = rows2 // parts, hidden // parts
    pieces = width // chunk
    me, others, met = greet_seq(ns)
    at = pl.ds(pl.multiple_of(me * depth, depth), depth)
    cols = pl.ds(pl.multiple_of(me * hidden, hidden), hidden)
    own = pltpu.make_async_copy(w1.at[:, cols], stage.at[at], local)
    own.start()
    met()
    copies = [own]
    for d, to in enumerate(others):
        cols = pl.ds(pl.multiple_of(to[0] * hidden, hidden), hidden)
        copies.append(send(w1.at[:, cols], stage.at[at], s1.at[d], r1.at[d], to))
    for c in range(parts):
        for p in range(pieces):
            span = slice(ns * depth + p * part, ns * depth + (p + 1) * part)
            packs[c][span, :] = w2[c * part : (c + 1) * part, p * chunk : (p + 1) * chunk]
    for one in copies:
        one.wait()
    for c in range(parts):
        for b in range(nb):
            source = (b * parts + c) * part
            packs[c][: ns * depth, b * part : (b + 1) * part] = stage[:, source : source + part]


def spread_ff(ns, nb, parts, w1, w2):
    depth, hidden = w1.shape[0], w1.shape[1] // ns
    vm = pl.BlockSpec(memory_space=pltpu.VMEM)
    dma = pltpu.SemaphoreType.DMA
    pack = jax.ShapeDtypeStruct((2 * ns * depth, hidden // parts), BF)
    return pl.pallas_call(
        functools.partial(spread_ff_kernel, ns, nb, parts),
        out_shape=(pack,) * parts,
        in_specs=[pl.BlockSpec(memory_space=pl.ANY), vm],
        out_specs=(vm,) * parts,
        scratch_shapes=[pltpu.VMEM((ns * depth, hidden), BF), dma, dma((ns - 1,)), dma((ns - 1,))],
        compiler_params=pltpu.CompilerParams(collective_id=11, has_side_effects=True),
        cost_estimate=pl.CostEstimate(flops=10**6, bytes_accessed=10**4, transcendentals=0),
        name="spread_ff",
    )(w1, w2)


def whole_row(ns, nb, vecs, row, width):
    pieces = jnp.concatenate([vecs[b, s, row : row + 1, :] for b in range(nb) for s in range(ns)], 0)
    lanes = jnp.concatenate([pieces] * (width // pieces.shape[1]), 1)
    owner = lax.broadcasted_iota(jnp.int32, lanes.shape, 0)
    owner = lax.rem(owner, ns) * nb + owner // ns
    place = lax.broadcasted_iota(jnp.int32, lanes.shape, 1) // (width // (ns * nb))
    return jnp.sum(jnp.where(owner == place, lanes, 0.0), 0, keepdims=True)


def collect_kernel(ns, nb, mine, cot, vec, h1, cots, vecs, acts, local, s1, r1, s2, r2, s3, r3, s4, r4):
    rows, width = mine.shape
    half = rows // 2
    me, batch = lax.axis_index("seq"), lax.axis_index("batch")
    by_x = me + 1 - 2 * lax.rem(me, 2)
    by_y = lax.rem(me + 2, 4)
    others = [(lax.rem(me + d, ns), batch) for d in range(1, ns)]
    column = [(me, lax.rem(batch + d, nb)) for d in range(1, nb)]
    barrier = pltpu.get_barrier_semaphore()
    for other in others + column:
        pl.semaphore_signal(barrier, inc=1, device_id=other, device_id_type=MESH)
    vecs[batch, me] = vec[...]
    at_me = pl.ds(pl.multiple_of(me * rows, rows), rows)
    acts[at_me, :] = mine[...]
    own = pltpu.make_async_copy(cot, cots.at[at_me], local)
    own.start()
    pl.semaphore_wait(barrier, ns + nb - 2)
    to_x, to_y = (by_x, batch), (by_y, batch)
    small = vecs.at[batch, me]
    near = [send(small, small, s3.at[d], r3.at[d], to) for d, to in enumerate(others)]

    def normalise(block):
        span = pl.ds(pl.multiple_of(block * rows, rows), rows)
        normed, _ = norm_stats(acts[span, :].astype(F32))
        h1[span, :] = (normed * gain + shift).astype(BF)

    def copy(k, full, block, side, to, sends, recvs):
        span = full.at[pl.ds(pl.multiple_of(block * rows + side * half, half), half)]
        return send(span, span, sends.at[k], recvs.at[k], to)

    c0 = copy(0, acts, me, 0, to_x, s1, r1)
    c3 = copy(3, acts, me, 1, to_y, s1, r1)
    c2 = copy(2, acts, me, 0, to_y, s1, r1)
    c1 = copy(1, acts, me, 1, to_x, s1, r1)
    for one in near:
        one.wait_recv()
    row = vecs.at[batch]
    wide = [send(row, row, s4.at[d], r4.at[d], to) for d, to in enumerate(column)]
    for one in wide:
        one.wait_recv()
    gain, shift = whole_row(ns, nb, vecs, 0, width), whole_row(ns, nb, vecs, 1, width)
    normalise(me)
    c0.wait_recv()
    c4 = copy(4, acts, by_x, 0, to_y, s1, r1)
    c3.wait_recv()
    c5 = copy(5, acts, by_y, 1, to_x, s1, r1)
    own.wait()
    d0 = copy(0, cots, me, 0, to_x, s2, r2)
    d3 = copy(3, cots, me, 1, to_y, s2, r2)
    d2 = copy(2, cots, me, 0, to_y, s2, r2)
    d1 = copy(1, cots, me, 1, to_x, s2, r2)
    c1.wait_recv()
    normalise(by_x)
    c2.wait_recv()
    normalise(by_y)
    c4.wait_recv()
    c5.wait_recv()
    normalise(3 - me)
    d0.wait_recv()
    d4 = copy(4, cots, by_x, 0, to_y, s2, r2)
    d3.wait_recv()
    d5 = copy(5, cots, by_y, 1, to_x, s2, r2)
    for one in (d1, d2, d4, d5):
        one.wait_recv()
    for one in (c0, c1, c2, c3, c4, c5, d0, d1, d2, d3, d4, d5, *near, *wide):
        one.wait_send()


def collect(ns, nb, mine, cot, vec):
    rows, width = mine.shape
    vm = pl.BlockSpec(memory_space=pltpu.VMEM)
    hbm = pl.BlockSpec(memory_space=pl.ANY)
    dma = pltpu.SemaphoreType.DMA
    full = jax.ShapeDtypeStruct((ns * rows, width), BF)
    return pl.pallas_call(
        functools.partial(collect_kernel, ns, nb),
        out_shape=(full, full, jax.ShapeDtypeStruct((nb, ns) + vec.shape, F32)),
        in_specs=[vm, hbm, vm],
        out_specs=(vm, hbm, vm),
        scratch_shapes=[pltpu.VMEM((ns * rows, width), BF), dma]
        + [dma((6,))] * 4
        + [dma((ns - 1,))] * 2
        + [dma((nb - 1,))] * 2,
        compiler_params=pltpu.CompilerParams(collective_id=6, has_side_effects=True, vmem_limit_bytes=40 * 2**20),
        cost_estimate=pl.CostEstimate(flops=10**6, bytes_accessed=10**4, transcendentals=0),
        name="collect",
    )(mine, cot, vec)


def home_kernel(ns, nb, summed, sums, gqkv, gout, small, stage, near, mid, far, local, s0, r0, s1, r1, s2, r2):
    depth, width = gout.shape
    share = width // ns
    me, batch, others, column = greet_all(ns, nb)
    first = [send(sums.at[to[1]], near.at[d], s1.at[d], r1.at[d], to) for d, to in enumerate(column)]
    copies = []
    for t in range(3):
        cols = pl.ds(pl.multiple_of(t * width + me * share, share), share)
        for d, to in enumerate(others):
            rows = pl.ds(pl.multiple_of((t * ns + to[0]) * depth, depth), depth)
            copies.append(send(summed.at[rows], stage.at[:, cols], s0.at[t, d], r0.at[t, d], to))
        rows = pl.ds(pl.multiple_of((t * ns + me) * depth, depth), depth)
        own = pltpu.make_async_copy(summed.at[rows], stage.at[:, cols], local.at[t])
        own.start()
        copies.append(own)
    for p in range(ns):
        rows = slice((3 * ns + p) * depth, (3 * ns + p + 1) * depth)
        gout[:, p * share : (p + 1) * share] = summed[rows, :].astype(F32)
    total = sums[batch]
    for d, one in enumerate(first):
        one.wait_recv()
        total += near[d]
    mid[...] = total
    second = [send(mid.at[to[0]], far.at[d], s2.at[d], r2.at[d], to) for d, to in enumerate(others)]
    for one in copies:
        one.wait()
    gqkv[...] = stage[...].astype(F32)
    total = mid[me]
    for d, one in enumerate(second):
        one.wait_recv()
        total += far[d]
    small[...] = total
    for one in first + second:
        one.wait_send()


def home(ns, nb, summed, sums):
    rows, share = summed.shape
    depth, width = rows // (4 * ns), ns * share
    tail = sums.shape[2:]
    vm = pl.BlockSpec(memory_space=pltpu.VMEM)
    dma = pltpu.SemaphoreType.DMA
    return pl.pallas_call(
        functools.partial(home_kernel, ns, nb),
        out_shape=(
            jax.ShapeDtypeStruct((depth, 3 * width), F32),
            jax.ShapeDtypeStruct((depth, width), F32),
            jax.ShapeDtypeStruct(tail, F32),
        ),
        in_specs=[vm, vm],
        out_specs=(vm, vm, vm),
        scratch_shapes=[
            pltpu.VMEM((depth, 3 * width), BF),
            pltpu.VMEM((nb - 1, ns) + tail, F32),
            pltpu.VMEM((ns,) + tail, F32),
            pltpu.VMEM((ns - 1,) + tail, F32),
            dma((3,)),
            dma((3, ns - 1)),
            dma((3, ns - 1)),
            dma((nb - 1,)),
            dma((nb - 1,)),
            dma((ns - 1,)),
            dma((ns - 1,)),
        ],
        compiler_params=pltpu.CompilerParams(collective_id=8, has_side_effects=True),
        cost_estimate=pl.CostEstimate(flops=5 * 10**9, bytes_accessed=4 * summed.size, transcendentals=0),
        name="home",
    )(summed, sums)


PARTS = 2


def gather_seq(value):
    return lax.all_gather(value, "seq", axis=0, tiled=True)


def scatter_seq(partial):
    return lax.psum_scatter(partial, "seq", scatter_dimension=0, tiled=True)


def scatter_batch(parts):
    flat = parts.reshape(-1, parts.shape[-1])
    return lax.psum_scatter(flat, "batch", scatter_dimension=0, tiled=True)


def unpermute(ns, nb, gathered):
    depth = gathered.shape[1] // ns
    return gathered.reshape(nb, ns, depth, -1).transpose(1, 0, 2, 3).reshape(ns * nb * depth, -1)


def unpack_attention(ns, nb, packed):
    share = packed.shape[2]
    parts = packed.reshape(nb, 3, ns, -1, share)
    return parts.transpose(2, 0, 3, 1, 4).reshape(ns * share, 3 * share)


def body(
    block_input,
    lengths,
    ln1_gain,
    ln1_bias,
    w_qkv,
    qv_bias,
    w_out,
    out_bias,
    ln2_gain,
    ln2_bias,
    w_fc1,
    fc1_bias,
    w_fc2,
    fc2_bias,
    out_cotangent,
):
    ns, nb = lax.axis_size("seq"), lax.axis_size("batch")
    seq = lax.axis_index("seq")
    rows, width = block_input.shape[1:]
    share = width // ns
    depth = width // (ns * nb)
    hidden = w_fc1.shape[1] // ns
    chunk = hidden // PARTS
    part = chunk // nb
    pieces = width // chunk
    planar = ns == 4 and nb == 8
    mine, cot_mine = block_input[0], out_cotangent[0]

    vectors = (ln1_gain, ln1_bias, qv_bias, out_bias, ln2_gain, ln2_bias, fc1_bias, fc2_bias)
    wout = lax.all_gather(w_out, "batch", axis=0, tiled=True)
    if planar:
        wq = spread(ns, w_qkv)
        wq, w_fc1 = lax.optimization_barrier((wq, w_fc1))
        packs = spread_ff(ns, nb, PARTS, w_fc1, w_fc2)
        packs, vectors, wout = lax.optimization_barrier((packs, vectors, wout))
        spare = jnp.zeros((1024 - 2 * depth - sum(vec.shape[0] for vec in vectors),), BF)
        block = jnp.concatenate([vectors[0], vectors[0], vectors[1], vectors[1], *vectors[2:], spare])
        block = block.astype(F32).reshape(8, 128)
        h1, cot, packed = collect(ns, nb, mine, cot_mine, block)
        packed = packed.transpose(1, 0, 2, 3).reshape(ns * nb, 1024)
        packed = jnp.concatenate([packed[:, :depth], packed[:, 2 * depth : 3 * depth], packed[:, 4 * depth :]], 1)
    else:
        wq = lax.all_to_all(w_qkv.reshape(depth, 3, ns, share), "seq", 2, 0).transpose(2, 0, 1, 3)
        wq = wq.reshape(3 * ns * depth, share)
        vector = jnp.concatenate(vectors).astype(F32)
        packed = lax.all_gather(vector, ("seq", "batch"), axis=0, tiled=False)
    wq = lax.all_gather(wq, "batch", axis=0, tiled=True).reshape(nb, 3 * ns * depth, share)
    full, at = [], 0
    for vec in vectors:
        full.append(packed[:, at : at + vec.shape[0]].reshape(1, -1))
        at += vec.shape[0]
    gain1, shift1, qv, obias, gain2, shift2, bias1, bias2 = full
    bias1 = lax.dynamic_slice_in_dim(bias1, seq * hidden, hidden, 1).reshape(nb, PARTS, part)
    qbias = lax.dynamic_slice_in_dim(qv, seq * share, share, 1)
    vbias = lax.dynamic_slice_in_dim(qv, width + seq * share, share, 1)
    bias3 = jnp.concatenate([qbias, jnp.zeros_like(qbias), vbias], 1)

    if not planar:
        fc1_part = lax.all_to_all(w_fc1.reshape(depth, ns, hidden), "seq", 1, 0)
        fc1_part = fc1_part.reshape(ns * depth, nb, PARTS, part)
        fc2_part = w_fc2.reshape(PARTS, part, pieces, chunk)
        packs = []
        for c in range(PARTS):
            first = fc1_part[:, :, c].reshape(ns * depth, chunk)
            second = fc2_part[c].transpose(1, 0, 2).reshape(pieces * part, chunk)
            packs.append(jnp.concatenate([first, second], 0))
        h1 = (norm_stats(gather_seq(mine).astype(F32))[0] * gain1 + shift1).astype(BF)
        cot = gather_seq(cot_mine)
    wgs = [lax.all_gather(pack, "batch", axis=0, tiled=True).reshape(nb, -1, chunk) for pack in packs]

    qkv, o, h1t = attend(ns, nb, lengths, h1, wq, bias3)
    if planar:
        x1, h2 = middle(o, wout, mine, obias, gain2, shift2)
    else:
        a = scatter_seq(jnp.dot(o, wout, preferred_element_type=F32))
        x1 = mine.astype(F32) + (a + obias)
        h2 = gather_seq((norm_stats(x1)[0] * gain2 + shift2).astype(BF))

    line = ()
    if planar:
        own, g, du, gb, h2t, before = ff_first(ns, nb, h2, cot, wgs[0], bias1[:, 0].reshape(1, chunk))
        line = (own,)
        h2t, gain1, gain2, bias2 = lax.optimization_barrier((h2t, gain1, gain2, bias2))
        gws = [None]
    else:
        gw, g, du, gb, h2t, before = ff_chunk(ns, nb, h2, None, cot, wgs[0], bias1[:, 0].reshape(1, chunk))
        gws = [scatter_batch(gw)]
    gs, dus, gb1 = [g], [du], [gb.reshape(nb, 1, part)]
    for c in range(1, PARTS):
        gw, g, du, gb, *got = ff_chunk(ns, nb, h2, h2t, cot, wgs[c], bias1[:, c].reshape(1, chunk), *line)
        gws.append(scatter_batch(gw))
        gs.append(g)
        dus.append(du)
        gb1.append(gb.reshape(nb, 1, part))
    if planar:
        dx1, da, rows2, got = ff_back(ns, nb, dus[1], wgs[1], before, x1, cot_mine, gain2, own, got[0])
        line = own, got, *gs, *wgs
    else:
        dh2 = before.astype(F32) + dot_t(dus[1], unpermute(ns, nb, wgs[1][:, : ns * depth]))
        dh2 = scatter_seq(dh2)
        normed2, rstd2 = norm_stats(x1)
        dx1 = cot_mine.astype(F32) + norm_back(dh2, normed2, rstd2, gain2)
        da_mine = dx1.astype(BF)
        rows2 = jnp.stack([jnp.sum(term, 0) for term in (da_mine.astype(F32), dh2 * normed2, dh2)])
        da = gather_seq(da_mine)

    gattn, dproj, gqv, *more = attend_back(ns, nb, lengths, h1t, da, wout, o, qkv, *line)
    if planar:
        gws[0], y = more
    gattn = scatter_batch(gattn)
    if planar:
        gx, rows1, gw1, gw2, lower = finish(ns, nb, dproj, wq, gws, gs, wgs, mine, gain1)
        gx, rows2, gqv, gb1, cot_mine, y = lax.optimization_barrier((gx, rows2, gqv, gb1, cot_mine, y))
        gx = dx1 + gx
        out = (x1 + (jnp.concatenate([y, lower], 0) + bias2)).astype(BF)
        gw1, gw2 = gw1.astype(F32), gw2.astype(F32)
    else:
        dh1 = scatter_seq(dot_t(dproj, unpack_attention(ns, nb, wq)))
        normed1, rstd1 = norm_stats(mine.astype(F32))
        rows1 = jnp.stack([jnp.sum(dh1 * normed1, 0), jnp.sum(dh1, 0)])
        gx = dx1 + norm_back(dh1, normed1, rstd1, gain1)
        y = 0.0
        for g, wg in zip(gs, wgs):
            w2 = wg[:, ns * depth :].reshape(nb, pieces, part, chunk).transpose(0, 2, 1, 3).reshape(chunk, width)
            y += jnp.dot(g, w2, preferred_element_type=F32)
        out = (x1 + (scatter_seq(y) + bias2)).astype(BF)

    if not planar:
        gw1 = jnp.stack([gw[: ns * depth].reshape(ns, depth, nb, part) for gw in gws], 3)
        gw1 = lax.all_to_all(gw1, "seq", 0, 1).astype(F32).reshape(depth, ns * hidden)
        gw2 = jnp.stack([gw[ns * depth :].reshape(pieces, part, chunk) for gw in gws], 0)
        gw2 = gw2.astype(F32).transpose(0, 2, 1, 3).reshape(PARTS * part, width)
        gwqkv = gattn[: 3 * ns * depth].reshape(3, ns, depth, share)
        gwqkv = lax.all_to_all(gwqkv, "seq", 1, 2).astype(F32).transpose(1, 0, 2, 3).reshape(depth, 3 * width)
        gwo = gattn[3 * ns * depth :].reshape(ns, depth, share).astype(F32).transpose(1, 0, 2).reshape(depth, width)

    def place(part, size):
        return lax.dynamic_update_slice_in_dim(jnp.zeros((size,), F32), part, seq * part.shape[0], 0)

    gqv = gqv[0]
    gqv = jnp.concatenate([place(gqv[:share], width), place(gqv[2 * share :], width)])
    gb1 = place(jnp.stack(gb1, 1).reshape(-1), ns * hidden)
    gb2 = jnp.sum(cot_mine.astype(F32), 0)

    def shards(grads):
        return grads.reshape(grads.shape[0], ns * nb, -1).transpose(1, 0, 2).reshape(ns * nb, -1)

    sums = [shards(rows1), gqv.reshape(ns * nb, -1), shards(rows2), gb1.reshape(ns * nb, -1), gb2.reshape(ns * nb, -1)]
    sums = jnp.concatenate(sums, 1)
    if planar:
        sums = jnp.pad(sums, ((0, 0), (0, 1024 - sums.shape[1]))).reshape(ns, nb, 8, 128)
        sums, gx, out, gw1, gw2 = lax.optimization_barrier((sums.transpose(1, 0, 2, 3), gx, out, gw1, gw2))
        gwqkv, gwo, sums = home(ns, nb, gattn, sums)
        sums = sums.reshape(-1)
    else:
        sums = lax.psum_scatter(sums, ("seq", "batch"), scatter_dimension=0, tiled=True)[0]
    small, at = [], 0
    for vec in vectors:
        small.append(sums[at : at + vec.shape[0]])
        at += vec.shape[0]
    return (
        out[None],
        gx[None],
        small[0],
        small[1],
        gwqkv,
        small[2],
        gwo,
        small[3],
        small[4],
        small[5],
        gw1,
        small[6],
        gw2,
        small[7],
    )


def solution(mesh):
    shard = P(("seq", "batch"))
    shard2 = P(("seq", "batch"), None)
    acts = P("batch", "seq", None)
    return jax.shard_map(
        body,
        mesh=mesh,
        in_specs=(acts, P("batch"), shard, shard, shard2, shard, shard2, shard, shard, shard, shard2, shard, shard2, shard, acts),
        out_specs=(acts, acts, shard, shard, shard2, shard, shard2, shard, shard, shard, shard2, shard, shard2, shard),
        check_vma=False,
    )
```

```python
import functools
import math

import jax
import jax.numpy as jnp
from jax import lax
from jax.experimental import pallas as pl
from jax.experimental.pallas import tpu as pltpu
from jax.sharding import PartitionSpec as P

HEAD_DIM = 128
WINDOW = 256
EPS = 1e-05
BF = jnp.bfloat16
F32 = jnp.float32
ROOT = math.sqrt(2.0 / math.pi)


def norm_stats(values):
    mean = jnp.mean(values, -1, keepdims=True)
    centred = values - mean
    rstd = lax.rsqrt(jnp.mean(centred * centred, -1, keepdims=True) + EPS)
    return centred * rstd, rstd


def norm_back(grad, normed, rstd, gain):
    dn = grad * gain
    return rstd * (
        dn - jnp.mean(dn, -1, keepdims=True) - normed * jnp.mean(dn * normed, -1, keepdims=True)
    )


MESH = pl.DeviceIdType.MESH


def send(src, dst, sends, recvs, to):
    one = pltpu.make_async_remote_copy(
        src_ref=src, dst_ref=dst, send_sem=sends, recv_sem=recvs, device_id=to, device_id_type=MESH
    )
    one.start()
    return one


class Line:
    def __init__(self, step, own, prior, got, held, load, sends, recvs):
        self.step, self.own, self.prior, self.got, self.held = step, own, prior, got, held
        self.load, self.sends, self.recvs = load, sends, recvs
        self.last = own.shape[0] - 1
        self.seq, batch = lax.axis_index("seq"), lax.axis_index("batch")
        self.chip, self.core = batch // 2, lax.rem(batch, 2)

    def ready(self):
        self.got[...] = jnp.zeros_like(self.got)
        ahead = self.last - self.step
        wanted = jnp.minimum(self.chip + ahead, self.last), jnp.maximum(self.chip - ahead, 0)
        for way, chunk in enumerate(wanted):
            pltpu.make_async_copy(self.own.at[chunk], self.held.at[way], self.load.at[way]).start()

    def neighbours(self):
        count = self.last + 1
        return [(self.seq, 2 * lax.rem(self.chip + d, count) + self.core) for d in (1, count - 1)]

    def copy(self, way):
        to = jnp.minimum(self.chip + 1, self.last) if way == 0 else jnp.maximum(self.chip - 1, 0)
        return pltpu.make_async_remote_copy(
            src_ref=self.held.at[way],
            dst_ref=self.got.at[way],
            send_sem=self.sends.at[way],
            recv_sem=self.recvs.at[way],
            device_id=(self.seq, 2 * to + self.core),
            device_id_type=MESH,
        )

    def roles(self):
        chip, last, step = self.chip, self.last, self.step
        gives = chip <= step, chip >= last - step
        takes = (chip >= 1) & (chip <= step + 1), (chip <= last - 1) & (chip >= last - 1 - step)
        return gives, takes

    def go(self):
        for way in range(2):
            here = self.held.at[way]
            pltpu.make_async_copy(here, here, self.load.at[way]).wait()
            if self.prior is not None:
                total = self.held[way].astype(F32) + self.prior[way].astype(F32)
                self.held[way] = total.astype(BF)

            @pl.when(self.roles()[0][way])
            def _():
                self.copy(way).start()

    def stop(self):
        gives, takes = self.roles()
        for way in range(2):

            @pl.when(takes[way])
            def _():
                self.copy(way).wait_recv()

            @pl.when(gives[way])
            def _():
                self.copy(way).wait_send()


def line_scratch(rows, width):
    dma = pltpu.SemaphoreType.DMA
    return [pltpu.VMEM((2, rows, width), BF), dma((2,)), dma((2,)), dma((2,))]


def dot_t(left, right):
    return lax.dot_general(left, right, (((1,), (1,)), ((), ())), preferred_element_type=F32)


def t_dot(left, right):
    return lax.dot_general(left, right, (((0,), (0,)), ((), ())), preferred_element_type=F32)


def load_rows(ns, nb, depth, src, dst, sem):
    def one(k, carry):
        s, b = k // nb, lax.rem(k, nb)
        pltpu.make_async_copy(
            src.at[b, pl.ds(s * depth, depth), :], dst.at[pl.ds(k * depth, depth), :], sem
        ).start()
        return carry

    lax.fori_loop(0, ns * nb, one, 0)


def load_attention(ns, nb, packed, w, sem):
    share = packed.shape[2]
    depth = packed.shape[1] // (3 * ns)

    def one(k, carry):
        s, b = k // nb, lax.rem(k, nb)
        for t in range(3):
            pltpu.make_async_copy(
                packed.at[b, pl.ds((t * ns + s) * depth, depth), :],
                w.at[pl.ds(k * depth, depth), t * share : (t + 1) * share],
                sem,
            ).start()
        return carry

    lax.fori_loop(0, ns * nb, one, 0)


def load_second(nb, packed, w, sem):
    chunk, width = w.shape
    part, pieces, base = chunk // nb, width // chunk, width // nb

    def one(k, carry):
        for p in range(pieces):
            pltpu.make_async_copy(
                packed.at[k, pl.ds(base + p * part, part), :],
                w.at[pl.ds(k * part, part), p * chunk : (p + 1) * chunk],
                sem,
            ).start()
        return carry

    lax.fori_loop(0, nb, one, 0)


def soft_block(query, keys, block, first, length):
    rows, count = query.shape[0], keys.shape[0]
    scores = dot_t(query, keys) * HEAD_DIM ** (-0.5)
    query_pos = block * rows + lax.broadcasted_iota(jnp.int32, (rows, count), 0)
    key_pos = first + lax.broadcasted_iota(jnp.int32, (rows, count), 1)
    back = query_pos - key_pos
    valid = (back >= 0) & (back < WINDOW) & ((key_pos < length) | (back == 0))
    scores = jnp.where(valid, scores, -1e30)
    expo = jnp.exp(scores - jnp.max(scores, -1, keepdims=True))
    return expo / jnp.sum(expo, -1, keepdims=True)


def attend_kernel(ns, nb, length, h1, wq, bias, qkv, o, h1t, w, sem):
    tokens, width = h1.shape
    share = o.shape[1]
    rows = tokens // ns
    load_attention(ns, nb, wq, w, sem)
    for r in range(0, tokens, 256):
        h1t[:, r : r + 256] = h1[r : r + 256, :].T
    pltpu.make_async_copy(w, w, sem).wait()
    wide = min(512, 3 * share)

    def project(j, carry):
        cols = pl.ds(pl.multiple_of(j * wide, wide), wide)
        for r in range(0, tokens, 256):
            part = jnp.dot(h1[r : r + 256, :], w[:, cols], preferred_element_type=F32)
            qkv[r : r + 256, cols] = (part + bias[:, cols]).astype(BF)
        return carry

    lax.fori_loop(0, 3 * share // wide, project, 0)
    limit = length[0]

    def head(h, carry):
        at = h * HEAD_DIM
        col_q = pl.ds(pl.multiple_of(at, HEAD_DIM), HEAD_DIM)
        col_k = pl.ds(pl.multiple_of(share + at, HEAD_DIM), HEAD_DIM)
        col_v = pl.ds(pl.multiple_of(2 * share + at, HEAD_DIM), HEAD_DIM)
        for n in range(ns):
            first = max(n - 1, 0) * rows
            mine, seen = slice(n * rows, n * rows + rows), slice(first, first + 2 * rows)
            probs = soft_block(qkv[mine, col_q], qkv[seen, col_k], n, first, limit)
            part = jnp.dot(probs.astype(BF), qkv[seen, col_v], preferred_element_type=F32)
            o[mine, col_q] = part.astype(BF)
        return carry

    lax.fori_loop(0, share // HEAD_DIM, head, 0)


def attend(ns, nb, lengths, h1, wq, bias):
    tokens, width = h1.shape
    share = wq.shape[2]
    vm = pl.BlockSpec(memory_space=pltpu.VMEM)
    return pl.pallas_call(
        functools.partial(attend_kernel, ns, nb),
        out_shape=(
            jax.ShapeDtypeStruct((tokens, 3 * share), BF),
            jax.ShapeDtypeStruct((tokens, share), BF),
            jax.ShapeDtypeStruct((width, tokens), BF),
        ),
        in_specs=[pl.BlockSpec(memory_space=pltpu.SMEM), vm, pl.BlockSpec(memory_space=pl.ANY), vm],
        out_specs=(vm, vm, vm),
        scratch_shapes=[pltpu.VMEM((width, 3 * share), BF), pltpu.SemaphoreType.DMA],
        compiler_params=pltpu.CompilerParams(vmem_limit_bytes=56 * 2**20),
        cost_estimate=pl.CostEstimate(flops=10**6, bytes_accessed=10**4, transcendentals=0),
        name="attend",
    )(lengths, h1, wq, bias)


def upper_rows(rows):
    return 3 * rows // 4


def attend_back_kernel(ns, nb, moving, length, h1t_in, da, wout, o, qkv_in, *refs):
    line = None
    if moving:
        own, prior, g0_in, g1_in, wg0, wg1, pair, dproj, gqv, sums, branch_sum, *rest = refs
        do, gw, gwo, acc_k, acc_v, sems, h1t, qkv, g0, g1, near, to_twin, from_twin, *rest = rest
        out, via, from_x, from_y, s1, r1, got, *rest = rest
        line = Line(2, own, prior, got, *rest)
    else:
        packed, dproj, gqv, do, gw, gwo, acc_k, acc_v, sems, h1t, qkv = refs
    width, tokens = h1t.shape
    share = o.shape[1]
    rows = tokens // ns
    depth = width // (ns * nb)
    scale = HEAD_DIM ** (-0.5)
    limit = length[0]
    steps = None
    loads = [pltpu.make_async_copy(qkv_in, qkv, sems.at[4]), pltpu.make_async_copy(h1t_in, h1t, sems.at[5])]
    if moving:
        chunk = g0.shape[1]
        halves = gw.at[:chunk], gw.at[chunk:]
        line.ready()
        for k, (wg, src, dst) in enumerate(((wg0, g0_in, g0), (wg1, g1_in, g1))):
            loads.append(pltpu.make_async_copy(src, dst, sems.at[6 + k]))
            loads[-1].start()
            load_second(nb, wg, halves[k], sems.at[2 + k])
        loads[0].start()
        loads[1].start()
        chips = nb // 2
        twin = (line.seq, 2 * line.chip + 1 - line.core)
        place = greet([*line.neighbours(), twin])
        line.go()

        def strip(row, core):
            return pl.ds(pl.multiple_of((row + core) * depth, depth), depth)

        def exchange(t, source):
            for c in range(chips):
                for k in range(ns):
                    ref, row, cols = source(c, k)
                    there = near.at[c, (t * ns + k) * depth : (t * ns + k + 1) * depth]
                    send(ref.at[strip(row, 1 - line.core), cols], there, to_twin.at[t], from_twin.at[t], twin)

        def combine(t, source):
            got_piece = near.at[:, t * ns * depth : (t + 1) * ns * depth]
            whole = pltpu.make_async_remote_copy(
                src_ref=got_piece,
                dst_ref=got_piece,
                send_sem=to_twin.at[t],
                recv_sem=from_twin.at[t],
                device_id=twin,
                device_id_type=MESH,
            )
            whole.wait()
            for c in range(chips):
                for k in range(ns):
                    ref, row, cols = source(c, k)
                    here = slice((t * ns + k) * depth, (t * ns + k + 1) * depth)
                    total = ref[strip(row, line.core), cols].astype(F32) + near[c, here].astype(F32)
                    pair[c, here] = total.astype(BF)

        def piece_out(c, k):
            return gwo, 2 * c, slice(k * share, (k + 1) * share)

        def piece_qkv(t):
            return lambda c, k: (gw, k * nb + 2 * c, slice(t * share, (t + 1) * share))

        def branch(block):
            at = pl.ds(pl.multiple_of(block * rows, rows), upper_rows(rows))
            total = jnp.dot(g0[at, :], halves[0][...], preferred_element_type=F32)
            return total + jnp.dot(g1[at, :], halves[1][...], preferred_element_type=F32)

        steps = scatter_steps(branch, place, (out, via, from_x, from_y), s1, r1)
    else:
        loads[0].start()
        loads[1].start()
    for r in range(0, tokens, 256):
        do[r : r + 256, :] = dot_t(da[r : r + 256, :], wout[...]).astype(BF)
    ot = o[...].T
    for c in range(0, width, 512):
        gwo[:, c : c + 512] = jnp.dot(ot, da[:, c : c + 512], preferred_element_type=F32).astype(BF)

    def store_out(b, carry):
        for p in range(ns):
            pltpu.make_async_copy(
                gwo.at[pl.ds(b * depth, depth), p * share : (p + 1) * share],
                packed.at[b, (3 * ns + p) * depth : (3 * ns + p + 1) * depth, :],
                sems.at[0],
            ).start()
        return carry

    if not moving:
        lax.fori_loop(0, nb, store_out, 0)
    if moving:
        exchange(3, piece_out)
        for k in range(2):
            loads[2 + k].wait()
            pltpu.make_async_copy(halves[k], halves[k], sems.at[2 + k]).wait()
        for _ in range(3):
            next(steps)
    loads[0].wait()

    def head(h, carry):
        at = h * HEAD_DIM
        col_q = pl.ds(pl.multiple_of(at, HEAD_DIM), HEAD_DIM)
        col_k = pl.ds(pl.multiple_of(share + at, HEAD_DIM), HEAD_DIM)
        col_v = pl.ds(pl.multiple_of(2 * share + at, HEAD_DIM), HEAD_DIM)
        acc_k[...] = jnp.zeros_like(acc_k)
        acc_v[...] = jnp.zeros_like(acc_v)
        for n in range(ns):
            first = max(n - 1, 0) * rows
            mine, seen = slice(n * rows, n * rows + rows), slice(first, first + 2 * rows)
            query, keys, grad = qkv[mine, col_q], qkv[seen, col_k], do[mine, col_q]
            probs = soft_block(query, keys, n, first, limit)
            dp = dot_t(grad, qkv[seen, col_v])
            ds = (probs * (dp - jnp.sum(dp * probs, -1, keepdims=True))).astype(BF)
            dq = jnp.dot(ds, keys, preferred_element_type=F32) * scale
            dproj[mine, col_q] = dq.astype(BF)
            acc_k[seen, :] += t_dot(ds, query)
            acc_v[seen, :] += t_dot(probs.astype(BF), grad)
        dproj[:, col_k] = (acc_k[...] * scale).astype(BF)
        dproj[:, col_v] = acc_v[...].astype(BF)
        return carry

    lax.fori_loop(0, share // HEAD_DIM, head, 0)
    loads[1].wait()
    if moving:
        next(steps)
        next(steps)
    wide = min(512, 3 * share)

    def weights(j, carry):
        cols = pl.ds(pl.multiple_of(j * wide, wide), wide)
        gqv[:, cols] = jnp.sum(dproj[:, cols].astype(F32), 0, keepdims=True)
        for r in range(0, width, 512):
            gw[r : r + 512, cols] = jnp.dot(
                h1t[r : r + 512, :], dproj[:, cols], preferred_element_type=F32
            ).astype(BF)
        return carry

    if moving:
        for t in range(3):
            weights(t, 0)
            exchange(t, piece_qkv(t))
        combine(3, piece_out)
        size = upper_rows(rows) // 2
        for part, total in enumerate(next(steps)):
            branch_sum[part * size : (part + 1) * size, :] = total
        for t in range(3):
            combine(t, piece_qkv(t))
        line.stop()
        mine = pltpu.make_async_copy(own.at[line.chip], line.held.at[0], sems.at[2])
        mine.start()
        mine.wait()
        sums[...] = (line.held[0].astype(F32) + got[0].astype(F32) + got[1].astype(F32)).astype(BF)
        return
    lax.fori_loop(0, 3 * share // wide, weights, 0)

    def store(k, c):
        s, b = k // nb, lax.rem(k, nb)
        for t in range(3):
            pltpu.make_async_copy(
                gw.at[pl.ds(k * depth, depth), t * share : (t + 1) * share],
                packed.at[b, pl.ds((t * ns + s) * depth, depth), :],
                sems.at[1],
            ).start()
        return c

    lax.fori_loop(0, ns * nb, store, 0)
    pltpu.make_async_copy(gw, gw, sems.at[1]).wait()
    pltpu.make_async_copy(gwo, gwo, sems.at[0]).wait()


def attend_back(ns, nb, lengths, h1t, da, wout, o, qkv, *more):
    width, tokens = h1t.shape
    share = o.shape[1]
    rows = tokens // ns
    vm = pl.BlockSpec(memory_space=pltpu.VMEM)
    hbm = pl.BlockSpec(memory_space=pl.ANY)
    moving = len(more) > 0
    extra, scratch = (), []
    if moving:
        prior = more[1]
        extra = jax.ShapeDtypeStruct(prior.shape[1:], BF), jax.ShapeDtypeStruct((upper_rows(rows), width), F32)
        scratch = [pltpu.VMEM(one.shape, BF) for one in more[2:4]]
        scratch += [pltpu.VMEM((nb // 2, 4 * width // nb, share), BF)] + [pltpu.SemaphoreType.DMA((4,))] * 2
        scratch += scatter_scratch(upper_rows(rows), width) + [pltpu.VMEM(prior.shape, BF)] + line_scratch(*prior.shape[1:])
    return pl.pallas_call(
        functools.partial(attend_back_kernel, ns, nb, moving),
        out_shape=(
            jax.ShapeDtypeStruct((nb // 2 if moving else nb, 4 * width // nb, share), BF),
            jax.ShapeDtypeStruct((tokens, 3 * share), BF),
            jax.ShapeDtypeStruct((1, 3 * share), F32),
        )
        + extra,
        in_specs=[pl.BlockSpec(memory_space=pltpu.SMEM), hbm, vm, vm, vm, hbm] + [hbm, vm, hbm, hbm, hbm, hbm][: len(more)],
        out_specs=(vm if moving else hbm, vm, vm) + (vm,) * len(extra),
        scratch_shapes=[
            pltpu.VMEM((tokens, share), BF),
            pltpu.VMEM((width, width if moving else 3 * share), BF),
            pltpu.VMEM((share, width), BF),
            pltpu.VMEM((tokens, HEAD_DIM), F32),
            pltpu.VMEM((tokens, HEAD_DIM), F32),
            pltpu.SemaphoreType.DMA((8,)),
            pltpu.VMEM((width, tokens), BF),
            pltpu.VMEM((tokens, 3 * share), BF),
        ]
        + scratch,
        compiler_params=pltpu.CompilerParams(
            collective_id=9 if moving else None, has_side_effects=moving, vmem_limit_bytes=60 * 2**20
        ),
        cost_estimate=pl.CostEstimate(
            flops=40 * 10**9, bytes_accessed=12 * width * share, transcendentals=tokens * 512 * share // 128
        ),
        name="attend_back",
    )(lengths, h1t, da, wout, o, qkv, *more)


def slopes(u, dg):
    sq = u * u
    th = jnp.tanh(ROOT * u * (1.0 + 0.044715 * sq))
    cdf = 0.5 * (1.0 + th)
    slope = cdf + 0.5 * u * (1.0 - th * th) * (ROOT * (1.0 + 3.0 * 0.044715 * sq))
    return (u * cdf).astype(BF), (dg * slope).astype(BF)


def ff_first_kernel(ns, nb, h2, cot, wg, bias, own, g_out, du_out, gb, h2t, dh2, w1, w2, gw1, gw2, near2, near1, *sems):
    load, to2, from2, to1, from1 = sems
    tokens, width = h2.shape
    chunk = g_out.shape[1]
    depth = width // (ns * nb)
    part = chunk // nb
    pieces = width // chunk
    half = ns * depth
    chips = nb // 2
    tile = min(512, chunk)
    step = min(256, tokens)
    seq, batch = lax.axis_index("seq"), lax.axis_index("batch")
    chip, core = batch // 2, lax.rem(batch, 2)
    twin = (seq, 2 * chip + 1 - core)
    load_rows(ns, nb, depth, wg, w1, load.at[0])

    def load2(k, carry):
        for p in range(pieces):
            pltpu.make_async_copy(
                wg.at[k, pl.ds(half + p * part, part), :],
                w2.at[pl.ds(k * part, part), p * chunk : (p + 1) * chunk],
                load.at[1],
            ).start()
        return carry

    lax.fori_loop(0, nb, load2, 0)
    barrier = pltpu.get_barrier_semaphore()
    pl.semaphore_signal(barrier, inc=1, device_id=twin, device_id_type=MESH)
    for r in range(0, tokens, step):
        h2t[:, r : r + step] = h2[r : r + step, :].T
    pltpu.make_async_copy(w1, w1, load.at[0]).wait()
    pltpu.make_async_copy(w2, w2, load.at[1]).wait()

    def one_tile(j, carry):
        cols = pl.ds(pl.multiple_of(j * tile, tile), tile)
        total = jnp.zeros((1, tile), F32)
        for r in range(0, tokens, step):
            rows = slice(r, r + step)
            u = jnp.dot(h2[rows, :], w1[:, cols], preferred_element_type=F32) + bias[:, cols]
            g, du = slopes(u, dot_t(cot[rows, :], w2[cols, :]))
            g_out[rows, cols] = g
            du_out[rows, cols] = du
            total += jnp.sum(du.astype(F32), 0, keepdims=True)
        gb[:, cols] = total
        return carry

    lax.fori_loop(0, chunk // tile, one_tile, 0)

    def second(j, carry):
        cols = pl.ds(pl.multiple_of(j * tile, tile), tile)
        gt = g_out[:, cols].T
        for r in range(0, width, 512):
            gw2[cols, r : r + 512] = jnp.dot(gt, cot[:, r : r + 512], preferred_element_type=F32).astype(BF)
        return carry

    lax.fori_loop(0, chunk // tile, second, 0)
    pl.semaphore_wait(barrier, 1)

    def rows2(c, kept):
        return pl.ds(pl.multiple_of((2 * c + (core if kept else 1 - core)) * part, part), part)

    def rows1(c, s, kept):
        return pl.ds(pl.multiple_of((s * nb + 2 * c + (core if kept else 1 - core)) * depth, depth), depth)

    for c in range(chips):
        for p in range(pieces):
            span = slice(p * part, (p + 1) * part)
            send(gw2.at[rows2(c, False), p * chunk : (p + 1) * chunk], near2.at[c, span], to2, from2, twin)

    def first(j, carry):
        cols = pl.ds(pl.multiple_of(j * tile, tile), tile)
        for r in range(0, width, 512):
            gw1[r : r + 512, cols] = jnp.dot(
                h2t[r : r + 512, :], du_out[:, cols], preferred_element_type=F32
            ).astype(BF)
        return carry

    lax.fori_loop(0, chunk // tile, first, 0)
    for c in range(chips):
        for s in range(ns):
            send(gw1.at[rows1(c, s, False)], near1.at[c, s * depth : (s + 1) * depth], to1, from1, twin)

    def whole(near, send_sem, recv_sem):
        return pltpu.make_async_remote_copy(
            src_ref=near, dst_ref=near, send_sem=send_sem, recv_sem=recv_sem, device_id=twin, device_id_type=MESH
        )

    def back(k, carry):
        rows = pl.ds(pl.multiple_of(k * step, step), step)
        for c in range(0, width, 512):
            dh2[rows, c : c + 512] = dot_t(du_out[rows, :], w1[c : c + 512, :]).astype(BF)
        return carry

    lax.fori_loop(0, tokens // step, back, 0)
    whole(near2, to2, from2).wait_recv()
    for c in range(chips):
        for p in range(pieces):
            mine = gw2[rows2(c, True), p * chunk : (p + 1) * chunk]
            total = mine.astype(F32) + near2[c, p * part : (p + 1) * part].astype(F32)
            own[c, half + p * part : half + (p + 1) * part] = total.astype(BF)
    whole(near1, to1, from1).wait_recv()
    for c in range(chips):
        for s in range(ns):
            total = gw1[rows1(c, s, True), :].astype(F32) + near1[c, s * depth : (s + 1) * depth].astype(F32)
            own[c, s * depth : (s + 1) * depth] = total.astype(BF)
    whole(near2, to2, from2).wait_send()
    whole(near1, to1, from1).wait_send()


def ff_first(ns, nb, h2, cot, wg, bias):
    tokens, width = h2.shape
    chunk = wg.shape[2]
    half = width // nb
    vm = pl.BlockSpec(memory_space=pltpu.VMEM)
    dma = pltpu.SemaphoreType.DMA
    inner = jax.ShapeDtypeStruct((tokens, chunk), BF)
    near = pltpu.VMEM((nb // 2, half, chunk), BF)
    return pl.pallas_call(
        functools.partial(ff_first_kernel, ns, nb),
        out_shape=(
            jax.ShapeDtypeStruct((nb // 2, 2 * half, chunk), BF),
            inner,
            inner,
            jax.ShapeDtypeStruct((1, chunk), F32),
            jax.ShapeDtypeStruct((width, tokens), BF),
            jax.ShapeDtypeStruct((tokens, width), BF),
        ),
        in_specs=[vm, vm, pl.BlockSpec(memory_space=pl.ANY), vm],
        out_specs=(vm,) * 6,
        scratch_shapes=[
            pltpu.VMEM((width, chunk), BF),
            pltpu.VMEM((chunk, width), BF),
            pltpu.VMEM((width, chunk), BF),
            pltpu.VMEM((chunk, width), BF),
            near,
            near,
            dma((2,)),
            dma,
            dma,
            dma,
            dma,
        ],
        compiler_params=pltpu.CompilerParams(collective_id=7, has_side_effects=True, vmem_limit_bytes=60 * 2**20),
        cost_estimate=pl.CostEstimate(flops=40 * 10**9, bytes_accessed=8 * wg.size, transcendentals=tokens * chunk),
        name="ff_first",
    )(h2, cot, wg, bias)


def ff_kernel(ns, nb, first, moving, *refs):
    line = None
    if first:
        h2_in, cot_in, wg, bias, gwg, g_out, du_out, gb, h2t, dh2, w1, w2, gw1, gw2, h2, cot, u_part, sems = refs
    elif moving:
        h2_in, h2t_in, cot_in, wg, bias, own, gwg, g_out, du_out, gb, got, *refs = refs
        w1, w2, gw1, gw2, h2, cot, u_part, sems, h2t, held, s0, s1, s2 = refs
        line = Line(0, own, None, got, held, s0, s1, s2)
    else:
        h2_in, h2t_in, cot_in, wg, bias, gwg, g_out, du_out, gb, *refs = refs
        w1, w2, gw1, gw2, h2, cot, u_part, sems, h2t = refs
    tokens, width = h2_in.shape
    chunk = g_out.shape[1]
    depth = width // (ns * nb)
    part = chunk // nb
    pieces = width // chunk
    half = ns * depth
    tile = min(512, chunk)
    tiles = chunk // tile
    step = min(256, tokens)

    def load1(k, carry):
        s, b = k // nb, lax.rem(k, nb)
        pltpu.make_async_copy(
            wg.at[b, pl.ds(s * depth, depth), :], w1.at[pl.ds(k * depth, depth), :], sems.at[0]
        ).start()
        return carry

    def load2(k, carry):
        for p in range(pieces):
            pltpu.make_async_copy(
                wg.at[k, pl.ds(half + p * part, part), :],
                w2.at[pl.ds(k * part, part), p * chunk : (p + 1) * chunk],
                sems.at[1],
            ).start()
        return carry

    first_load = pltpu.make_async_copy(h2_in, h2, sems.at[4])
    first_load.start()
    lax.fori_loop(0, ns * nb, load1, 0)
    second_load = pltpu.make_async_copy(cot_in, cot, sems.at[5])
    second_load.start()
    lax.fori_loop(0, nb, load2, 0)
    if not first:
        third_load = pltpu.make_async_copy(h2t_in, h2t, sems.at[6])
        third_load.start()
    if moving:
        line.ready()
        barrier = pltpu.get_barrier_semaphore()
        for other in line.neighbours():
            pl.semaphore_signal(barrier, inc=1, device_id=other, device_id_type=MESH)
        pl.semaphore_wait(barrier, 2)
        line.go()
    first_load.wait()
    if first:
        for r in range(0, tokens, step):
            h2t[:, r : r + step] = h2[r : r + step, :].T
    pltpu.make_async_copy(w1, w1, sems.at[0]).wait()

    def one_tile(j, carry):
        at = pl.multiple_of(j * tile, tile)
        cols = pl.ds(at, tile)
        total = jnp.zeros((1, tile), F32)
        for r in range(0, tokens, step):
            rows = slice(r, r + step)
            u_part[rows, :] = jnp.dot(h2[rows, :], w1[:, cols], preferred_element_type=F32) + bias[:, cols]

        @pl.when(j == 0)
        def _():
            second_load.wait()
            pltpu.make_async_copy(w2, w2, sems.at[1]).wait()
            if not first:
                third_load.wait()

        for r in range(0, tokens, step):
            rows = slice(r, r + step)
            g, du = slopes(u_part[rows, :], dot_t(cot[rows, :], w2[cols, :]))
            g_out[rows, cols] = g
            du_out[rows, cols] = du
            total += jnp.sum(du.astype(F32), 0, keepdims=True)
        gb[:, cols] = total
        for r in range(0, width, 512):
            gw1[j, r : r + 512, :] = jnp.dot(
                h2t[r : r + 512, :], du_out[:, cols], preferred_element_type=F32
            ).astype(BF)
        gt = g_out[:, cols].T
        for r in range(0, width, 512):
            gw2[j, :, r : r + 512] = jnp.dot(
                gt, cot[:, r : r + 512], preferred_element_type=F32
            ).astype(BF)

        def store1(k, c):
            s, b = k // nb, lax.rem(k, nb)
            pltpu.make_async_copy(
                gw1.at[j, pl.ds(k * depth, depth), :],
                gwg.at[b, pl.ds(s * depth, depth), cols],
                sems.at[2],
            ).start()
            return c

        lax.fori_loop(0, ns * nb, store1, 0)
        count = tile // part

        def store2(k, c):
            for p in range(pieces):
                pltpu.make_async_copy(
                    gw2.at[j, pl.ds(k * part, part), p * chunk : (p + 1) * chunk],
                    gwg.at[j * count + k, pl.ds(half + p * part, part), :],
                    sems.at[3],
                ).start()
            return c

        lax.fori_loop(0, count, store2, 0)
        return carry

    lax.fori_loop(0, tiles, one_tile, 0)
    if first:
        for r in range(0, tokens, step):
            for c in range(0, width, 512):
                part_sum = dot_t(du_out[r : r + step, :], w1[c : c + 512, :])
                dh2[r : r + step, c : c + 512] = part_sum.astype(BF)
    pltpu.make_async_copy(gw1, gw1, sems.at[2]).wait()
    pltpu.make_async_copy(gw2, gw2, sems.at[3]).wait()
    if moving:
        line.stop()


def ff_chunk(ns, nb, h2, h2t, cot, wg, bias, own=None):
    tokens, width = h2.shape
    chunk = wg.shape[2]
    tile = min(512, chunk)
    first = h2t is None
    vm = pl.BlockSpec(memory_space=pltpu.VMEM)
    hbm = pl.BlockSpec(memory_space=pl.ANY)
    inner = jax.ShapeDtypeStruct((tokens, chunk), BF)
    extra = (jax.ShapeDtypeStruct((width, tokens), BF), jax.ShapeDtypeStruct((tokens, width), BF)) if first else ()
    given = (h2, cot, wg, bias) if first else (h2, h2t, cot, wg, bias)
    moving = own is not None
    more = []
    if moving:
        given += (own,)
        extra = (jax.ShapeDtypeStruct((2,) + own.shape[1:], BF),)
        more = line_scratch(*own.shape[1:])
    if not first:
        more = [pltpu.VMEM((width, tokens), BF)] + more
    return pl.pallas_call(
        functools.partial(ff_kernel, ns, nb, first, moving),
        out_shape=(jax.ShapeDtypeStruct(wg.shape, BF), inner, inner, jax.ShapeDtypeStruct((1, chunk), F32)) + extra,
        in_specs=[vm if one is bias else hbm for one in given],
        out_specs=(hbm,) + (vm,) * (3 + len(extra)),
        scratch_shapes=[
            pltpu.VMEM((width, chunk), BF),
            pltpu.VMEM((chunk, width), BF),
            pltpu.VMEM((chunk // tile, width, tile), BF),
            pltpu.VMEM((chunk // tile, tile, width), BF),
            pltpu.VMEM((tokens, width), BF),
            pltpu.VMEM((tokens, width), BF),
            pltpu.VMEM((tokens, tile), F32),
            pltpu.SemaphoreType.DMA((7,)),
        ]
        + more,
        compiler_params=pltpu.CompilerParams(
            collective_id=4 if moving else None, has_side_effects=moving, vmem_limit_bytes=60 * 2**20
        ),
        cost_estimate=pl.CostEstimate(
            flops=40 * 10**9,
            bytes_accessed=4 * wg.size,
            transcendentals=tokens * chunk,
        ),
        name="ff_chunk",
    )(*given)


def greet(more=()):
    me, batch = lax.axis_index("seq"), lax.axis_index("batch")
    by_x = me + 1 - 2 * lax.rem(me, 2)
    by_y = lax.rem(me + 2, 4)
    barrier = pltpu.get_barrier_semaphore()
    for other in [(by_x, batch), (by_y, batch), *more]:
        pl.semaphore_signal(barrier, inc=1, device_id=other, device_id_type=MESH)
    pl.semaphore_wait(barrier, 2 + len(more))
    return me, by_x, by_y, (by_x, batch), (by_y, batch)


def scatter_steps(partial, place, buffers, send, recv):
    me, by_x, by_y, to_x, to_y = place
    out, via, from_x, from_y = buffers
    half = via.shape[1]
    top, low = slice(0, half), slice(half, 2 * half)
    far = 3 - me

    def copy(k, src, dst, to):
        one = pltpu.make_async_remote_copy(
            src_ref=src, dst_ref=dst, send_sem=send.at[k], recv_sem=recv.at[k], device_id=to, device_id_type=MESH
        )
        one.start()
        return one

    out[0] = partial(far).astype(BF)
    c0 = copy(0, out.at[0, top], via.at[0], to_y)
    c1 = copy(1, out.at[0, low], via.at[1], to_x)
    yield
    block = partial(by_x)
    out[1, low] = block[low].astype(BF)
    c2 = copy(2, out.at[1, low], from_x.at[low], to_x)
    x_top = block[top]
    yield
    block = partial(by_y)
    out[2, top] = block[top].astype(BF)
    c3 = copy(3, out.at[2, top], from_y.at[top], to_y)
    y_low = block[low]
    yield
    c0.wait_recv()
    out[1, top] = (x_top + via[0].astype(F32)).astype(BF)
    c4 = copy(4, out.at[1, top], from_x.at[top], to_x)
    c1.wait_recv()
    out[2, low] = (y_low + via[1].astype(F32)).astype(BF)
    c5 = copy(5, out.at[2, low], from_y.at[low], to_y)
    yield
    mine = partial(me)
    yield
    c3.wait_recv()
    c4.wait_recv()
    mine_top = mine[top] + from_x[top].astype(F32) + from_y[top].astype(F32)
    c2.wait_recv()
    c5.wait_recv()
    mine_low = mine[low] + from_x[low].astype(F32) + from_y[low].astype(F32)
    for one in (c0, c1, c2, c3, c4, c5):
        one.wait_send()
    yield mine_top, mine_low


def scatter_sum(partial, place, buffers, send, recv):
    return list(scatter_steps(partial, place, buffers, send, recv))[-1]


def scatter_scratch(rows, width):
    return [
        pltpu.VMEM((3, rows, width), BF),
        pltpu.VMEM((2, rows // 2, width), BF),
        pltpu.VMEM((rows, width), BF),
        pltpu.VMEM((rows, width), BF),
        pltpu.SemaphoreType.DMA((6,)),
        pltpu.SemaphoreType.DMA((6,)),
    ]


def gather_steps(full, rows, place, send_sems, recv_sems):
    me, by_x, by_y, to_x, to_y = place
    half = rows // 2

    def copy(k, block, part, to):
        at = full.at[pl.ds(pl.multiple_of(block * rows + part * half, half), half)]
        return send(at, at, send_sems.at[k], recv_sems.at[k], to)

    c0 = copy(0, me, 0, to_x)
    c3 = copy(3, me, 1, to_y)
    c2 = copy(2, me, 0, to_y)
    c1 = copy(1, me, 1, to_x)
    yield
    c0.wait_recv()
    c4 = copy(4, by_x, 0, to_y)
    c3.wait_recv()
    c5 = copy(5, by_y, 1, to_x)
    yield
    for one in (c1, c2, c4, c5):
        one.wait_recv()
    for one in (c0, c1, c2, c3, c4, c5):
        one.wait_send()


def gather_blocks(full, rows, place, send_sems, recv_sems):
    for _ in gather_steps(full, rows, place, send_sems, recv_sems):
        pass


GATHER_SEMS = [pltpu.SemaphoreType.DMA((6,)), pltpu.SemaphoreType.DMA((6,))]


def middle_kernel(o, wout, mine, obias, gain, shift, x1, h2, out, via, from_x, from_y, s1, r1, s2, r2):
    rows, width = mine.shape
    half = rows // 2
    place = greet()

    def partial(block):
        at = pl.multiple_of(block * rows, rows)
        return jnp.dot(o[pl.ds(at, rows), :], wout[...], preferred_element_type=F32)

    sums = scatter_sum(partial, place, (out, via, from_x, from_y), s1, r1)
    for part, total in enumerate(sums):
        span = slice(part * half, part * half + half)
        res = mine[span, :].astype(F32) + (total + obias[...])
        x1[span, :] = res
        normed, _ = norm_stats(res)
        at = pl.multiple_of(place[0] * rows + part * half, half)
        h2[pl.ds(at, half), :] = (normed * gain[...] + shift[...]).astype(BF)
    gather_blocks(h2, rows, place, s2, r2)


def middle(o, wout, mine, obias, gain, shift):
    tokens = o.shape[0]
    rows, width = mine.shape
    vm = pl.BlockSpec(memory_space=pltpu.VMEM)
    return pl.pallas_call(
        middle_kernel,
        out_shape=(jax.ShapeDtypeStruct((rows, width), F32), jax.ShapeDtypeStruct((tokens, width), BF)),
        in_specs=[vm] * 6,
        out_specs=(vm, vm),
        scratch_shapes=scatter_scratch(rows, width) + GATHER_SEMS,
        compiler_params=pltpu.CompilerParams(collective_id=1, has_side_effects=True, vmem_limit_bytes=56 * 2**20),
        cost_estimate=pl.CostEstimate(flops=40 * 10**9, bytes_accessed=12 * tokens * width, transcendentals=0),
        name="project_out",
    )(o, wout, mine, obias, gain, shift)


def ff_back_kernel(ns, nb, du, wg, before_in, x1_in, cot_in, gain, own, prior, *refs):
    dx1, da, sums, got, before, x1, cot, loads, w, load_sem, out, via, from_x, from_y, s1, r1, s2, r2, *moving = refs
    line = Line(1, own, prior, got, *moving)
    rows, width = x1.shape
    half = rows // 2
    load_rows(ns, nb, width // (ns * nb), wg, w, load_sem)
    pairs = (before_in, before), (x1_in, x1), (cot_in, cot)
    copies = [pltpu.make_async_copy(src, dst, loads.at[k]) for k, (src, dst) in enumerate(pairs)]
    for one in copies:
        one.start()
    line.ready()
    place = greet(line.neighbours())
    pltpu.make_async_copy(w, w, load_sem).wait()
    copies[0].wait()

    def partial(block):
        at = pl.multiple_of(block * rows, rows)
        return before[pl.ds(at, rows), :].astype(F32) + dot_t(du[pl.ds(at, rows), :], w[...])

    steps = scatter_steps(partial, place, (out, via, from_x, from_y), s1, r1)
    next(steps)
    line.go()
    *_, halves = steps
    copies[1].wait()
    copies[2].wait()
    totals = [jnp.zeros((1, width), F32)] * 3
    for part, grad in enumerate(halves):
        span = slice(part * half, part * half + half)
        normed, rstd = norm_stats(x1[span, :])
        res = cot[span, :].astype(F32) + norm_back(grad, normed, rstd, gain[...])
        dx1[span, :] = res
        low = res.astype(BF)
        at = pl.multiple_of(place[0] * rows + part * half, half)
        da[pl.ds(at, half), :] = low
        for k, term in enumerate((low.astype(F32), grad * normed, grad)):
            totals[k] += jnp.sum(term, 0, keepdims=True)
    gather = gather_steps(da, rows, place, s2, r2)
    next(gather)
    for k in range(3):
        sums[k : k + 1, :] = totals[k]
    for _ in gather:
        pass
    line.stop()


def ff_back(ns, nb, du, wg, before, x1, cot, gain, own, prior):
    rows, width = x1.shape
    tokens, chunk = du.shape
    vm = pl.BlockSpec(memory_space=pltpu.VMEM)
    hbm = pl.BlockSpec(memory_space=pl.ANY)
    return pl.pallas_call(
        functools.partial(ff_back_kernel, ns, nb),
        out_shape=(
            jax.ShapeDtypeStruct((rows, width), F32),
            jax.ShapeDtypeStruct((tokens, width), BF),
            jax.ShapeDtypeStruct((3, width), F32),
            jax.ShapeDtypeStruct(prior.shape, BF),
        ),
        in_specs=[vm] + [hbm] * 4 + [vm, hbm, vm],
        out_specs=(vm,) * 4,
        scratch_shapes=[pltpu.VMEM(before.shape, BF), pltpu.VMEM((rows, width), F32), pltpu.VMEM((rows, width), BF)]
        + [pltpu.SemaphoreType.DMA((3,)), pltpu.VMEM((width, chunk), BF), pltpu.SemaphoreType.DMA]
        + scatter_scratch(rows, width)
        + GATHER_SEMS
        + line_scratch(*prior.shape[1:]),
        compiler_params=pltpu.CompilerParams(collective_id=2, has_side_effects=True, vmem_limit_bytes=56 * 2**20),
        cost_estimate=pl.CostEstimate(flops=40 * 10**9, bytes_accessed=12 * tokens * width, transcendentals=0),
        name="ff_back",
    )(du, wg, before, x1, cot, gain, own, prior)


def finish_kernel(ns, nb, count, dproj, wq, *refs):
    summed, gs, wgs = refs[:count], refs[count : 2 * count], refs[2 * count : 3 * count]
    mine, gain, part_grad, gains, stage, gw2, low_sum, w = refs[3 * count : 3 * count + 8]
    ws = refs[3 * count + 8 : 4 * count + 8]
    load, s0, r0, *buffers = refs[4 * count + 8 :]
    buffers, more = buffers[:6], buffers[6:]
    rows, width = mine.shape
    half, cut = rows // 2, upper_rows(rows)
    chunk = summed[0].shape[1]
    part_rows, pieces = chunk // nb, width // chunk
    load_attention(ns, nb, wq, w, load.at[0])
    for c in range(count):
        load_second(nb, wgs[c], ws[c], load.at[3 + c])
    me, others, met = greet_seq(ns)
    by_x, by_y, batch = me + 1 - 2 * lax.rem(me, 2), lax.rem(me + 2, 4), lax.axis_index("batch")
    place = me, by_x, by_y, (by_x, batch), (by_y, batch)
    depth, hidden = stage.shape[0], stage.shape[1] // ns

    def ship(b, carry):
        for c in range(count):
            cols = pl.ds(pl.multiple_of(me * hidden + (b * count + c) * part_rows, part_rows), part_rows)
            from_cols = pl.ds(pl.multiple_of(b * part_rows, part_rows), part_rows)
            own = pl.ds(pl.multiple_of(me * depth, depth), depth)
            pltpu.make_async_copy(summed[c].at[own, from_cols], stage.at[:, cols], load.at[1]).start()
            for d, to in enumerate(others):
                theirs = pl.ds(pl.multiple_of(to[0] * depth, depth), depth)
                send(summed[c].at[theirs, from_cols], stage.at[:, cols], s0.at[d], r0.at[d], to)
        return carry

    for c in range(count):
        for p in range(pieces):
            pltpu.make_async_copy(
                summed[c].at[ns * depth + p * part_rows : ns * depth + (p + 1) * part_rows],
                gw2.at[c * part_rows : (c + 1) * part_rows, p * chunk : (p + 1) * chunk],
                load.at[2],
            ).start()

    def input_grad(block):
        at = pl.multiple_of(block * rows, rows)
        return dot_t(dproj[pl.ds(at, rows), :], w[...])

    def branch(block):
        at = pl.ds(pl.multiple_of(block * rows + cut, rows - cut), rows - cut)
        total = jnp.dot(gs[0][at, :], ws[0][...], preferred_element_type=F32)
        for c in range(1, count):
            total += jnp.dot(gs[c][at, :], ws[c][...], preferred_element_type=F32)
        return total

    met()
    pltpu.make_async_copy(w, w, load.at[0]).wait()
    steps = scatter_steps(input_grad, place, buffers[:4], *buffers[4:])
    for _ in range(3):
        next(steps)
    for c in range(count):
        pltpu.make_async_copy(ws[c], ws[c], load.at[3 + c]).wait()
    others_steps = scatter_steps(branch, place, more[:4], *more[4:])
    next(others_steps)
    next(steps)
    next(others_steps)
    next(others_steps)
    lax.fori_loop(0, nb, ship, 0)
    *_, sums = steps
    totals = [jnp.zeros((1, width), F32)] * 2
    for part, grad in enumerate(sums):
        span = slice(part * half, part * half + half)
        normed, rstd = norm_stats(mine[span, :].astype(F32))
        part_grad[span, :] = norm_back(grad, normed, rstd, gain[...])
        for k, term in enumerate((grad * normed, grad)):
            totals[k] += jnp.sum(term, 0, keepdims=True)
    for k in range(2):
        gains[k : k + 1, :] = totals[k]
    *_, lows = others_steps
    for part, total in enumerate(lows):
        size = (rows - cut) // 2
        low_sum[part * size : (part + 1) * size, :] = total
    pltpu.make_async_copy(gw2, gw2, load.at[2]).wait()
    strip = stage.at[:, :hidden]
    pltpu.make_async_copy(strip, strip, load.at[1]).wait()
    for d, to in enumerate(others):
        pltpu.make_async_remote_copy(
            src_ref=strip, dst_ref=strip, send_sem=s0.at[d], recv_sem=r0.at[d], device_id=to, device_id_type=MESH
        ).wait()


def finish(ns, nb, dproj, wq, summed, gs, wgs, mine, gain):
    rows, width = mine.shape
    count, chunk = len(summed), summed[0].shape[1]
    depth, hidden = width // (ns * nb), count * chunk
    vm = pl.BlockSpec(memory_space=pltpu.VMEM)
    hbm = pl.BlockSpec(memory_space=pl.ANY)
    dma = pltpu.SemaphoreType.DMA
    return pl.pallas_call(
        functools.partial(finish_kernel, ns, nb, count),
        out_shape=(
            jax.ShapeDtypeStruct((rows, width), F32),
            jax.ShapeDtypeStruct((2, width), F32),
            jax.ShapeDtypeStruct((depth, hidden * ns), BF),
            jax.ShapeDtypeStruct((hidden // nb, width), BF),
            jax.ShapeDtypeStruct((rows - upper_rows(rows), width), F32),
        ),
        in_specs=[vm, hbm] + [hbm] * count + [vm] * count + [hbm] * count + [vm] * 2,
        out_specs=(vm,) * 5,
        scratch_shapes=[pltpu.VMEM((width, dproj.shape[1]), BF)]
        + [pltpu.VMEM((chunk, width), BF)] * count
        + [dma((3 + count,)), dma((ns - 1,)), dma((ns - 1,))]
        + scatter_scratch(rows, width)
        + scatter_scratch(rows - upper_rows(rows), width),
        compiler_params=pltpu.CompilerParams(collective_id=3, has_side_effects=True, vmem_limit_bytes=56 * 2**20),
        cost_estimate=pl.CostEstimate(flops=40 * 10**9, bytes_accessed=24 * rows * width, transcendentals=0),
        name="finish",
    )(dproj, wq, *summed, *gs, *wgs, mine, gain)


def greet_all(ns, nb):
    me, batch = lax.axis_index("seq"), lax.axis_index("batch")
    along_seq = [(lax.rem(me + d, ns), batch) for d in range(1, ns)]
    along_batch = [(me, lax.rem(batch + d, nb)) for d in range(1, nb)]
    barrier = pltpu.get_barrier_semaphore()
    for other in along_seq + along_batch:
        pl.semaphore_signal(barrier, inc=1, device_id=other, device_id_type=MESH)
    pl.semaphore_wait(barrier, ns + nb - 2)
    return me, batch, along_seq, along_batch


def greet_seq(ns, more=()):
    me, batch = lax.axis_index("seq"), lax.axis_index("batch")
    others = [(lax.rem(me + d, ns), batch) for d in range(1, ns)]
    barrier = pltpu.get_barrier_semaphore()
    for other in [*others, *more]:
        pl.semaphore_signal(barrier, inc=1, device_id=other, device_id_type=MESH)
    return me, others, lambda: pl.semaphore_wait(barrier, ns - 1 + len(more))


def spread_kernel(ns, w_qkv, qkv, local, s0, r0):
    depth = w_qkv.shape[0]
    share = qkv.shape[1]
    width = ns * share
    me, others, met = greet_seq(ns)
    copies = []
    for t in range(3):
        cols = pl.ds(pl.multiple_of(t * width + me * share, share), share)
        rows = pl.ds(pl.multiple_of((t * ns + me) * depth, depth), depth)
        one = pltpu.make_async_copy(w_qkv.at[:, cols], qkv.at[rows], local.at[t])
        one.start()
        copies.append(one)
    met()
    for t in range(3):
        rows = pl.ds(pl.multiple_of((t * ns + me) * depth, depth), depth)
        for d, to in enumerate(others):
            cols = pl.ds(pl.multiple_of(t * width + to[0] * share, share), share)
            copies.append(send(w_qkv.at[:, cols], qkv.at[rows], s0.at[t, d], r0.at[t, d], to))
    for one in copies:
        one.wait()


def spread(ns, w_qkv):
    depth, width = w_qkv.shape[0], w_qkv.shape[1] // 3
    hbm = pl.BlockSpec(memory_space=pl.ANY)
    dma = pltpu.SemaphoreType.DMA
    return pl.pallas_call(
        functools.partial(spread_kernel, ns),
        out_shape=jax.ShapeDtypeStruct((3 * ns * depth, width // ns), BF),
        in_specs=[hbm],
        out_specs=hbm,
        scratch_shapes=[dma((3,)), dma((3, ns - 1)), dma((3, ns - 1))],
        compiler_params=pltpu.CompilerParams(collective_id=5, has_side_effects=True),
        cost_estimate=pl.CostEstimate(flops=10**6, bytes_accessed=10**4, transcendentals=0),
        name="spread",
    )(w_qkv)


def spread_ff_kernel(ns, nb, parts, w1, w2, *refs):
    packs, (stage, local, s1, r1) = refs[:parts], refs[parts:]
    depth, rows2, width = w1.shape[0], w2.shape[0], w2.shape[1]
    hidden = w1.shape[1] // ns
    part, chunk = rows2 // parts, hidden // parts
    pieces = width // chunk
    me, others, met = greet_seq(ns)
    at = pl.ds(pl.multiple_of(me * depth, depth), depth)
    cols = pl.ds(pl.multiple_of(me * hidden, hidden), hidden)
    own = pltpu.make_async_copy(w1.at[:, cols], stage.at[at], local)
    own.start()
    met()
    copies = [own]
    for d, to in enumerate(others):
        cols = pl.ds(pl.multiple_of(to[0] * hidden, hidden), hidden)
        copies.append(send(w1.at[:, cols], stage.at[at], s1.at[d], r1.at[d], to))
    for c in range(parts):
        for p in range(pieces):
            span = slice(ns * depth + p * part, ns * depth + (p + 1) * part)
            packs[c][span, :] = w2[c * part : (c + 1) * part, p * chunk : (p + 1) * chunk]
    for one in copies:
        one.wait()
    for c in range(parts):
        for b in range(nb):
            source = (b * parts + c) * part
            packs[c][: ns * depth, b * part : (b + 1) * part] = stage[:, source : source + part]


def spread_ff(ns, nb, parts, w1, w2):
    depth, hidden = w1.shape[0], w1.shape[1] // ns
    vm = pl.BlockSpec(memory_space=pltpu.VMEM)
    dma = pltpu.SemaphoreType.DMA
    pack = jax.ShapeDtypeStruct((2 * ns * depth, hidden // parts), BF)
    return pl.pallas_call(
        functools.partial(spread_ff_kernel, ns, nb, parts),
        out_shape=(pack,) * parts,
        in_specs=[pl.BlockSpec(memory_space=pl.ANY), vm],
        out_specs=(vm,) * parts,
        scratch_shapes=[pltpu.VMEM((ns * depth, hidden), BF), dma, dma((ns - 1,)), dma((ns - 1,))],
        compiler_params=pltpu.CompilerParams(collective_id=11, has_side_effects=True),
        cost_estimate=pl.CostEstimate(flops=10**6, bytes_accessed=10**4, transcendentals=0),
        name="spread_ff",
    )(w1, w2)


def whole_row(ns, nb, vecs, row, width):
    pieces = jnp.concatenate([vecs[b, s, row : row + 1, :] for b in range(nb) for s in range(ns)], 0)
    lanes = jnp.concatenate([pieces] * (width // pieces.shape[1]), 1)
    owner = lax.broadcasted_iota(jnp.int32, lanes.shape, 0)
    owner = lax.rem(owner, ns) * nb + owner // ns
    place = lax.broadcasted_iota(jnp.int32, lanes.shape, 1) // (width // (ns * nb))
    return jnp.sum(jnp.where(owner == place, lanes, 0.0), 0, keepdims=True)


def collect_kernel(ns, nb, mine, cot, vec, h1, cots, vecs, acts, local, s1, r1, s2, r2, s3, r3, s4, r4):
    rows, width = mine.shape
    half = rows // 2
    me, batch = lax.axis_index("seq"), lax.axis_index("batch")
    by_x = me + 1 - 2 * lax.rem(me, 2)
    by_y = lax.rem(me + 2, 4)
    others = [(lax.rem(me + d, ns), batch) for d in range(1, ns)]
    column = [(me, lax.rem(batch + d, nb)) for d in range(1, nb)]
    barrier = pltpu.get_barrier_semaphore()
    for other in others + column:
        pl.semaphore_signal(barrier, inc=1, device_id=other, device_id_type=MESH)
    vecs[batch, me] = vec[...]
    at_me = pl.ds(pl.multiple_of(me * rows, rows), rows)
    acts[at_me, :] = mine[...]
    own = pltpu.make_async_copy(cot, cots.at[at_me], local)
    own.start()
    pl.semaphore_wait(barrier, ns + nb - 2)
    to_x, to_y = (by_x, batch), (by_y, batch)
    small = vecs.at[batch, me]
    near = [send(small, small, s3.at[d], r3.at[d], to) for d, to in enumerate(others)]

    def normalise(block):
        span = pl.ds(pl.multiple_of(block * rows, rows), rows)
        normed, _ = norm_stats(acts[span, :].astype(F32))
        h1[span, :] = (normed * gain + shift).astype(BF)

    def copy(k, full, block, side, to, sends, recvs):
        span = full.at[pl.ds(pl.multiple_of(block * rows + side * half, half), half)]
        return send(span, span, sends.at[k], recvs.at[k], to)

    c0 = copy(0, acts, me, 0, to_x, s1, r1)
    c3 = copy(3, acts, me, 1, to_y, s1, r1)
    c2 = copy(2, acts, me, 0, to_y, s1, r1)
    c1 = copy(1, acts, me, 1, to_x, s1, r1)
    for one in near:
        one.wait_recv()
    row = vecs.at[batch]
    wide = [send(row, row, s4.at[d], r4.at[d], to) for d, to in enumerate(column)]
    for one in wide:
        one.wait_recv()
    gain, shift = whole_row(ns, nb, vecs, 0, width), whole_row(ns, nb, vecs, 1, width)
    normalise(me)
    c0.wait_recv()
    c4 = copy(4, acts, by_x, 0, to_y, s1, r1)
    c3.wait_recv()
    c5 = copy(5, acts, by_y, 1, to_x, s1, r1)
    own.wait()
    d0 = copy(0, cots, me, 0, to_x, s2, r2)
    d3 = copy(3, cots, me, 1, to_y, s2, r2)
    d2 = copy(2, cots, me, 0, to_y, s2, r2)
    d1 = copy(1, cots, me, 1, to_x, s2, r2)
    c1.wait_recv()
    normalise(by_x)
    c2.wait_recv()
    normalise(by_y)
    c4.wait_recv()
    c5.wait_recv()
    normalise(3 - me)
    d0.wait_recv()
    d4 = copy(4, cots, by_x, 0, to_y, s2, r2)
    d3.wait_recv()
    d5 = copy(5, cots, by_y, 1, to_x, s2, r2)
    for one in (d1, d2, d4, d5):
        one.wait_recv()
    for one in (c0, c1, c2, c3, c4, c5, d0, d1, d2, d3, d4, d5, *near, *wide):
        one.wait_send()


def collect(ns, nb, mine, cot, vec):
    rows, width = mine.shape
    vm = pl.BlockSpec(memory_space=pltpu.VMEM)
    hbm = pl.BlockSpec(memory_space=pl.ANY)
    dma = pltpu.SemaphoreType.DMA
    full = jax.ShapeDtypeStruct((ns * rows, width), BF)
    return pl.pallas_call(
        functools.partial(collect_kernel, ns, nb),
        out_shape=(full, full, jax.ShapeDtypeStruct((nb, ns) + vec.shape, F32)),
        in_specs=[vm, hbm, vm],
        out_specs=(vm, hbm, vm),
        scratch_shapes=[pltpu.VMEM((ns * rows, width), BF), dma]
        + [dma((6,))] * 4
        + [dma((ns - 1,))] * 2
        + [dma((nb - 1,))] * 2,
        compiler_params=pltpu.CompilerParams(collective_id=6, has_side_effects=True, vmem_limit_bytes=40 * 2**20),
        cost_estimate=pl.CostEstimate(flops=10**6, bytes_accessed=10**4, transcendentals=0),
        name="collect",
    )(mine, cot, vec)


def home_kernel(ns, nb, summed, sums, gqkv, gout, small, stage, near, mid, far, local, s0, r0, s1, r1, s2, r2):
    depth, width = gout.shape
    share = width // ns
    me, batch, others, column = greet_all(ns, nb)
    first = [send(sums.at[to[1]], near.at[d], s1.at[d], r1.at[d], to) for d, to in enumerate(column)]
    copies = []
    for t in range(3):
        cols = pl.ds(pl.multiple_of(t * width + me * share, share), share)
        for d, to in enumerate(others):
            rows = pl.ds(pl.multiple_of((t * ns + to[0]) * depth, depth), depth)
            copies.append(send(summed.at[rows], stage.at[:, cols], s0.at[t, d], r0.at[t, d], to))
        rows = pl.ds(pl.multiple_of((t * ns + me) * depth, depth), depth)
        own = pltpu.make_async_copy(summed.at[rows], stage.at[:, cols], local.at[t])
        own.start()
        copies.append(own)
    for p in range(ns):
        rows = slice((3 * ns + p) * depth, (3 * ns + p + 1) * depth)
        gout[:, p * share : (p + 1) * share] = summed[rows, :].astype(F32)
    total = sums[batch]
    for d, one in enumerate(first):
        one.wait_recv()
        total += near[d]
    mid[...] = total
    second = [send(mid.at[to[0]], far.at[d], s2.at[d], r2.at[d], to) for d, to in enumerate(others)]
    for one in copies:
        one.wait()
    gqkv[...] = stage[...].astype(F32)
    total = mid[me]
    for d, one in enumerate(second):
        one.wait_recv()
        total += far[d]
    small[...] = total
    for one in first + second:
        one.wait_send()


def home(ns, nb, summed, sums):
    rows, share = summed.shape
    depth, width = rows // (4 * ns), ns * share
    tail = sums.shape[2:]
    vm = pl.BlockSpec(memory_space=pltpu.VMEM)
    dma = pltpu.SemaphoreType.DMA
    return pl.pallas_call(
        functools.partial(home_kernel, ns, nb),
        out_shape=(
            jax.ShapeDtypeStruct((depth, 3 * width), F32),
            jax.ShapeDtypeStruct((depth, width), F32),
            jax.ShapeDtypeStruct(tail, F32),
        ),
        in_specs=[vm, vm],
        out_specs=(vm, vm, vm),
        scratch_shapes=[
            pltpu.VMEM((depth, 3 * width), BF),
            pltpu.VMEM((nb - 1, ns) + tail, F32),
            pltpu.VMEM((ns,) + tail, F32),
            pltpu.VMEM((ns - 1,) + tail, F32),
            dma((3,)),
            dma((3, ns - 1)),
            dma((3, ns - 1)),
            dma((nb - 1,)),
            dma((nb - 1,)),
            dma((ns - 1,)),
            dma((ns - 1,)),
        ],
        compiler_params=pltpu.CompilerParams(collective_id=8, has_side_effects=True),
        cost_estimate=pl.CostEstimate(flops=5 * 10**9, bytes_accessed=4 * summed.size, transcendentals=0),
        name="home",
    )(summed, sums)


PARTS = 2


def gather_seq(value):
    return lax.all_gather(value, "seq", axis=0, tiled=True)


def scatter_seq(partial):
    return lax.psum_scatter(partial, "seq", scatter_dimension=0, tiled=True)


def scatter_batch(parts):
    flat = parts.reshape(-1, parts.shape[-1])
    return lax.psum_scatter(flat, "batch", scatter_dimension=0, tiled=True)


def scatter_chips(parts):
    count = lax.axis_size("batch")
    groups = [list(range(core, count, 2)) for core in range(2)]
    flat = parts.reshape(-1, parts.shape[-1])
    return lax.psum_scatter(flat, "batch", scatter_dimension=0, tiled=True, axis_index_groups=groups)


def unpermute(ns, nb, gathered):
    depth = gathered.shape[1] // ns
    return gathered.reshape(nb, ns, depth, -1).transpose(1, 0, 2, 3).reshape(ns * nb * depth, -1)


def unpack_attention(ns, nb, packed):
    share = packed.shape[2]
    parts = packed.reshape(nb, 3, ns, -1, share)
    return parts.transpose(2, 0, 3, 1, 4).reshape(ns * share, 3 * share)


def body(
    block_input,
    lengths,
    ln1_gain,
    ln1_bias,
    w_qkv,
    qv_bias,
    w_out,
    out_bias,
    ln2_gain,
    ln2_bias,
    w_fc1,
    fc1_bias,
    w_fc2,
    fc2_bias,
    out_cotangent,
):
    ns, nb = lax.axis_size("seq"), lax.axis_size("batch")
    seq = lax.axis_index("seq")
    rows, width = block_input.shape[1:]
    share = width // ns
    depth = width // (ns * nb)
    hidden = w_fc1.shape[1] // ns
    chunk = hidden // PARTS
    part = chunk // nb
    pieces = width // chunk
    planar = ns == 4 and nb == 8
    mine, cot_mine = block_input[0], out_cotangent[0]

    vectors = (ln1_gain, ln1_bias, qv_bias, out_bias, ln2_gain, ln2_bias, fc1_bias, fc2_bias)
    wout = lax.all_gather(w_out, "batch", axis=0, tiled=True)
    if planar:
        wq = spread(ns, w_qkv)
        wq, w_fc1 = lax.optimization_barrier((wq, w_fc1))
        packs = spread_ff(ns, nb, PARTS, w_fc1, w_fc2)
        packs, vectors, wout = lax.optimization_barrier((packs, vectors, wout))
        spare = jnp.zeros((1024 - 2 * depth - sum(vec.shape[0] for vec in vectors),), BF)
        block = jnp.concatenate([vectors[0], vectors[0], vectors[1], vectors[1], *vectors[2:], spare])
        block = block.astype(F32).reshape(8, 128)
        h1, cot, packed = collect(ns, nb, mine, cot_mine, block)
        packed = packed.transpose(1, 0, 2, 3).reshape(ns * nb, 1024)
        packed = jnp.concatenate([packed[:, :depth], packed[:, 2 * depth : 3 * depth], packed[:, 4 * depth :]], 1)
    else:
        wq = lax.all_to_all(w_qkv.reshape(depth, 3, ns, share), "seq", 2, 0).transpose(2, 0, 1, 3)
        wq = wq.reshape(3 * ns * depth, share)
        vector = jnp.concatenate(vectors).astype(F32)
        packed = lax.all_gather(vector, ("seq", "batch"), axis=0, tiled=False)
    wq = lax.all_gather(wq, "batch", axis=0, tiled=True).reshape(nb, 3 * ns * depth, share)
    full, at = [], 0
    for vec in vectors:
        full.append(packed[:, at : at + vec.shape[0]].reshape(1, -1))
        at += vec.shape[0]
    gain1, shift1, qv, obias, gain2, shift2, bias1, bias2 = full
    bias1 = lax.dynamic_slice_in_dim(bias1, seq * hidden, hidden, 1).reshape(nb, PARTS, part)
    qbias = lax.dynamic_slice_in_dim(qv, seq * share, share, 1)
    vbias = lax.dynamic_slice_in_dim(qv, width + seq * share, share, 1)
    bias3 = jnp.concatenate([qbias, jnp.zeros_like(qbias), vbias], 1)

    if not planar:
        fc1_part = lax.all_to_all(w_fc1.reshape(depth, ns, hidden), "seq", 1, 0)
        fc1_part = fc1_part.reshape(ns * depth, nb, PARTS, part)
        fc2_part = w_fc2.reshape(PARTS, part, pieces, chunk)
        packs = []
        for c in range(PARTS):
            first = fc1_part[:, :, c].reshape(ns * depth, chunk)
            second = fc2_part[c].transpose(1, 0, 2).reshape(pieces * part, chunk)
            packs.append(jnp.concatenate([first, second], 0))
        h1 = (norm_stats(gather_seq(mine).astype(F32))[0] * gain1 + shift1).astype(BF)
        cot = gather_seq(cot_mine)
    wgs = [lax.all_gather(pack, "batch", axis=0, tiled=True).reshape(nb, -1, chunk) for pack in packs]

    qkv, o, h1t = attend(ns, nb, lengths, h1, wq, bias3)
    if planar:
        x1, h2 = middle(o, wout, mine, obias, gain2, shift2)
    else:
        a = scatter_seq(jnp.dot(o, wout, preferred_element_type=F32))
        x1 = mine.astype(F32) + (a + obias)
        h2 = gather_seq((norm_stats(x1)[0] * gain2 + shift2).astype(BF))

    line = ()
    if planar:
        own, g, du, gb, h2t, before = ff_first(ns, nb, h2, cot, wgs[0], bias1[:, 0].reshape(1, chunk))
        line = (own,)
        h2t, gain1, gain2, bias2 = lax.optimization_barrier((h2t, gain1, gain2, bias2))
        gws = [None]
    else:
        gw, g, du, gb, h2t, before = ff_chunk(ns, nb, h2, None, cot, wgs[0], bias1[:, 0].reshape(1, chunk))
        gws = [scatter_batch(gw)]
    gs, dus, gb1 = [g], [du], [gb.reshape(nb, 1, part)]
    for c in range(1, PARTS):
        gw, g, du, gb, *got = ff_chunk(ns, nb, h2, h2t, cot, wgs[c], bias1[:, c].reshape(1, chunk), *line)
        gws.append(scatter_batch(gw))
        gs.append(g)
        dus.append(du)
        gb1.append(gb.reshape(nb, 1, part))
    if planar:
        dx1, da, rows2, got = ff_back(ns, nb, dus[1], wgs[1], before, x1, cot_mine, gain2, own, got[0])
        line = own, got, *gs, *wgs
    else:
        dh2 = before.astype(F32) + dot_t(dus[1], unpermute(ns, nb, wgs[1][:, : ns * depth]))
        dh2 = scatter_seq(dh2)
        normed2, rstd2 = norm_stats(x1)
        dx1 = cot_mine.astype(F32) + norm_back(dh2, normed2, rstd2, gain2)
        da_mine = dx1.astype(BF)
        rows2 = jnp.stack([jnp.sum(term, 0) for term in (da_mine.astype(F32), dh2 * normed2, dh2)])
        da = gather_seq(da_mine)

    gattn, dproj, gqv, *more = attend_back(ns, nb, lengths, h1t, da, wout, o, qkv, *line)
    if planar:
        gws[0], y = more
    gattn = scatter_chips(gattn) if planar else scatter_batch(gattn)
    if planar:
        gx, rows1, gw1, gw2, lower = finish(ns, nb, dproj, wq, gws, gs, wgs, mine, gain1)
        gx, rows2, gqv, gb1, cot_mine, y = lax.optimization_barrier((gx, rows2, gqv, gb1, cot_mine, y))
        gx = dx1 + gx
        out = (x1 + (jnp.concatenate([y, lower], 0) + bias2)).astype(BF)
        gw1, gw2 = gw1.astype(F32), gw2.astype(F32)
    else:
        dh1 = scatter_seq(dot_t(dproj, unpack_attention(ns, nb, wq)))
        normed1, rstd1 = norm_stats(mine.astype(F32))
        rows1 = jnp.stack([jnp.sum(dh1 * normed1, 0), jnp.sum(dh1, 0)])
        gx = dx1 + norm_back(dh1, normed1, rstd1, gain1)
        y = 0.0
        for g, wg in zip(gs, wgs):
            w2 = wg[:, ns * depth :].reshape(nb, pieces, part, chunk).transpose(0, 2, 1, 3).reshape(chunk, width)
            y += jnp.dot(g, w2, preferred_element_type=F32)
        out = (x1 + (scatter_seq(y) + bias2)).astype(BF)

    if not planar:
        gw1 = jnp.stack([gw[: ns * depth].reshape(ns, depth, nb, part) for gw in gws], 3)
        gw1 = lax.all_to_all(gw1, "seq", 0, 1).astype(F32).reshape(depth, ns * hidden)
        gw2 = jnp.stack([gw[ns * depth :].reshape(pieces, part, chunk) for gw in gws], 0)
        gw2 = gw2.astype(F32).transpose(0, 2, 1, 3).reshape(PARTS * part, width)
        gwqkv = gattn[: 3 * ns * depth].reshape(3, ns, depth, share)
        gwqkv = lax.all_to_all(gwqkv, "seq", 1, 2).astype(F32).transpose(1, 0, 2, 3).reshape(depth, 3 * width)
        gwo = gattn[3 * ns * depth :].reshape(ns, depth, share).astype(F32).transpose(1, 0, 2).reshape(depth, width)

    def place(part, size):
        return lax.dynamic_update_slice_in_dim(jnp.zeros((size,), F32), part, seq * part.shape[0], 0)

    gqv = gqv[0]
    gqv = jnp.concatenate([place(gqv[:share], width), place(gqv[2 * share :], width)])
    gb1 = place(jnp.stack(gb1, 1).reshape(-1), ns * hidden)
    gb2 = jnp.sum(cot_mine.astype(F32), 0)

    def shards(grads):
        return grads.reshape(grads.shape[0], ns * nb, -1).transpose(1, 0, 2).reshape(ns * nb, -1)

    sums = [shards(rows1), gqv.reshape(ns * nb, -1), shards(rows2), gb1.reshape(ns * nb, -1), gb2.reshape(ns * nb, -1)]
    sums = jnp.concatenate(sums, 1)
    if planar:
        sums = jnp.pad(sums, ((0, 0), (0, 1024 - sums.shape[1]))).reshape(ns, nb, 8, 128)
        sums, gx, out, gw1, gw2 = lax.optimization_barrier((sums.transpose(1, 0, 2, 3), gx, out, gw1, gw2))
        gwqkv, gwo, sums = home(ns, nb, gattn, sums)
        sums = sums.reshape(-1)
    else:
        sums = lax.psum_scatter(sums, ("seq", "batch"), scatter_dimension=0, tiled=True)[0]
    small, at = [], 0
    for vec in vectors:
        small.append(sums[at : at + vec.shape[0]])
        at += vec.shape[0]
    return (
        out[None],
        gx[None],
        small[0],
        small[1],
        gwqkv,
        small[2],
        gwo,
        small[3],
        small[4],
        small[5],
        gw1,
        small[6],
        gw2,
        small[7],
    )


def solution(mesh):
    shard = P(("seq", "batch"))
    shard2 = P(("seq", "batch"), None)
    acts = P("batch", "seq", None)
    return jax.shard_map(
        body,
        mesh=mesh,
        in_specs=(acts, P("batch"), shard, shard, shard2, shard, shard2, shard, shard, shard, shard2, shard, shard2, shard, acts),
        out_specs=(acts, acts, shard, shard, shard2, shard, shard2, shard, shard, shard, shard2, shard, shard2, shard),
        check_vma=False,
    )
```

```python
import functools
import math

import jax
import jax.numpy as jnp
from jax import lax
from jax.experimental import pallas as pl
from jax.experimental.pallas import tpu as pltpu
from jax.sharding import PartitionSpec as P

HEAD_DIM = 128
WINDOW = 256
EPS = 1e-05
BF = jnp.bfloat16
F32 = jnp.float32
ROOT = math.sqrt(2.0 / math.pi)


def norm_stats(values):
    mean = jnp.mean(values, -1, keepdims=True)
    centred = values - mean
    rstd = lax.rsqrt(jnp.mean(centred * centred, -1, keepdims=True) + EPS)
    return centred * rstd, rstd


def norm_back(grad, normed, rstd, gain):
    dn = grad * gain
    return rstd * (
        dn - jnp.mean(dn, -1, keepdims=True) - normed * jnp.mean(dn * normed, -1, keepdims=True)
    )


MESH = pl.DeviceIdType.MESH


def send(src, dst, sends, recvs, to):
    one = pltpu.make_async_remote_copy(
        src_ref=src, dst_ref=dst, send_sem=sends, recv_sem=recvs, device_id=to, device_id_type=MESH
    )
    one.start()
    return one


class Line:
    def __init__(self, step, own, prior, got, held, load, sends, recvs):
        self.step, self.own, self.prior, self.got, self.held = step, own, prior, got, held
        self.load, self.sends, self.recvs = load, sends, recvs
        self.last = own.shape[0] - 1
        self.seq, batch = lax.axis_index("seq"), lax.axis_index("batch")
        self.chip, self.core = batch // 2, lax.rem(batch, 2)

    def ready(self):
        self.got[...] = jnp.zeros_like(self.got)
        ahead = self.last - self.step
        wanted = jnp.minimum(self.chip + ahead, self.last), jnp.maximum(self.chip - ahead, 0)
        for way, chunk in enumerate(wanted):
            pltpu.make_async_copy(self.own.at[chunk], self.held.at[way], self.load.at[way]).start()

    def neighbours(self):
        count = self.last + 1
        return [(self.seq, 2 * lax.rem(self.chip + d, count) + self.core) for d in (1, count - 1)]

    def copy(self, way):
        to = jnp.minimum(self.chip + 1, self.last) if way == 0 else jnp.maximum(self.chip - 1, 0)
        return pltpu.make_async_remote_copy(
            src_ref=self.held.at[way],
            dst_ref=self.got.at[way],
            send_sem=self.sends.at[way],
            recv_sem=self.recvs.at[way],
            device_id=(self.seq, 2 * to + self.core),
            device_id_type=MESH,
        )

    def roles(self):
        chip, last, step = self.chip, self.last, self.step
        gives = chip <= step, chip >= last - step
        takes = (chip >= 1) & (chip <= step + 1), (chip <= last - 1) & (chip >= last - 1 - step)
        return gives, takes

    def go(self):
        for way in range(2):
            here = self.held.at[way]
            pltpu.make_async_copy(here, here, self.load.at[way]).wait()
            if self.prior is not None:
                total = self.held[way].astype(F32) + self.prior[way].astype(F32)
                self.held[way] = total.astype(BF)

            @pl.when(self.roles()[0][way])
            def _():
                self.copy(way).start()

    def stop(self):
        gives, takes = self.roles()
        for way in range(2):

            @pl.when(takes[way])
            def _():
                self.copy(way).wait_recv()

            @pl.when(gives[way])
            def _():
                self.copy(way).wait_send()


def line_scratch(rows, width):
    dma = pltpu.SemaphoreType.DMA
    return [pltpu.VMEM((2, rows, width), BF), dma((2,)), dma((2,)), dma((2,))]


def dot_t(left, right):
    return lax.dot_general(left, right, (((1,), (1,)), ((), ())), preferred_element_type=F32)


def t_dot(left, right):
    return lax.dot_general(left, right, (((0,), (0,)), ((), ())), preferred_element_type=F32)


def load_rows(ns, nb, depth, src, dst, sem):
    def one(k, carry):
        s, b = k // nb, lax.rem(k, nb)
        pltpu.make_async_copy(
            src.at[b, pl.ds(s * depth, depth), :], dst.at[pl.ds(k * depth, depth), :], sem
        ).start()
        return carry

    lax.fori_loop(0, ns * nb, one, 0)


def load_attention(ns, nb, packed, w, sem):
    share = packed.shape[2]
    depth = packed.shape[1] // (3 * ns)

    def one(k, carry):
        s, b = k // nb, lax.rem(k, nb)
        for t in range(3):
            pltpu.make_async_copy(
                packed.at[b, pl.ds((t * ns + s) * depth, depth), :],
                w.at[pl.ds(k * depth, depth), t * share : (t + 1) * share],
                sem,
            ).start()
        return carry

    lax.fori_loop(0, ns * nb, one, 0)


def load_second(nb, packed, w, sem):
    chunk, width = w.shape
    part, pieces, base = chunk // nb, width // chunk, width // nb

    def one(k, carry):
        for p in range(pieces):
            pltpu.make_async_copy(
                packed.at[k, pl.ds(base + p * part, part), :],
                w.at[pl.ds(k * part, part), p * chunk : (p + 1) * chunk],
                sem,
            ).start()
        return carry

    lax.fori_loop(0, nb, one, 0)


def soft_block(query, keys, block, first, length):
    rows, count = query.shape[0], keys.shape[0]
    scores = dot_t(query, keys) * HEAD_DIM ** (-0.5)
    query_pos = block * rows + lax.broadcasted_iota(jnp.int32, (rows, count), 0)
    key_pos = first + lax.broadcasted_iota(jnp.int32, (rows, count), 1)
    back = query_pos - key_pos
    valid = (back >= 0) & (back < WINDOW) & ((key_pos < length) | (back == 0))
    scores = jnp.where(valid, scores, -1e30)
    expo = jnp.exp(scores - jnp.max(scores, -1, keepdims=True))
    return expo / jnp.sum(expo, -1, keepdims=True)


def attend_kernel(ns, nb, length, h1, wq, bias, qkv, o, h1t, w, sem):
    tokens, width = h1.shape
    share = o.shape[1]
    rows = tokens // ns
    load_attention(ns, nb, wq, w, sem)
    for r in range(0, tokens, 256):
        h1t[:, r : r + 256] = h1[r : r + 256, :].T
    pltpu.make_async_copy(w, w, sem).wait()
    wide = min(512, 3 * share)

    def project(j, carry):
        cols = pl.ds(pl.multiple_of(j * wide, wide), wide)
        for r in range(0, tokens, 256):
            part = jnp.dot(h1[r : r + 256, :], w[:, cols], preferred_element_type=F32)
            qkv[r : r + 256, cols] = (part + bias[:, cols]).astype(BF)
        return carry

    lax.fori_loop(0, 3 * share // wide, project, 0)
    limit = length[0]

    def head(h, carry):
        at = h * HEAD_DIM
        col_q = pl.ds(pl.multiple_of(at, HEAD_DIM), HEAD_DIM)
        col_k = pl.ds(pl.multiple_of(share + at, HEAD_DIM), HEAD_DIM)
        col_v = pl.ds(pl.multiple_of(2 * share + at, HEAD_DIM), HEAD_DIM)
        for n in range(ns):
            first = max(n - 1, 0) * rows
            mine, seen = slice(n * rows, n * rows + rows), slice(first, first + 2 * rows)
            probs = soft_block(qkv[mine, col_q], qkv[seen, col_k], n, first, limit)
            part = jnp.dot(probs.astype(BF), qkv[seen, col_v], preferred_element_type=F32)
            o[mine, col_q] = part.astype(BF)
        return carry

    lax.fori_loop(0, share // HEAD_DIM, head, 0)


def attend(ns, nb, lengths, h1, wq, bias):
    tokens, width = h1.shape
    share = wq.shape[2]
    vm = pl.BlockSpec(memory_space=pltpu.VMEM)
    return pl.pallas_call(
        functools.partial(attend_kernel, ns, nb),
        out_shape=(
            jax.ShapeDtypeStruct((tokens, 3 * share), BF),
            jax.ShapeDtypeStruct((tokens, share), BF),
            jax.ShapeDtypeStruct((width, tokens), BF),
        ),
        in_specs=[pl.BlockSpec(memory_space=pltpu.SMEM), vm, pl.BlockSpec(memory_space=pl.ANY), vm],
        out_specs=(vm, vm, vm),
        scratch_shapes=[pltpu.VMEM((width, 3 * share), BF), pltpu.SemaphoreType.DMA],
        compiler_params=pltpu.CompilerParams(vmem_limit_bytes=56 * 2**20),
        cost_estimate=pl.CostEstimate(flops=10**6, bytes_accessed=10**4, transcendentals=0),
        name="attend",
    )(lengths, h1, wq, bias)


def upper_rows(rows):
    return 3 * rows // 4


def attend_back_kernel(ns, nb, moving, length, h1t_in, da, wout, o, qkv_in, *refs):
    line = None
    if moving:
        own, prior, g0_in, g1_in, wg0, wg1, pair, dproj, gqv, sums, branch_sum, *rest = refs
        do, gw, gwo, acc_k, acc_v, sems, h1t, qkv, g0, g1, near, to_twin, from_twin, *rest = rest
        out, via, from_x, from_y, s1, r1, got, *rest = rest
        line = Line(2, own, prior, got, *rest)
    else:
        packed, dproj, gqv, do, gw, gwo, acc_k, acc_v, sems, h1t, qkv = refs
    width, tokens = h1t.shape
    share = o.shape[1]
    rows = tokens // ns
    depth = width // (ns * nb)
    scale = HEAD_DIM ** (-0.5)
    limit = length[0]
    steps = None
    loads = [pltpu.make_async_copy(qkv_in, qkv, sems.at[4]), pltpu.make_async_copy(h1t_in, h1t, sems.at[5])]
    if moving:
        chunk = g0.shape[1]
        halves = gw.at[:chunk], gw.at[chunk:]
        line.ready()
        for k, (wg, src, dst) in enumerate(((wg0, g0_in, g0), (wg1, g1_in, g1))):
            loads.append(pltpu.make_async_copy(src, dst, sems.at[6 + k]))
            loads[-1].start()
            load_second(nb, wg, halves[k], sems.at[2 + k])
        loads[0].start()
        loads[1].start()
        chips = nb // 2
        twin = (line.seq, 2 * line.chip + 1 - line.core)
        place = greet([*line.neighbours(), twin])
        line.go()

        def strip(row, core):
            return pl.ds(pl.multiple_of((row + core) * depth, depth), depth)

        def exchange(t, source):
            for c in range(chips):
                for k in range(ns):
                    ref, row, cols = source(c, k)
                    there = near.at[c, (t * ns + k) * depth : (t * ns + k + 1) * depth]
                    send(ref.at[strip(row, 1 - line.core), cols], there, to_twin.at[t], from_twin.at[t], twin)

        def combine(t, source):
            got_piece = near.at[:, t * ns * depth : (t + 1) * ns * depth]
            whole = pltpu.make_async_remote_copy(
                src_ref=got_piece,
                dst_ref=got_piece,
                send_sem=to_twin.at[t],
                recv_sem=from_twin.at[t],
                device_id=twin,
                device_id_type=MESH,
            )
            whole.wait()
            for c in range(chips):
                for k in range(ns):
                    ref, row, cols = source(c, k)
                    here = slice((t * ns + k) * depth, (t * ns + k + 1) * depth)
                    total = ref[strip(row, line.core), cols].astype(F32) + near[c, here].astype(F32)
                    pair[c, here] = total.astype(BF)

        def piece_out(c, k):
            return gwo, 2 * c, slice(k * share, (k + 1) * share)

        def piece_qkv(t):
            return lambda c, k: (gw, k * nb + 2 * c, slice(t * share, (t + 1) * share))

        def branch(block):
            at = pl.ds(pl.multiple_of(block * rows, rows), upper_rows(rows))
            total = jnp.dot(g0[at, :], halves[0][...], preferred_element_type=F32)
            return total + jnp.dot(g1[at, :], halves[1][...], preferred_element_type=F32)

        steps = scatter_steps(branch, place, (out, via, from_x, from_y), s1, r1)
    else:
        loads[0].start()
        loads[1].start()
    for r in range(0, tokens, 256):
        do[r : r + 256, :] = dot_t(da[r : r + 256, :], wout[...]).astype(BF)
    ot = o[...].T
    for c in range(0, width, 512):
        gwo[:, c : c + 512] = jnp.dot(ot, da[:, c : c + 512], preferred_element_type=F32).astype(BF)

    def store_out(b, carry):
        for p in range(ns):
            pltpu.make_async_copy(
                gwo.at[pl.ds(b * depth, depth), p * share : (p + 1) * share],
                packed.at[b, (3 * ns + p) * depth : (3 * ns + p + 1) * depth, :],
                sems.at[0],
            ).start()
        return carry

    if not moving:
        lax.fori_loop(0, nb, store_out, 0)
    if moving:
        exchange(3, piece_out)
        for k in range(2):
            loads[2 + k].wait()
            pltpu.make_async_copy(halves[k], halves[k], sems.at[2 + k]).wait()
        for _ in range(3):
            next(steps)
    loads[0].wait()

    def head(h, carry):
        at = h * HEAD_DIM
        col_q = pl.ds(pl.multiple_of(at, HEAD_DIM), HEAD_DIM)
        col_k = pl.ds(pl.multiple_of(share + at, HEAD_DIM), HEAD_DIM)
        col_v = pl.ds(pl.multiple_of(2 * share + at, HEAD_DIM), HEAD_DIM)
        acc_k[...] = jnp.zeros_like(acc_k)
        acc_v[...] = jnp.zeros_like(acc_v)
        for n in range(ns):
            first = max(n - 1, 0) * rows
            mine, seen = slice(n * rows, n * rows + rows), slice(first, first + 2 * rows)
            query, keys, grad = qkv[mine, col_q], qkv[seen, col_k], do[mine, col_q]
            probs = soft_block(query, keys, n, first, limit)
            dp = dot_t(grad, qkv[seen, col_v])
            ds = (probs * (dp - jnp.sum(dp * probs, -1, keepdims=True))).astype(BF)
            dq = jnp.dot(ds, keys, preferred_element_type=F32) * scale
            dproj[mine, col_q] = dq.astype(BF)
            acc_k[seen, :] += t_dot(ds, query)
            acc_v[seen, :] += t_dot(probs.astype(BF), grad)
        dproj[:, col_k] = (acc_k[...] * scale).astype(BF)
        dproj[:, col_v] = acc_v[...].astype(BF)
        return carry

    lax.fori_loop(0, share // HEAD_DIM, head, 0)
    loads[1].wait()
    if moving:
        next(steps)
        next(steps)
    wide = min(512, 3 * share)

    def weights(j, carry):
        cols = pl.ds(pl.multiple_of(j * wide, wide), wide)
        gqv[:, cols] = jnp.sum(dproj[:, cols].astype(F32), 0, keepdims=True)
        for r in range(0, width, 512):
            gw[r : r + 512, cols] = jnp.dot(
                h1t[r : r + 512, :], dproj[:, cols], preferred_element_type=F32
            ).astype(BF)
        return carry

    if moving:
        for t in range(3):
            weights(t, 0)
            exchange(t, piece_qkv(t))
        combine(3, piece_out)
        size = upper_rows(rows) // 2
        for part, total in enumerate(next(steps)):
            branch_sum[part * size : (part + 1) * size, :] = total
        for t in range(3):
            combine(t, piece_qkv(t))
        line.stop()
        mine = pltpu.make_async_copy(own.at[line.chip], line.held.at[0], sems.at[2])
        mine.start()
        mine.wait()
        sums[...] = (line.held[0].astype(F32) + got[0].astype(F32) + got[1].astype(F32)).astype(BF)
        return
    lax.fori_loop(0, 3 * share // wide, weights, 0)

    def store(k, c):
        s, b = k // nb, lax.rem(k, nb)
        for t in range(3):
            pltpu.make_async_copy(
                gw.at[pl.ds(k * depth, depth), t * share : (t + 1) * share],
                packed.at[b, pl.ds((t * ns + s) * depth, depth), :],
                sems.at[1],
            ).start()
        return c

    lax.fori_loop(0, ns * nb, store, 0)
    pltpu.make_async_copy(gw, gw, sems.at[1]).wait()
    pltpu.make_async_copy(gwo, gwo, sems.at[0]).wait()


def attend_back(ns, nb, lengths, h1t, da, wout, o, qkv, *more):
    width, tokens = h1t.shape
    share = o.shape[1]
    rows = tokens // ns
    vm = pl.BlockSpec(memory_space=pltpu.VMEM)
    hbm = pl.BlockSpec(memory_space=pl.ANY)
    moving = len(more) > 0
    extra, scratch = (), []
    if moving:
        prior = more[1]
        extra = jax.ShapeDtypeStruct(prior.shape[1:], BF), jax.ShapeDtypeStruct((upper_rows(rows), width), F32)
        scratch = [pltpu.VMEM(one.shape, BF) for one in more[2:4]]
        scratch += [pltpu.VMEM((nb // 2, 4 * width // nb, share), BF)] + [pltpu.SemaphoreType.DMA((4,))] * 2
        scratch += scatter_scratch(upper_rows(rows), width) + [pltpu.VMEM(prior.shape, BF)] + line_scratch(*prior.shape[1:])
    return pl.pallas_call(
        functools.partial(attend_back_kernel, ns, nb, moving),
        out_shape=(
            jax.ShapeDtypeStruct((nb // 2 if moving else nb, 4 * width // nb, share), BF),
            jax.ShapeDtypeStruct((tokens, 3 * share), BF),
            jax.ShapeDtypeStruct((1, 3 * share), F32),
        )
        + extra,
        in_specs=[pl.BlockSpec(memory_space=pltpu.SMEM), hbm, vm, vm, vm, hbm] + [hbm, vm, hbm, hbm, hbm, hbm][: len(more)],
        out_specs=(vm if moving else hbm, vm, vm) + (vm,) * len(extra),
        scratch_shapes=[
            pltpu.VMEM((tokens, share), BF),
            pltpu.VMEM((width, width if moving else 3 * share), BF),
            pltpu.VMEM((share, width), BF),
            pltpu.VMEM((tokens, HEAD_DIM), F32),
            pltpu.VMEM((tokens, HEAD_DIM), F32),
            pltpu.SemaphoreType.DMA((8,)),
            pltpu.VMEM((width, tokens), BF),
            pltpu.VMEM((tokens, 3 * share), BF),
        ]
        + scratch,
        compiler_params=pltpu.CompilerParams(
            collective_id=9 if moving else None, has_side_effects=moving, vmem_limit_bytes=60 * 2**20
        ),
        cost_estimate=pl.CostEstimate(
            flops=40 * 10**9, bytes_accessed=12 * width * share, transcendentals=tokens * 512 * share // 128
        ),
        name="attend_back",
    )(lengths, h1t, da, wout, o, qkv, *more)


def slopes(u, dg):
    sq = u * u
    th = jnp.tanh(ROOT * u * (1.0 + 0.044715 * sq))
    cdf = 0.5 * (1.0 + th)
    slope = cdf + 0.5 * u * (1.0 - th * th) * (ROOT * (1.0 + 3.0 * 0.044715 * sq))
    return (u * cdf).astype(BF), (dg * slope).astype(BF)


def ff_first_kernel(ns, nb, h2, cot, wg, bias, own, g_out, du_out, gb, h2t, dh2, w1, w2, gw1, gw2, near2, near1, *sems):
    load, to2, from2, to1, from1 = sems
    tokens, width = h2.shape
    chunk = g_out.shape[1]
    depth = width // (ns * nb)
    part = chunk // nb
    pieces = width // chunk
    half = ns * depth
    chips = nb // 2
    tile = min(512, chunk)
    step = min(256, tokens)
    seq, batch = lax.axis_index("seq"), lax.axis_index("batch")
    chip, core = batch // 2, lax.rem(batch, 2)
    twin = (seq, 2 * chip + 1 - core)
    load_rows(ns, nb, depth, wg, w1, load.at[0])

    def load2(k, carry):
        for p in range(pieces):
            pltpu.make_async_copy(
                wg.at[k, pl.ds(half + p * part, part), :],
                w2.at[pl.ds(k * part, part), p * chunk : (p + 1) * chunk],
                load.at[1],
            ).start()
        return carry

    lax.fori_loop(0, nb, load2, 0)
    barrier = pltpu.get_barrier_semaphore()
    pl.semaphore_signal(barrier, inc=1, device_id=twin, device_id_type=MESH)
    for r in range(0, tokens, step):
        h2t[:, r : r + step] = h2[r : r + step, :].T
    pltpu.make_async_copy(w1, w1, load.at[0]).wait()
    pltpu.make_async_copy(w2, w2, load.at[1]).wait()

    def one_tile(j, carry):
        cols = pl.ds(pl.multiple_of(j * tile, tile), tile)
        total = jnp.zeros((1, tile), F32)
        for r in range(0, tokens, step):
            rows = slice(r, r + step)
            u = jnp.dot(h2[rows, :], w1[:, cols], preferred_element_type=F32) + bias[:, cols]
            g, du = slopes(u, dot_t(cot[rows, :], w2[cols, :]))
            g_out[rows, cols] = g
            du_out[rows, cols] = du
            total += jnp.sum(du.astype(F32), 0, keepdims=True)
        gb[:, cols] = total
        return carry

    lax.fori_loop(0, chunk // tile, one_tile, 0)

    def second(j, carry):
        cols = pl.ds(pl.multiple_of(j * tile, tile), tile)
        gt = g_out[:, cols].T
        for r in range(0, width, 512):
            gw2[cols, r : r + 512] = jnp.dot(gt, cot[:, r : r + 512], preferred_element_type=F32).astype(BF)
        return carry

    lax.fori_loop(0, chunk // tile, second, 0)
    pl.semaphore_wait(barrier, 1)

    def rows2(c, kept):
        return pl.ds(pl.multiple_of((2 * c + (core if kept else 1 - core)) * part, part), part)

    def rows1(c, s, kept):
        return pl.ds(pl.multiple_of((s * nb + 2 * c + (core if kept else 1 - core)) * depth, depth), depth)

    for c in range(chips):
        for p in range(pieces):
            span = slice(p * part, (p + 1) * part)
            send(gw2.at[rows2(c, False), p * chunk : (p + 1) * chunk], near2.at[c, span], to2, from2, twin)

    def first(j, carry):
        cols = pl.ds(pl.multiple_of(j * tile, tile), tile)
        for r in range(0, width, 512):
            gw1[r : r + 512, cols] = jnp.dot(
                h2t[r : r + 512, :], du_out[:, cols], preferred_element_type=F32
            ).astype(BF)
        return carry

    lax.fori_loop(0, chunk // tile, first, 0)
    for c in range(chips):
        for s in range(ns):
            send(gw1.at[rows1(c, s, False)], near1.at[c, s * depth : (s + 1) * depth], to1, from1, twin)

    def whole(near, send_sem, recv_sem):
        return pltpu.make_async_remote_copy(
            src_ref=near, dst_ref=near, send_sem=send_sem, recv_sem=recv_sem, device_id=twin, device_id_type=MESH
        )

    def back(k, carry):
        rows = pl.ds(pl.multiple_of(k * step, step), step)
        for c in range(0, width, 512):
            dh2[rows, c : c + 512] = dot_t(du_out[rows, :], w1[c : c + 512, :]).astype(BF)
        return carry

    lax.fori_loop(0, tokens // step, back, 0)
    whole(near2, to2, from2).wait_recv()
    for c in range(chips):
        for p in range(pieces):
            mine = gw2[rows2(c, True), p * chunk : (p + 1) * chunk]
            total = mine.astype(F32) + near2[c, p * part : (p + 1) * part].astype(F32)
            own[c, half + p * part : half + (p + 1) * part] = total.astype(BF)
    whole(near1, to1, from1).wait_recv()
    for c in range(chips):
        for s in range(ns):
            total = gw1[rows1(c, s, True), :].astype(F32) + near1[c, s * depth : (s + 1) * depth].astype(F32)
            own[c, s * depth : (s + 1) * depth] = total.astype(BF)
    whole(near2, to2, from2).wait_send()
    whole(near1, to1, from1).wait_send()


def ff_first(ns, nb, h2, cot, wg, bias):
    tokens, width = h2.shape
    chunk = wg.shape[2]
    half = width // nb
    vm = pl.BlockSpec(memory_space=pltpu.VMEM)
    dma = pltpu.SemaphoreType.DMA
    inner = jax.ShapeDtypeStruct((tokens, chunk), BF)
    near = pltpu.VMEM((nb // 2, half, chunk), BF)
    return pl.pallas_call(
        functools.partial(ff_first_kernel, ns, nb),
        out_shape=(
            jax.ShapeDtypeStruct((nb // 2, 2 * half, chunk), BF),
            inner,
            inner,
            jax.ShapeDtypeStruct((1, chunk), F32),
            jax.ShapeDtypeStruct((width, tokens), BF),
            jax.ShapeDtypeStruct((tokens, width), BF),
        ),
        in_specs=[vm, vm, pl.BlockSpec(memory_space=pl.ANY), vm],
        out_specs=(vm,) * 6,
        scratch_shapes=[
            pltpu.VMEM((width, chunk), BF),
            pltpu.VMEM((chunk, width), BF),
            pltpu.VMEM((width, chunk), BF),
            pltpu.VMEM((chunk, width), BF),
            near,
            near,
            dma((2,)),
            dma,
            dma,
            dma,
            dma,
        ],
        compiler_params=pltpu.CompilerParams(collective_id=7, has_side_effects=True, vmem_limit_bytes=60 * 2**20),
        cost_estimate=pl.CostEstimate(flops=40 * 10**9, bytes_accessed=8 * wg.size, transcendentals=tokens * chunk),
        name="ff_first",
    )(h2, cot, wg, bias)


def ff_kernel(ns, nb, first, moving, *refs):
    line = None
    if first:
        h2_in, cot_in, wg, bias, gwg, g_out, du_out, gb, h2t, dh2, w1, w2, gw1, gw2, h2, cot, u_part, sems = refs
    elif moving:
        h2_in, h2t_in, cot_in, wg, bias, own, gwg, g_out, du_out, gb, got, *refs = refs
        w1, w2, gw1, gw2, h2, cot, u_part, sems, h2t, held, s0, s1, s2 = refs
        line = Line(0, own, None, got, held, s0, s1, s2)
    else:
        h2_in, h2t_in, cot_in, wg, bias, gwg, g_out, du_out, gb, *refs = refs
        w1, w2, gw1, gw2, h2, cot, u_part, sems, h2t = refs
    tokens, width = h2_in.shape
    chunk = g_out.shape[1]
    depth = width // (ns * nb)
    part = chunk // nb
    pieces = width // chunk
    half = ns * depth
    tile = min(512, chunk)
    tiles = chunk // tile
    step = min(256, tokens)

    def load1(k, carry):
        s, b = k // nb, lax.rem(k, nb)
        pltpu.make_async_copy(
            wg.at[b, pl.ds(s * depth, depth), :], w1.at[pl.ds(k * depth, depth), :], sems.at[0]
        ).start()
        return carry

    def load2(k, carry):
        for p in range(pieces):
            pltpu.make_async_copy(
                wg.at[k, pl.ds(half + p * part, part), :],
                w2.at[pl.ds(k * part, part), p * chunk : (p + 1) * chunk],
                sems.at[1],
            ).start()
        return carry

    first_load = pltpu.make_async_copy(h2_in, h2, sems.at[4])
    first_load.start()
    lax.fori_loop(0, ns * nb, load1, 0)
    if moving:
        line.ready()
        barrier = pltpu.get_barrier_semaphore()
        for other in line.neighbours():
            pl.semaphore_signal(barrier, inc=1, device_id=other, device_id_type=MESH)
        pl.semaphore_wait(barrier, 2)
        line.go()
    first_load.wait()
    pltpu.make_async_copy(w1, w1, sems.at[0]).wait()
    second_load = pltpu.make_async_copy(cot_in, cot, sems.at[5])
    second_load.start()
    lax.fori_loop(0, nb, load2, 0)
    if not first:
        third_load = pltpu.make_async_copy(h2t_in, h2t, sems.at[6])
        third_load.start()
    if first:
        for r in range(0, tokens, step):
            h2t[:, r : r + step] = h2[r : r + step, :].T

    def one_tile(j, carry):
        at = pl.multiple_of(j * tile, tile)
        cols = pl.ds(at, tile)
        total = jnp.zeros((1, tile), F32)
        for r in range(0, tokens, step):
            rows = slice(r, r + step)
            u_part[rows, :] = jnp.dot(h2[rows, :], w1[:, cols], preferred_element_type=F32) + bias[:, cols]

        @pl.when(j == 0)
        def _():
            second_load.wait()
            pltpu.make_async_copy(w2, w2, sems.at[1]).wait()
            if not first:
                third_load.wait()

        for r in range(0, tokens, step):
            rows = slice(r, r + step)
            g, du = slopes(u_part[rows, :], dot_t(cot[rows, :], w2[cols, :]))
            g_out[rows, cols] = g
            du_out[rows, cols] = du
            total += jnp.sum(du.astype(F32), 0, keepdims=True)
        gb[:, cols] = total
        for r in range(0, width, 512):
            gw1[j, r : r + 512, :] = jnp.dot(
                h2t[r : r + 512, :], du_out[:, cols], preferred_element_type=F32
            ).astype(BF)
        def store1(k, c):
            s, b = k // nb, lax.rem(k, nb)
            pltpu.make_async_copy(
                gw1.at[j, pl.ds(k * depth, depth), :],
                gwg.at[b, pl.ds(s * depth, depth), cols],
                sems.at[2],
            ).start()
            return c

        lax.fori_loop(0, ns * nb, store1, 0)
        gt = g_out[:, cols].T
        for r in range(0, width, 512):
            gw2[j, :, r : r + 512] = jnp.dot(
                gt, cot[:, r : r + 512], preferred_element_type=F32
            ).astype(BF)
        count = tile // part

        def store2(k, c):
            for p in range(pieces):
                pltpu.make_async_copy(
                    gw2.at[j, pl.ds(k * part, part), p * chunk : (p + 1) * chunk],
                    gwg.at[j * count + k, pl.ds(half + p * part, part), :],
                    sems.at[3],
                ).start()
            return c

        lax.fori_loop(0, count, store2, 0)
        return carry

    lax.fori_loop(0, tiles, one_tile, 0)
    if first:
        for r in range(0, tokens, step):
            for c in range(0, width, 512):
                part_sum = dot_t(du_out[r : r + step, :], w1[c : c + 512, :])
                dh2[r : r + step, c : c + 512] = part_sum.astype(BF)
    pltpu.make_async_copy(gw1, gw1, sems.at[2]).wait()
    pltpu.make_async_copy(gw2, gw2, sems.at[3]).wait()
    if moving:
        line.stop()


def ff_chunk(ns, nb, h2, h2t, cot, wg, bias, own=None):
    tokens, width = h2.shape
    chunk = wg.shape[2]
    tile = min(512, chunk)
    first = h2t is None
    vm = pl.BlockSpec(memory_space=pltpu.VMEM)
    hbm = pl.BlockSpec(memory_space=pl.ANY)
    inner = jax.ShapeDtypeStruct((tokens, chunk), BF)
    extra = (jax.ShapeDtypeStruct((width, tokens), BF), jax.ShapeDtypeStruct((tokens, width), BF)) if first else ()
    given = (h2, cot, wg, bias) if first else (h2, h2t, cot, wg, bias)
    moving = own is not None
    more = []
    if moving:
        given += (own,)
        extra = (jax.ShapeDtypeStruct((2,) + own.shape[1:], BF),)
        more = line_scratch(*own.shape[1:])
    if not first:
        more = [pltpu.VMEM((width, tokens), BF)] + more
    return pl.pallas_call(
        functools.partial(ff_kernel, ns, nb, first, moving),
        out_shape=(jax.ShapeDtypeStruct(wg.shape, BF), inner, inner, jax.ShapeDtypeStruct((1, chunk), F32)) + extra,
        in_specs=[vm if one is bias else hbm for one in given],
        out_specs=(hbm,) + (vm,) * (3 + len(extra)),
        scratch_shapes=[
            pltpu.VMEM((width, chunk), BF),
            pltpu.VMEM((chunk, width), BF),
            pltpu.VMEM((chunk // tile, width, tile), BF),
            pltpu.VMEM((chunk // tile, tile, width), BF),
            pltpu.VMEM((tokens, width), BF),
            pltpu.VMEM((tokens, width), BF),
            pltpu.VMEM((tokens, tile), F32),
            pltpu.SemaphoreType.DMA((7,)),
        ]
        + more,
        compiler_params=pltpu.CompilerParams(
            collective_id=4 if moving else None, has_side_effects=moving, vmem_limit_bytes=60 * 2**20
        ),
        cost_estimate=pl.CostEstimate(
            flops=40 * 10**9,
            bytes_accessed=4 * wg.size,
            transcendentals=tokens * chunk,
        ),
        name="ff_chunk",
    )(*given)


def greet(more=(), later=False):
    me, batch = lax.axis_index("seq"), lax.axis_index("batch")
    by_x = me + 1 - 2 * lax.rem(me, 2)
    by_y = lax.rem(me + 2, 4)
    barrier = pltpu.get_barrier_semaphore()
    for other in [(by_x, batch), (by_y, batch), *more]:
        pl.semaphore_signal(barrier, inc=1, device_id=other, device_id_type=MESH)
    place = me, by_x, by_y, (by_x, batch), (by_y, batch)
    if later:
        return place, lambda: pl.semaphore_wait(barrier, 2 + len(more))
    pl.semaphore_wait(barrier, 2 + len(more))
    return place


def scatter_steps(partial, place, buffers, send, recv, met=None, split=False):
    me, by_x, by_y, to_x, to_y = place
    out, via, from_x, from_y = buffers
    half = via.shape[1]
    top, low = slice(0, half), slice(half, 2 * half)
    far = 3 - me

    def copy(k, src, dst, to):
        one = pltpu.make_async_remote_copy(
            src_ref=src, dst_ref=dst, send_sem=send.at[k], recv_sem=recv.at[k], device_id=to, device_id_type=MESH
        )
        one.start()
        return one

    out[0] = partial(far).astype(BF)
    if met:
        met()
    c0 = copy(0, out.at[0, top], via.at[0], to_y)
    c1 = copy(1, out.at[0, low], via.at[1], to_x)
    yield
    block = partial(by_x)
    out[1, low] = block[low].astype(BF)
    c2 = copy(2, out.at[1, low], from_x.at[low], to_x)
    x_top = block[top]
    yield
    block = partial(by_y)
    out[2, top] = block[top].astype(BF)
    c3 = copy(3, out.at[2, top], from_y.at[top], to_y)
    y_low = block[low]
    yield
    c0.wait_recv()
    out[1, top] = (x_top + via[0].astype(F32)).astype(BF)
    c4 = copy(4, out.at[1, top], from_x.at[top], to_x)
    c1.wait_recv()
    out[2, low] = (y_low + via[1].astype(F32)).astype(BF)
    c5 = copy(5, out.at[2, low], from_y.at[low], to_y)
    yield
    mine = partial(me)
    yield
    c3.wait_recv()
    c4.wait_recv()
    mine_top = mine[top] + from_x[top].astype(F32) + from_y[top].astype(F32)
    if split:
        yield mine_top
    c2.wait_recv()
    c5.wait_recv()
    mine_low = mine[low] + from_x[low].astype(F32) + from_y[low].astype(F32)
    if split:
        yield mine_low
    for one in (c0, c1, c2, c3, c4, c5):
        one.wait_send()
    if not split:
        yield mine_top, mine_low


def scatter_sum(partial, place, buffers, send, recv):
    return list(scatter_steps(partial, place, buffers, send, recv))[-1]


def scatter_scratch(rows, width):
    return [
        pltpu.VMEM((3, rows, width), BF),
        pltpu.VMEM((2, rows // 2, width), BF),
        pltpu.VMEM((rows, width), BF),
        pltpu.VMEM((rows, width), BF),
        pltpu.SemaphoreType.DMA((6,)),
        pltpu.SemaphoreType.DMA((6,)),
    ]


def gather_steps(full, rows, place, send_sems, recv_sems):
    me, by_x, by_y, to_x, to_y = place
    half = rows // 2

    def copy(k, block, part, to):
        at = full.at[pl.ds(pl.multiple_of(block * rows + part * half, half), half)]
        return send(at, at, send_sems.at[k], recv_sems.at[k], to)

    c0 = copy(0, me, 0, to_x)
    c2 = copy(2, me, 0, to_y)
    yield
    c3 = copy(3, me, 1, to_y)
    c1 = copy(1, me, 1, to_x)
    yield
    c0.wait_recv()
    c4 = copy(4, by_x, 0, to_y)
    c3.wait_recv()
    c5 = copy(5, by_y, 1, to_x)
    yield
    for one in (c1, c2, c4, c5):
        one.wait_recv()
    for one in (c0, c1, c2, c3, c4, c5):
        one.wait_send()


def gather_blocks(full, rows, place, send_sems, recv_sems):
    for _ in gather_steps(full, rows, place, send_sems, recv_sems):
        pass


GATHER_SEMS = [pltpu.SemaphoreType.DMA((6,)), pltpu.SemaphoreType.DMA((6,))]


def middle_kernel(o, wout, mine, obias, gain, shift, x1, h2, out, via, from_x, from_y, s1, r1, s2, r2):
    rows, width = mine.shape
    half = rows // 2
    place = greet()

    def partial(block):
        at = pl.multiple_of(block * rows, rows)
        return jnp.dot(o[pl.ds(at, rows), :], wout[...], preferred_element_type=F32)

    sums = scatter_sum(partial, place, (out, via, from_x, from_y), s1, r1)
    for part, total in enumerate(sums):
        span = slice(part * half, part * half + half)
        res = mine[span, :].astype(F32) + (total + obias[...])
        x1[span, :] = res
        normed, _ = norm_stats(res)
        at = pl.multiple_of(place[0] * rows + part * half, half)
        h2[pl.ds(at, half), :] = (normed * gain[...] + shift[...]).astype(BF)
    gather_blocks(h2, rows, place, s2, r2)


def middle(o, wout, mine, obias, gain, shift):
    tokens = o.shape[0]
    rows, width = mine.shape
    vm = pl.BlockSpec(memory_space=pltpu.VMEM)
    return pl.pallas_call(
        middle_kernel,
        out_shape=(jax.ShapeDtypeStruct((rows, width), F32), jax.ShapeDtypeStruct((tokens, width), BF)),
        in_specs=[vm] * 6,
        out_specs=(vm, vm),
        scratch_shapes=scatter_scratch(rows, width) + GATHER_SEMS,
        compiler_params=pltpu.CompilerParams(collective_id=1, has_side_effects=True, vmem_limit_bytes=56 * 2**20),
        cost_estimate=pl.CostEstimate(flops=40 * 10**9, bytes_accessed=12 * tokens * width, transcendentals=0),
        name="project_out",
    )(o, wout, mine, obias, gain, shift)


def ff_back_kernel(ns, nb, du, wg, before_in, x1_in, cot_in, gain, own, prior, *refs):
    dx1, da, sums, got, before, x1, cot, loads, w, load_sem, out, via, from_x, from_y, s1, r1, s2, r2, *moving = refs
    line = Line(1, own, prior, got, *moving)
    rows, width = x1.shape
    half = rows // 2
    load_rows(ns, nb, width // (ns * nb), wg, w, load_sem)
    pairs = (before_in, before), (x1_in, x1), (cot_in, cot)
    copies = [pltpu.make_async_copy(src, dst, loads.at[k]) for k, (src, dst) in enumerate(pairs)]
    for one in copies:
        one.start()
    line.ready()
    place, met = greet(line.neighbours(), True)
    pltpu.make_async_copy(w, w, load_sem).wait()
    copies[0].wait()

    def partial(block):
        at = pl.multiple_of(block * rows, rows)
        return before[pl.ds(at, rows), :].astype(F32) + dot_t(du[pl.ds(at, rows), :], w[...])

    steps = scatter_steps(partial, place, (out, via, from_x, from_y), s1, r1, met, True)
    next(steps)
    line.go()
    for _ in range(4):
        next(steps)
    copies[1].wait()
    copies[2].wait()
    gather = gather_steps(da, rows, place, s2, r2)
    totals = [jnp.zeros((1, width), F32)] * 3
    for part in range(2):
        grad = next(steps)
        span = slice(part * half, part * half + half)
        normed, rstd = norm_stats(x1[span, :])
        res = cot[span, :].astype(F32) + norm_back(grad, normed, rstd, gain[...])
        dx1[span, :] = res
        low = res.astype(BF)
        at = pl.multiple_of(place[0] * rows + part * half, half)
        da[pl.ds(at, half), :] = low
        next(gather)
        for k, term in enumerate((low.astype(F32), grad * normed, grad)):
            totals[k] += jnp.sum(term, 0, keepdims=True)
    for k in range(3):
        sums[k : k + 1, :] = totals[k]
    for _ in gather:
        pass
    for _ in steps:
        pass
    line.stop()


def ff_back(ns, nb, du, wg, before, x1, cot, gain, own, prior):
    rows, width = x1.shape
    tokens, chunk = du.shape
    vm = pl.BlockSpec(memory_space=pltpu.VMEM)
    hbm = pl.BlockSpec(memory_space=pl.ANY)
    return pl.pallas_call(
        functools.partial(ff_back_kernel, ns, nb),
        out_shape=(
            jax.ShapeDtypeStruct((rows, width), F32),
            jax.ShapeDtypeStruct((tokens, width), BF),
            jax.ShapeDtypeStruct((3, width), F32),
            jax.ShapeDtypeStruct(prior.shape, BF),
        ),
        in_specs=[vm] + [hbm] * 4 + [vm, hbm, vm],
        out_specs=(vm,) * 4,
        scratch_shapes=[pltpu.VMEM(before.shape, BF), pltpu.VMEM((rows, width), F32), pltpu.VMEM((rows, width), BF)]
        + [pltpu.SemaphoreType.DMA((3,)), pltpu.VMEM((width, chunk), BF), pltpu.SemaphoreType.DMA]
        + scatter_scratch(rows, width)
        + GATHER_SEMS
        + line_scratch(*prior.shape[1:]),
        compiler_params=pltpu.CompilerParams(collective_id=2, has_side_effects=True, vmem_limit_bytes=56 * 2**20),
        cost_estimate=pl.CostEstimate(flops=40 * 10**9, bytes_accessed=12 * tokens * width, transcendentals=0),
        name="ff_back",
    )(du, wg, before, x1, cot, gain, own, prior)


def finish_kernel(ns, nb, count, dproj, wq, *refs):
    summed, gs, wgs = refs[:count], refs[count : 2 * count], refs[2 * count : 3 * count]
    mine, gain, part_grad, gains, stage, gw2, low_sum, w = refs[3 * count : 3 * count + 8]
    ws = refs[3 * count + 8 : 4 * count + 8]
    load, s0, r0, *buffers = refs[4 * count + 8 :]
    buffers, more = buffers[:6], buffers[6:]
    rows, width = mine.shape
    half, cut = rows // 2, upper_rows(rows)
    chunk = summed[0].shape[1]
    part_rows, pieces = chunk // nb, width // chunk
    load_attention(ns, nb, wq, w, load.at[0])
    for c in range(count):
        load_second(nb, wgs[c], ws[c], load.at[3 + c])
    me, others, met = greet_seq(ns)
    by_x, by_y, batch = me + 1 - 2 * lax.rem(me, 2), lax.rem(me + 2, 4), lax.axis_index("batch")
    place = me, by_x, by_y, (by_x, batch), (by_y, batch)
    depth, hidden = stage.shape[0], stage.shape[1] // ns

    def ship(b, carry):
        for c in range(count):
            cols = pl.ds(pl.multiple_of(me * hidden + (b * count + c) * part_rows, part_rows), part_rows)
            from_cols = pl.ds(pl.multiple_of(b * part_rows, part_rows), part_rows)
            own = pl.ds(pl.multiple_of(me * depth, depth), depth)
            pltpu.make_async_copy(summed[c].at[own, from_cols], stage.at[:, cols], load.at[1]).start()
            for d, to in enumerate(others):
                theirs = pl.ds(pl.multiple_of(to[0] * depth, depth), depth)
                send(summed[c].at[theirs, from_cols], stage.at[:, cols], s0.at[d], r0.at[d], to)
        return carry

    for c in range(count):
        for p in range(pieces):
            pltpu.make_async_copy(
                summed[c].at[ns * depth + p * part_rows : ns * depth + (p + 1) * part_rows],
                gw2.at[c * part_rows : (c + 1) * part_rows, p * chunk : (p + 1) * chunk],
                load.at[2],
            ).start()

    def input_grad(block):
        at = pl.multiple_of(block * rows, rows)
        return dot_t(dproj[pl.ds(at, rows), :], w[...])

    def branch(block):
        at = pl.ds(pl.multiple_of(block * rows + cut, rows - cut), rows - cut)
        total = jnp.dot(gs[0][at, :], ws[0][...], preferred_element_type=F32)
        for c in range(1, count):
            total += jnp.dot(gs[c][at, :], ws[c][...], preferred_element_type=F32)
        return total

    met()
    pltpu.make_async_copy(w, w, load.at[0]).wait()
    steps = scatter_steps(input_grad, place, buffers[:4], *buffers[4:])
    for _ in range(3):
        next(steps)
    for c in range(count):
        pltpu.make_async_copy(ws[c], ws[c], load.at[3 + c]).wait()
    others_steps = scatter_steps(branch, place, more[:4], *more[4:])
    next(others_steps)
    next(steps)
    next(others_steps)
    next(others_steps)
    lax.fori_loop(0, nb, ship, 0)
    *_, sums = steps
    totals = [jnp.zeros((1, width), F32)] * 2
    for part, grad in enumerate(sums):
        span = slice(part * half, part * half + half)
        normed, rstd = norm_stats(mine[span, :].astype(F32))
        part_grad[span, :] = norm_back(grad, normed, rstd, gain[...])
        for k, term in enumerate((grad * normed, grad)):
            totals[k] += jnp.sum(term, 0, keepdims=True)
    for k in range(2):
        gains[k : k + 1, :] = totals[k]
    *_, lows = others_steps
    for part, total in enumerate(lows):
        size = (rows - cut) // 2
        low_sum[part * size : (part + 1) * size, :] = total
    pltpu.make_async_copy(gw2, gw2, load.at[2]).wait()
    strip = stage.at[:, :hidden]
    pltpu.make_async_copy(strip, strip, load.at[1]).wait()
    for d, to in enumerate(others):
        pltpu.make_async_remote_copy(
            src_ref=strip, dst_ref=strip, send_sem=s0.at[d], recv_sem=r0.at[d], device_id=to, device_id_type=MESH
        ).wait()


def finish(ns, nb, dproj, wq, summed, gs, wgs, mine, gain):
    rows, width = mine.shape
    count, chunk = len(summed), summed[0].shape[1]
    depth, hidden = width // (ns * nb), count * chunk
    vm = pl.BlockSpec(memory_space=pltpu.VMEM)
    hbm = pl.BlockSpec(memory_space=pl.ANY)
    dma = pltpu.SemaphoreType.DMA
    return pl.pallas_call(
        functools.partial(finish_kernel, ns, nb, count),
        out_shape=(
            jax.ShapeDtypeStruct((rows, width), F32),
            jax.ShapeDtypeStruct((2, width), F32),
            jax.ShapeDtypeStruct((depth, hidden * ns), BF),
            jax.ShapeDtypeStruct((hidden // nb, width), BF),
            jax.ShapeDtypeStruct((rows - upper_rows(rows), width), F32),
        ),
        in_specs=[vm, hbm] + [hbm] * count + [vm] * count + [hbm] * count + [vm] * 2,
        out_specs=(vm,) * 5,
        scratch_shapes=[pltpu.VMEM((width, dproj.shape[1]), BF)]
        + [pltpu.VMEM((chunk, width), BF)] * count
        + [dma((3 + count,)), dma((ns - 1,)), dma((ns - 1,))]
        + scatter_scratch(rows, width)
        + scatter_scratch(rows - upper_rows(rows), width),
        compiler_params=pltpu.CompilerParams(collective_id=3, has_side_effects=True, vmem_limit_bytes=56 * 2**20),
        cost_estimate=pl.CostEstimate(flops=40 * 10**9, bytes_accessed=24 * rows * width, transcendentals=0),
        name="finish",
    )(dproj, wq, *summed, *gs, *wgs, mine, gain)


def greet_all(ns, nb):
    me, batch = lax.axis_index("seq"), lax.axis_index("batch")
    along_seq = [(lax.rem(me + d, ns), batch) for d in range(1, ns)]
    along_batch = [(me, lax.rem(batch + d, nb)) for d in range(1, nb)]
    barrier = pltpu.get_barrier_semaphore()
    for other in along_seq + along_batch:
        pl.semaphore_signal(barrier, inc=1, device_id=other, device_id_type=MESH)
    pl.semaphore_wait(barrier, ns + nb - 2)
    return me, batch, along_seq, along_batch


def greet_seq(ns, more=()):
    me, batch = lax.axis_index("seq"), lax.axis_index("batch")
    others = [(lax.rem(me + d, ns), batch) for d in range(1, ns)]
    barrier = pltpu.get_barrier_semaphore()
    for other in [*others, *more]:
        pl.semaphore_signal(barrier, inc=1, device_id=other, device_id_type=MESH)
    return me, others, lambda: pl.semaphore_wait(barrier, ns - 1 + len(more))


def spread_kernel(ns, w_qkv, qkv, local, s0, r0):
    depth = w_qkv.shape[0]
    share = qkv.shape[1]
    width = ns * share
    me, others, met = greet_seq(ns)
    copies = []
    for t in range(3):
        cols = pl.ds(pl.multiple_of(t * width + me * share, share), share)
        rows = pl.ds(pl.multiple_of((t * ns + me) * depth, depth), depth)
        one = pltpu.make_async_copy(w_qkv.at[:, cols], qkv.at[rows], local.at[t])
        one.start()
        copies.append(one)
    met()
    for t in range(3):
        rows = pl.ds(pl.multiple_of((t * ns + me) * depth, depth), depth)
        for d, to in enumerate(others):
            cols = pl.ds(pl.multiple_of(t * width + to[0] * share, share), share)
            copies.append(send(w_qkv.at[:, cols], qkv.at[rows], s0.at[t, d], r0.at[t, d], to))
    for one in copies:
        one.wait()


def spread(ns, w_qkv):
    depth, width = w_qkv.shape[0], w_qkv.shape[1] // 3
    hbm = pl.BlockSpec(memory_space=pl.ANY)
    dma = pltpu.SemaphoreType.DMA
    return pl.pallas_call(
        functools.partial(spread_kernel, ns),
        out_shape=jax.ShapeDtypeStruct((3 * ns * depth, width // ns), BF),
        in_specs=[hbm],
        out_specs=hbm,
        scratch_shapes=[dma((3,)), dma((3, ns - 1)), dma((3, ns - 1))],
        compiler_params=pltpu.CompilerParams(collective_id=5, has_side_effects=True),
        cost_estimate=pl.CostEstimate(flops=10**6, bytes_accessed=10**4, transcendentals=0),
        name="spread",
    )(w_qkv)


def spread_ff_kernel(ns, nb, parts, w1, w2, *refs):
    packs, (stage, local, s1, r1) = refs[:parts], refs[parts:]
    depth, rows2, width = w1.shape[0], w2.shape[0], w2.shape[1]
    hidden = w1.shape[1] // ns
    part, chunk = rows2 // parts, hidden // parts
    pieces = width // chunk
    me, others, met = greet_seq(ns)
    at = pl.ds(pl.multiple_of(me * depth, depth), depth)
    cols = pl.ds(pl.multiple_of(me * hidden, hidden), hidden)
    own = pltpu.make_async_copy(w1.at[:, cols], stage.at[at], local)
    own.start()
    met()
    copies = [own]
    for d, to in enumerate(others):
        cols = pl.ds(pl.multiple_of(to[0] * hidden, hidden), hidden)
        copies.append(send(w1.at[:, cols], stage.at[at], s1.at[d], r1.at[d], to))
    for c in range(parts):
        for p in range(pieces):
            span = slice(ns * depth + p * part, ns * depth + (p + 1) * part)
            packs[c][span, :] = w2[c * part : (c + 1) * part, p * chunk : (p + 1) * chunk]
    for one in copies:
        one.wait()
    for c in range(parts):
        for b in range(nb):
            source = (b * parts + c) * part
            packs[c][: ns * depth, b * part : (b + 1) * part] = stage[:, source : source + part]


def spread_ff(ns, nb, parts, w1, w2):
    depth, hidden = w1.shape[0], w1.shape[1] // ns
    vm = pl.BlockSpec(memory_space=pltpu.VMEM)
    dma = pltpu.SemaphoreType.DMA
    pack = jax.ShapeDtypeStruct((2 * ns * depth, hidden // parts), BF)
    return pl.pallas_call(
        functools.partial(spread_ff_kernel, ns, nb, parts),
        out_shape=(pack,) * parts,
        in_specs=[pl.BlockSpec(memory_space=pl.ANY), vm],
        out_specs=(vm,) * parts,
        scratch_shapes=[pltpu.VMEM((ns * depth, hidden), BF), dma, dma((ns - 1,)), dma((ns - 1,))],
        compiler_params=pltpu.CompilerParams(collective_id=11, has_side_effects=True),
        cost_estimate=pl.CostEstimate(flops=10**6, bytes_accessed=10**4, transcendentals=0),
        name="spread_ff",
    )(w1, w2)


def whole_row(ns, nb, vecs, row, width):
    pieces = jnp.concatenate([vecs[b, s, row : row + 1, :] for b in range(nb) for s in range(ns)], 0)
    lanes = jnp.concatenate([pieces] * (width // pieces.shape[1]), 1)
    owner = lax.broadcasted_iota(jnp.int32, lanes.shape, 0)
    owner = lax.rem(owner, ns) * nb + owner // ns
    place = lax.broadcasted_iota(jnp.int32, lanes.shape, 1) // (width // (ns * nb))
    return jnp.sum(jnp.where(owner == place, lanes, 0.0), 0, keepdims=True)


def collect_kernel(ns, nb, mine, cot, vec, h1, cots, vecs, acts, local, s1, r1, s2, r2, s3, r3, s4, r4):
    rows, width = mine.shape
    half = rows // 2
    me, batch = lax.axis_index("seq"), lax.axis_index("batch")
    by_x = me + 1 - 2 * lax.rem(me, 2)
    by_y = lax.rem(me + 2, 4)
    others = [(lax.rem(me + d, ns), batch) for d in range(1, ns)]
    column = [(me, lax.rem(batch + d, nb)) for d in range(1, nb)]
    barrier = pltpu.get_barrier_semaphore()
    for other in others + column:
        pl.semaphore_signal(barrier, inc=1, device_id=other, device_id_type=MESH)
    vecs[batch, me] = vec[...]
    at_me = pl.ds(pl.multiple_of(me * rows, rows), rows)
    acts[at_me, :] = mine[...]
    own = pltpu.make_async_copy(cot, cots.at[at_me], local)
    own.start()
    pl.semaphore_wait(barrier, ns + nb - 2)
    to_x, to_y = (by_x, batch), (by_y, batch)
    small = vecs.at[batch, me]
    near = [send(small, small, s3.at[d], r3.at[d], to) for d, to in enumerate(others)]

    def normalise(block):
        span = pl.ds(pl.multiple_of(block * rows, rows), rows)
        normed, _ = norm_stats(acts[span, :].astype(F32))
        h1[span, :] = (normed * gain + shift).astype(BF)

    def copy(k, full, block, side, to, sends, recvs):
        span = full.at[pl.ds(pl.multiple_of(block * rows + side * half, half), half)]
        return send(span, span, sends.at[k], recvs.at[k], to)

    c0 = copy(0, acts, me, 0, to_x, s1, r1)
    c3 = copy(3, acts, me, 1, to_y, s1, r1)
    c2 = copy(2, acts, me, 0, to_y, s1, r1)
    c1 = copy(1, acts, me, 1, to_x, s1, r1)
    for one in near:
        one.wait_recv()
    row = vecs.at[batch]
    wide = [send(row, row, s4.at[d], r4.at[d], to) for d, to in enumerate(column)]
    for one in wide:
        one.wait_recv()
    gain, shift = whole_row(ns, nb, vecs, 0, width), whole_row(ns, nb, vecs, 1, width)
    normalise(me)
    c0.wait_recv()
    c4 = copy(4, acts, by_x, 0, to_y, s1, r1)
    c3.wait_recv()
    c5 = copy(5, acts, by_y, 1, to_x, s1, r1)
    own.wait()
    d0 = copy(0, cots, me, 0, to_x, s2, r2)
    d3 = copy(3, cots, me, 1, to_y, s2, r2)
    d2 = copy(2, cots, me, 0, to_y, s2, r2)
    d1 = copy(1, cots, me, 1, to_x, s2, r2)
    c1.wait_recv()
    normalise(by_x)
    c2.wait_recv()
    normalise(by_y)
    c4.wait_recv()
    c5.wait_recv()
    normalise(3 - me)
    d0.wait_recv()
    d4 = copy(4, cots, by_x, 0, to_y, s2, r2)
    d3.wait_recv()
    d5 = copy(5, cots, by_y, 1, to_x, s2, r2)
    for one in (d1, d2, d4, d5):
        one.wait_recv()
    for one in (c0, c1, c2, c3, c4, c5, d0, d1, d2, d3, d4, d5, *near, *wide):
        one.wait_send()


def collect(ns, nb, mine, cot, vec):
    rows, width = mine.shape
    vm = pl.BlockSpec(memory_space=pltpu.VMEM)
    hbm = pl.BlockSpec(memory_space=pl.ANY)
    dma = pltpu.SemaphoreType.DMA
    full = jax.ShapeDtypeStruct((ns * rows, width), BF)
    return pl.pallas_call(
        functools.partial(collect_kernel, ns, nb),
        out_shape=(full, full, jax.ShapeDtypeStruct((nb, ns) + vec.shape, F32)),
        in_specs=[vm, hbm, vm],
        out_specs=(vm, hbm, vm),
        scratch_shapes=[pltpu.VMEM((ns * rows, width), BF), dma]
        + [dma((6,))] * 4
        + [dma((ns - 1,))] * 2
        + [dma((nb - 1,))] * 2,
        compiler_params=pltpu.CompilerParams(collective_id=6, has_side_effects=True, vmem_limit_bytes=40 * 2**20),
        cost_estimate=pl.CostEstimate(flops=10**6, bytes_accessed=10**4, transcendentals=0),
        name="collect",
    )(mine, cot, vec)


def home_kernel(ns, nb, summed, sums, gqkv, gout, small, stage, near, mid, far, local, s0, r0, s1, r1, s2, r2):
    depth, width = gout.shape
    share = width // ns
    me, batch, others, column = greet_all(ns, nb)
    first = [send(sums.at[to[1]], near.at[d], s1.at[d], r1.at[d], to) for d, to in enumerate(column)]
    copies = []
    for t in range(3):
        cols = pl.ds(pl.multiple_of(t * width + me * share, share), share)
        for d, to in enumerate(others):
            rows = pl.ds(pl.multiple_of((t * ns + to[0]) * depth, depth), depth)
            copies.append(send(summed.at[rows], stage.at[:, cols], s0.at[t, d], r0.at[t, d], to))
        rows = pl.ds(pl.multiple_of((t * ns + me) * depth, depth), depth)
        own = pltpu.make_async_copy(summed.at[rows], stage.at[:, cols], local.at[t])
        own.start()
        copies.append(own)
    for p in range(ns):
        rows = slice((3 * ns + p) * depth, (3 * ns + p + 1) * depth)
        gout[:, p * share : (p + 1) * share] = summed[rows, :].astype(F32)
    total = sums[batch]
    for d, one in enumerate(first):
        one.wait_recv()
        total += near[d]
    mid[...] = total
    second = [send(mid.at[to[0]], far.at[d], s2.at[d], r2.at[d], to) for d, to in enumerate(others)]
    for one in copies:
        one.wait()
    gqkv[...] = stage[...].astype(F32)
    total = mid[me]
    for d, one in enumerate(second):
        one.wait_recv()
        total += far[d]
    small[...] = total
    for one in first + second:
        one.wait_send()


def home(ns, nb, summed, sums):
    rows, share = summed.shape
    depth, width = rows // (4 * ns), ns * share
    tail = sums.shape[2:]
    vm = pl.BlockSpec(memory_space=pltpu.VMEM)
    dma = pltpu.SemaphoreType.DMA
    return pl.pallas_call(
        functools.partial(home_kernel, ns, nb),
        out_shape=(
            jax.ShapeDtypeStruct((depth, 3 * width), F32),
            jax.ShapeDtypeStruct((depth, width), F32),
            jax.ShapeDtypeStruct(tail, F32),
        ),
        in_specs=[vm, vm],
        out_specs=(vm, vm, vm),
        scratch_shapes=[
            pltpu.VMEM((depth, 3 * width), BF),
            pltpu.VMEM((nb - 1, ns) + tail, F32),
            pltpu.VMEM((ns,) + tail, F32),
            pltpu.VMEM((ns - 1,) + tail, F32),
            dma((3,)),
            dma((3, ns - 1)),
            dma((3, ns - 1)),
            dma((nb - 1,)),
            dma((nb - 1,)),
            dma((ns - 1,)),
            dma((ns - 1,)),
        ],
        compiler_params=pltpu.CompilerParams(collective_id=8, has_side_effects=True),
        cost_estimate=pl.CostEstimate(flops=5 * 10**9, bytes_accessed=4 * summed.size, transcendentals=0),
        name="home",
    )(summed, sums)


PARTS = 2


def gather_seq(value):
    return lax.all_gather(value, "seq", axis=0, tiled=True)


def scatter_seq(partial):
    return lax.psum_scatter(partial, "seq", scatter_dimension=0, tiled=True)


def scatter_batch(parts):
    flat = parts.reshape(-1, parts.shape[-1])
    return lax.psum_scatter(flat, "batch", scatter_dimension=0, tiled=True)


def scatter_chips(parts):
    count = lax.axis_size("batch")
    groups = [list(range(core, count, 2)) for core in range(2)]
    flat = parts.reshape(-1, parts.shape[-1])
    return lax.psum_scatter(flat, "batch", scatter_dimension=0, tiled=True, axis_index_groups=groups)


def unpermute(ns, nb, gathered):
    depth = gathered.shape[1] // ns
    return gathered.reshape(nb, ns, depth, -1).transpose(1, 0, 2, 3).reshape(ns * nb * depth, -1)


def unpack_attention(ns, nb, packed):
    share = packed.shape[2]
    parts = packed.reshape(nb, 3, ns, -1, share)
    return parts.transpose(2, 0, 3, 1, 4).reshape(ns * share, 3 * share)


def body(
    block_input,
    lengths,
    ln1_gain,
    ln1_bias,
    w_qkv,
    qv_bias,
    w_out,
    out_bias,
    ln2_gain,
    ln2_bias,
    w_fc1,
    fc1_bias,
    w_fc2,
    fc2_bias,
    out_cotangent,
):
    ns, nb = lax.axis_size("seq"), lax.axis_size("batch")
    seq = lax.axis_index("seq")
    rows, width = block_input.shape[1:]
    share = width // ns
    depth = width // (ns * nb)
    hidden = w_fc1.shape[1] // ns
    chunk = hidden // PARTS
    part = chunk // nb
    pieces = width // chunk
    planar = ns == 4 and nb == 8
    mine, cot_mine = block_input[0], out_cotangent[0]

    vectors = (ln1_gain, ln1_bias, qv_bias, out_bias, ln2_gain, ln2_bias, fc1_bias, fc2_bias)
    wout = lax.all_gather(w_out, "batch", axis=0, tiled=True)
    if planar:
        wq = spread(ns, w_qkv)
        wq, w_fc1 = lax.optimization_barrier((wq, w_fc1))
        packs = spread_ff(ns, nb, PARTS, w_fc1, w_fc2)
        packs, vectors, wout = lax.optimization_barrier((packs, vectors, wout))
        spare = jnp.zeros((1024 - 2 * depth - sum(vec.shape[0] for vec in vectors),), BF)
        block = jnp.concatenate([vectors[0], vectors[0], vectors[1], vectors[1], *vectors[2:], spare])
        block = block.astype(F32).reshape(8, 128)
        h1, cot, packed = collect(ns, nb, mine, cot_mine, block)
        packed = packed.transpose(1, 0, 2, 3).reshape(ns * nb, 1024)
        packed = jnp.concatenate([packed[:, :depth], packed[:, 2 * depth : 3 * depth], packed[:, 4 * depth :]], 1)
    else:
        wq = lax.all_to_all(w_qkv.reshape(depth, 3, ns, share), "seq", 2, 0).transpose(2, 0, 1, 3)
        wq = wq.reshape(3 * ns * depth, share)
        vector = jnp.concatenate(vectors).astype(F32)
        packed = lax.all_gather(vector, ("seq", "batch"), axis=0, tiled=False)
    wq = lax.all_gather(wq, "batch", axis=0, tiled=True).reshape(nb, 3 * ns * depth, share)
    full, at = [], 0
    for vec in vectors:
        full.append(packed[:, at : at + vec.shape[0]].reshape(1, -1))
        at += vec.shape[0]
    gain1, shift1, qv, obias, gain2, shift2, bias1, bias2 = full
    bias1 = lax.dynamic_slice_in_dim(bias1, seq * hidden, hidden, 1).reshape(nb, PARTS, part)
    qbias = lax.dynamic_slice_in_dim(qv, seq * share, share, 1)
    vbias = lax.dynamic_slice_in_dim(qv, width + seq * share, share, 1)
    bias3 = jnp.concatenate([qbias, jnp.zeros_like(qbias), vbias], 1)

    if not planar:
        fc1_part = lax.all_to_all(w_fc1.reshape(depth, ns, hidden), "seq", 1, 0)
        fc1_part = fc1_part.reshape(ns * depth, nb, PARTS, part)
        fc2_part = w_fc2.reshape(PARTS, part, pieces, chunk)
        packs = []
        for c in range(PARTS):
            first = fc1_part[:, :, c].reshape(ns * depth, chunk)
            second = fc2_part[c].transpose(1, 0, 2).reshape(pieces * part, chunk)
            packs.append(jnp.concatenate([first, second], 0))
        h1 = (norm_stats(gather_seq(mine).astype(F32))[0] * gain1 + shift1).astype(BF)
        cot = gather_seq(cot_mine)
    wgs = [lax.all_gather(pack, "batch", axis=0, tiled=True).reshape(nb, -1, chunk) for pack in packs]

    qkv, o, h1t = attend(ns, nb, lengths, h1, wq, bias3)
    if planar:
        x1, h2 = middle(o, wout, mine, obias, gain2, shift2)
    else:
        a = scatter_seq(jnp.dot(o, wout, preferred_element_type=F32))
        x1 = mine.astype(F32) + (a + obias)
        h2 = gather_seq((norm_stats(x1)[0] * gain2 + shift2).astype(BF))

    line = ()
    if planar:
        own, g, du, gb, h2t, before = ff_first(ns, nb, h2, cot, wgs[0], bias1[:, 0].reshape(1, chunk))
        line = (own,)
        h2t, gain1, gain2, bias2 = lax.optimization_barrier((h2t, gain1, gain2, bias2))
        gws = [None]
    else:
        gw, g, du, gb, h2t, before = ff_chunk(ns, nb, h2, None, cot, wgs[0], bias1[:, 0].reshape(1, chunk))
        gws = [scatter_batch(gw)]
    gs, dus, gb1 = [g], [du], [gb.reshape(nb, 1, part)]
    for c in range(1, PARTS):
        gw, g, du, gb, *got = ff_chunk(ns, nb, h2, h2t, cot, wgs[c], bias1[:, c].reshape(1, chunk), *line)
        gws.append(scatter_batch(gw))
        gs.append(g)
        dus.append(du)
        gb1.append(gb.reshape(nb, 1, part))
    if planar:
        dx1, da, rows2, got = ff_back(ns, nb, dus[1], wgs[1], before, x1, cot_mine, gain2, own, got[0])
        line = own, got, *gs, *wgs
    else:
        dh2 = before.astype(F32) + dot_t(dus[1], unpermute(ns, nb, wgs[1][:, : ns * depth]))
        dh2 = scatter_seq(dh2)
        normed2, rstd2 = norm_stats(x1)
        dx1 = cot_mine.astype(F32) + norm_back(dh2, normed2, rstd2, gain2)
        da_mine = dx1.astype(BF)
        rows2 = jnp.stack([jnp.sum(term, 0) for term in (da_mine.astype(F32), dh2 * normed2, dh2)])
        da = gather_seq(da_mine)

    gattn, dproj, gqv, *more = attend_back(ns, nb, lengths, h1t, da, wout, o, qkv, *line)
    if planar:
        gws[0], y = more
    gattn = scatter_chips(gattn) if planar else scatter_batch(gattn)
    if planar:
        gx, rows1, gw1, gw2, lower = finish(ns, nb, dproj, wq, gws, gs, wgs, mine, gain1)
        gx, rows2, gqv, gb1, cot_mine, y = lax.optimization_barrier((gx, rows2, gqv, gb1, cot_mine, y))
        gx = dx1 + gx
        out = (x1 + (jnp.concatenate([y, lower], 0) + bias2)).astype(BF)
        gw1, gw2 = gw1.astype(F32), gw2.astype(F32)
    else:
        dh1 = scatter_seq(dot_t(dproj, unpack_attention(ns, nb, wq)))
        normed1, rstd1 = norm_stats(mine.astype(F32))
        rows1 = jnp.stack([jnp.sum(dh1 * normed1, 0), jnp.sum(dh1, 0)])
        gx = dx1 + norm_back(dh1, normed1, rstd1, gain1)
        y = 0.0
        for g, wg in zip(gs, wgs):
            w2 = wg[:, ns * depth :].reshape(nb, pieces, part, chunk).transpose(0, 2, 1, 3).reshape(chunk, width)
            y += jnp.dot(g, w2, preferred_element_type=F32)
        out = (x1 + (scatter_seq(y) + bias2)).astype(BF)

    if not planar:
        gw1 = jnp.stack([gw[: ns * depth].reshape(ns, depth, nb, part) for gw in gws], 3)
        gw1 = lax.all_to_all(gw1, "seq", 0, 1).astype(F32).reshape(depth, ns * hidden)
        gw2 = jnp.stack([gw[ns * depth :].reshape(pieces, part, chunk) for gw in gws], 0)
        gw2 = gw2.astype(F32).transpose(0, 2, 1, 3).reshape(PARTS * part, width)
        gwqkv = gattn[: 3 * ns * depth].reshape(3, ns, depth, share)
        gwqkv = lax.all_to_all(gwqkv, "seq", 1, 2).astype(F32).transpose(1, 0, 2, 3).reshape(depth, 3 * width)
        gwo = gattn[3 * ns * depth :].reshape(ns, depth, share).astype(F32).transpose(1, 0, 2).reshape(depth, width)

    def place(part, size):
        return lax.dynamic_update_slice_in_dim(jnp.zeros((size,), F32), part, seq * part.shape[0], 0)

    gqv = gqv[0]
    gqv = jnp.concatenate([place(gqv[:share], width), place(gqv[2 * share :], width)])
    gb1 = place(jnp.stack(gb1, 1).reshape(-1), ns * hidden)
    gb2 = jnp.sum(cot_mine.astype(F32), 0)

    def shards(grads):
        return grads.reshape(grads.shape[0], ns * nb, -1).transpose(1, 0, 2).reshape(ns * nb, -1)

    sums = [shards(rows1), gqv.reshape(ns * nb, -1), shards(rows2), gb1.reshape(ns * nb, -1), gb2.reshape(ns * nb, -1)]
    sums = jnp.concatenate(sums, 1)
    if planar:
        sums = jnp.pad(sums, ((0, 0), (0, 1024 - sums.shape[1]))).reshape(ns, nb, 8, 128)
        sums, gx, out, gw1, gw2 = lax.optimization_barrier((sums.transpose(1, 0, 2, 3), gx, out, gw1, gw2))
        gwqkv, gwo, sums = home(ns, nb, gattn, sums)
        sums = sums.reshape(-1)
    else:
        sums = lax.psum_scatter(sums, ("seq", "batch"), scatter_dimension=0, tiled=True)[0]
    small, at = [], 0
    for vec in vectors:
        small.append(sums[at : at + vec.shape[0]])
        at += vec.shape[0]
    return (
        out[None],
        gx[None],
        small[0],
        small[1],
        gwqkv,
        small[2],
        gwo,
        small[3],
        small[4],
        small[5],
        gw1,
        small[6],
        gw2,
        small[7],
    )


def solution(mesh):
    shard = P(("seq", "batch"))
    shard2 = P(("seq", "batch"), None)
    acts = P("batch", "seq", None)
    return jax.shard_map(
        body,
        mesh=mesh,
        in_specs=(acts, P("batch"), shard, shard, shard2, shard, shard2, shard, shard, shard, shard2, shard, shard2, shard, acts),
        out_specs=(acts, acts, shard, shard, shard2, shard, shard2, shard, shard, shard, shard2, shard, shard2, shard),
        check_vma=False,
    )
```
